32 devices in a mesh: dp: 16 (over z, y, x), col: 2 (over core).
Axes of the slice: x: 2, y: 2, z: 4, core: 2. Of those that a mesh axis runs over, the one named last changes fastest.
Arguments:
- embeddings: bfloat16 [8192, 4096], P('dp'), may hold values from -16 to 16
- rotation: bfloat16 [4096, 4096], P(None, 'col'), may hold values from -0.09375 to 0.09375
- codes: int32 [8192, 512], P('dp', 'col'), may hold values from 0 to 255
- codebooks: bfloat16 [512, 256, 8], P('col'), may hold values from -16 to 16
Outputs:
- new_rotation: float32 [4096, 4096], P('dp', 'col')
The draws below stay inside these ranges and needn't reach their ends.
All inputs are finite; a program needn't handle non-finite values.
Results may differ from the reference program's by a relative error of at most 0.015.
Values may be sent and summed in bfloat16 or wider, within the bound.
No kernel may reach another device: no remote copies, remote signals or barrier semaphores. Data moves between devices by JAX's collectives and lax.ppermute only.
A program may use at most 128 MiB of HBM per device.

```python
import math
import jax
import jax.numpy as jnp
from jax import lax

D = 4096
DS = 8
K = 256
STEPS = 2
M = 512
ROWS = 8192
N_DP = 16


def draw_embeddings(key, part):
    key_scale, key_vals = jax.random.split(key, 2)
    ramp = jnp.arange(D, dtype=jnp.float32) / D
    spread = jax.random.uniform(key_scale, (D,), jnp.float32)
    col_scale = 0.3 * jnp.exp(math.log(10.0) * (0.5 * ramp + 0.5 * spread))
    values = jnp.clip(jax.random.normal(key_vals, (ROWS, D), jnp.float32), -4.0, 4.0)
    return (values * col_scale[None, :]).astype(jnp.bfloat16)


def draw_codebooks(key, part):
    key_scale, key_vals = jax.random.split(key, 2)
    ramp = jnp.arange(M, dtype=jnp.float32) / M
    spread = jax.random.uniform(key_scale, (M,), jnp.float32)
    sub_scale = 0.3 * jnp.exp(math.log(10.0) * (0.5 * ramp + 0.5 * spread))
    values = jnp.clip(jax.random.normal(key_vals, (M, K, DS), jnp.float32), -4.0, 4.0)
    return (values * sub_scale[:, None, None]).astype(jnp.bfloat16)


def touch_ends(result, stream_key, smallest, largest):
    longest = result.shape.index(max(result.shape))
    spots = []
    for shift in (0, 1):
        where = [jax.random.randint(jax.random.fold_in(stream_key, axis), (), 0, length) for axis, length in enumerate(result.shape)]
        where[longest] = (where[longest] + shift) % result.shape[longest]
        spots.append(tuple(where))
    return result.at[spots[0]].set(smallest).at[spots[1]].set(largest)


def block_scale(rng, shape, cuts, low, largest):
    factor_of, own = 1.0, jax.random.fold_in(rng, 6)
    for axis_at, blocks in cuts:
        steps = jnp.exp(jax.random.uniform(jax.random.fold_in(own, axis_at), (blocks,), jnp.float32, low / len(cuts), largest / len(cuts)))
        factor_of = factor_of * jnp.repeat(steps, shape[axis_at] // blocks).reshape([-1 if axis == axis_at else 1 for axis in range(len(shape))])
    return factor_of


def centred(rng, shape, scale, limit, cuts=(), held_as=jnp.bfloat16):
    loudness = block_scale(rng, shape, cuts, -0.22, 0.18) if cuts else 1.0
    array = jax.random.normal(rng, shape, jnp.float32) * scale * loudness
    return jnp.minimum(jnp.maximum(array, -limit), limit).astype(held_as)


def setup_inputs(seed: int = 0) -> dict:
    key_list = jax.random.split(jax.random.key(seed), 5)
    embeddings = draw_embeddings(jax.random.fold_in(key_list[4], 71), 0)
    rotation = centred(key_list[1], (D, D), D ** -0.5, 0.09375, ((1, 2),))
    codes = touch_ends(jax.random.randint(key_list[2], (ROWS, M), 0, K), jax.random.fold_in(key_list[2], 1), 0, K - 1).astype(jnp.int32)
    codebooks = draw_codebooks(jax.random.fold_in(key_list[4], 71), 0)
    return {"embeddings": embeddings, "rotation": rotation, "codes": codes, "codebooks": codebooks}


def reference(embeddings, rotation, codes, codebooks):
    rotated = jnp.dot(embeddings, rotation, preferred_element_type=jnp.float32)
    sub_index = jnp.arange(M, dtype=jnp.int32)[None, :]
    picked = codebooks[sub_index, codes]
    rebuilt = picked.reshape(ROWS, D)
    residue = rotated - rebuilt.astype(jnp.float32)
    row_error = lax.optimization_barrier(jnp.sum(residue * residue, axis=1))
    weights = 1.0 / (1.0 + row_error / (2.0 * D))
    weighted = (weights[:, None] * rebuilt.astype(jnp.float32)).astype(jnp.bfloat16)
    cross = jnp.dot(embeddings.T, weighted, preferred_element_type=jnp.float32)
    cross = cross + 0.2 * ROWS * rotation.astype(jnp.float32)
    norm_scale = 1.4 * jnp.sqrt(jnp.sum(cross * cross) / D)
    iterate = cross / norm_scale
    for step_index in range(STEPS):
        half_iter = iterate.astype(jnp.bfloat16)
        blocks = half_iter.reshape(N_DP, D // N_DP, D)

        def add_block(running, row_block):
            gram_term = jnp.dot(row_block.T, row_block, preferred_element_type=jnp.float32)
            rounded = lax.optimization_barrier(gram_term.astype(jnp.bfloat16))
            return (running + rounded.astype(jnp.float32), None)
        gram, unused = lax.scan(add_block, jnp.zeros((D, D), jnp.float32), blocks)
        product = jnp.dot(half_iter, gram.astype(jnp.bfloat16), preferred_element_type=jnp.float32)
        iterate = 1.5 * iterate - 0.5 * product
    return D ** 0.5 * iterate
```

```python
import functools
import math

import jax
import jax.numpy as jnp
from jax import lax
from jax.experimental import pallas as pl
from jax.experimental.pallas import tpu as pltpu
from jax.sharding import PartitionSpec as P

LANES = 128


def lookup_kernel(group, codes_ref, table_ref, out_ref, ids_ref):
    subs, rows = codes_ref.shape[1:]
    width = table_ref.shape[1]
    halves = table_ref.shape[2] // LANES
    ids_ref[...] = codes_ref[0].astype(jnp.float32).astype(jnp.int32)

    def body(step, carry):
        base = pl.multiple_of(step * group, group)
        for first in range(0, rows, LANES):
            ids_all = ids_ref[pl.ds(base, group), first : first + LANES]
            for pair in range(0, group, 2):
                both = []
                for sub in (pair, pair + 1):
                    ids = jnp.broadcast_to(ids_all[sub : sub + 1], (width, LANES))
                    lane = jnp.bitwise_and(ids, LANES - 1)
                    picked = None
                    for half in range(halves):
                        entries = table_ref[base + sub, :, half * LANES : (half + 1) * LANES]
                        got = jnp.take_along_axis(
                            entries, lane, axis=1, mode="promise_in_bounds"
                        )
                        picked = got if half == 0 else jnp.where(ids >= half * LANES, got, picked)
                    both.append(picked)
                out_ref[
                    pl.ds(pl.multiple_of((base + pair) * width, 2 * width), 2 * width),
                    first : first + LANES,
                ] = jnp.concatenate(both, axis=0).astype(out_ref.dtype)
        return carry

    lax.fori_loop(0, subs // group, body, 0)


def rebuild_rows(codes, table):
    blocks, subs, rows = codes.shape
    width, centroids = table.shape[1:]
    tile = min(32, subs)
    return pl.pallas_call(
        functools.partial(lookup_kernel, 8),
        grid=(subs // tile, blocks),
        in_specs=[
            pl.BlockSpec((1, tile, rows), lambda m, b: (b, m, 0)),
            pl.BlockSpec((tile, width, centroids), lambda m, b: (m, 0, 0)),
        ],
        out_specs=pl.BlockSpec((tile * width, rows), lambda m, b: (m, b)),
        out_shape=jax.ShapeDtypeStruct((subs * width, blocks * rows), jnp.bfloat16),
        scratch_shapes=[pltpu.VMEM((tile, rows), jnp.int32)],
        compiler_params=pltpu.CompilerParams(vmem_limit_bytes=32 * 1024 * 1024),
        name="lookup",
    )(codes, table)


def sum_over_col(value):
    if lax.axis_size("col") == 2:
        return value + lax.ppermute(
            value.astype(jnp.bfloat16), "col", [(0, 1), (1, 0)]
        ).astype(jnp.float32)
    return lax.psum(value, "col")


def shards(embeddings, rotation, codes, codebooks):
    tok_rows, model_width = embeddings.shape
    dp, col = lax.axis_size("dp"), lax.axis_size("col")
    rows_total = tok_rows * dp
    block_rows = model_width // dp
    part_rows = tok_rows // col

    table = jnp.transpose(codebooks, (0, 2, 1)).astype(jnp.float32)
    codes_t = codes.T.astype(jnp.bfloat16)
    all_codes = lax.all_gather(codes_t, "dp")

    own = rebuild_rows(codes_t[None], table)
    rotated = lax.dot_general(
        rotation, embeddings, (((0,), (1,)), ((), ())), preferred_element_type=jnp.float32
    )
    residue = rotated - own.astype(jnp.float32)
    row_error = lax.psum(jnp.sum(residue * residue, axis=0), "col")
    weights = 1.0 / (1.0 + row_error / (2.0 * model_width))
    scaled = (weights[:, None] * embeddings.astype(jnp.float32)).astype(jnp.bfloat16)

    mine = lax.dynamic_slice_in_dim(scaled, lax.axis_index("col") * part_rows, part_rows, 0)
    sent = lax.all_to_all(mine, "dp", split_axis=1, concat_axis=0, tiled=True)
    sent = sent.reshape(dp, part_rows, block_rows)
    columns = lax.all_gather(sent, "col", axis=1, tiled=True).reshape(rows_total, block_rows)

    rebuilt = rebuild_rows(all_codes, table)
    cross = lax.dot_general(
        columns, rebuilt, (((0,), (1,)), ((), ())), preferred_element_type=jnp.float32
    )
    start_row = lax.axis_index("dp") * block_rows
    prior = lax.dynamic_slice_in_dim(rotation, start_row, block_rows, 0).astype(jnp.float32)
    cross = cross + 0.2 * rows_total * prior

    panel = lax.all_gather(cross.astype(jnp.bfloat16), "dp", axis=0, tiled=True)
    wide = panel.astype(jnp.float32)
    frob_total = lax.psum(jnp.sum(wide * wide), "col")
    inv_square = model_width / (1.96 * frob_total)

    def times_gram(value):
        inner = lax.dot_general(
            value.astype(jnp.bfloat16), panel, (((1,), (1,)), ((), ())),
            preferred_element_type=jnp.float32,
        )
        inner = sum_over_col(inner * inv_square)
        return jnp.dot(inner.astype(jnp.bfloat16), panel, preferred_element_type=jnp.float32)

    start = cross * jnp.sqrt(inv_square)
    first = 1.5 * start - 0.5 * times_gram(start)
    inner = 1.5 * first - 0.5 * times_gram(first)
    inner = times_gram(inner)
    inner = 1.5 * inner - 0.5 * times_gram(inner)
    return math.sqrt(model_width) * (1.5 * first - 0.5 * inner)


def solution(mesh):
    placed = (P("dp", None), P(None, "col"), P("dp", "col"), P("col", None, None))
    return jax.shard_map(
        shards, mesh=mesh, in_specs=placed, out_specs=P("dp", "col"), check_vma=False
    )
```

```python
import functools
import math

import jax
import jax.numpy as jnp
from jax import lax
from jax.experimental import pallas as pl
from jax.experimental.pallas import tpu as pltpu
from jax.sharding import PartitionSpec as P

LANES = 128
GROUP = 8
CHUNKS = 4
VMEM_BYTES = 56 * 1024 * 1024
ANY = pl.BlockSpec(memory_space=pl.ANY)
VMEM = pl.BlockSpec(memory_space=pltpu.VMEM)


def split_kernel(place_ref, rows_ref, *refs):
    blocks, sems = refs[:-1], refs[-1]
    part_rows, block_cols = blocks[0].shape
    first_row = pl.multiple_of(place_ref[1] * part_rows, part_rows)
    copies = []
    for shift, block in enumerate(blocks):
        owner = lax.rem(place_ref[0] + shift, len(blocks))
        first_col = pl.multiple_of(owner * block_cols, block_cols)
        copies.append(
            pltpu.make_async_copy(
                rows_ref.at[pl.ds(first_row, part_rows), pl.ds(first_col, block_cols)],
                block,
                sems.at[shift],
            )
        )
    for copy in copies:
        copy.start()
    for copy in copies:
        copy.wait()


def split_blocks(place, embeddings, dp, col):
    rows, width = embeddings.shape
    block = jax.ShapeDtypeStruct((rows // col, width // dp), embeddings.dtype)
    return pl.pallas_call(
        split_kernel,
        grid_spec=pltpu.PrefetchScalarGridSpec(
            num_scalar_prefetch=1,
            grid=(),
            in_specs=[ANY],
            out_specs=[ANY] * dp,
            scratch_shapes=[pltpu.SemaphoreType.DMA((dp,))],
        ),
        out_shape=[block] * dp,
        name="split",
    )(place, embeddings)


def lookup_kernel(place_ref, codes_ref, table_ref, out_ref, ids_ref):
    subs, rows = codes_ref.shape[1:]
    width = table_ref.shape[1]
    halves = table_ref.shape[2] // LANES
    ids_ref[...] = codes_ref[0].astype(jnp.float32).astype(jnp.int32)

    def body(step, carry):
        base = pl.multiple_of(step * GROUP, GROUP)
        for first in range(0, rows, LANES):
            ids_all = ids_ref[pl.ds(base, GROUP), first : first + LANES]
            for pair in range(0, GROUP, 2):
                both = []
                for sub in (pair, pair + 1):
                    ids = jnp.broadcast_to(ids_all[sub : sub + 1], (width, LANES))
                    lane = jnp.bitwise_and(ids, LANES - 1)
                    picked = None
                    for half in range(halves):
                        entries = table_ref[base + sub, :, half * LANES : (half + 1) * LANES]
                        got = jnp.take_along_axis(
                            entries, lane, axis=1, mode="promise_in_bounds"
                        )
                        picked = got if half == 0 else jnp.where(ids >= half * LANES, got, picked)
                    both.append(picked)
                out_ref[
                    pl.ds(pl.multiple_of((base + pair) * width, 2 * width), 2 * width),
                    first : first + LANES,
                ] = jnp.concatenate(both, axis=0).astype(out_ref.dtype)
        return carry

    lax.fori_loop(0, subs // GROUP, body, 0)


def rebuild_rows(place, codes, table):
    blocks, subs, rows = codes.shape
    width, centroids = table.shape[1:]
    tile = min(64, subs)
    return pl.pallas_call(
        lookup_kernel,
        grid_spec=pltpu.PrefetchScalarGridSpec(
            num_scalar_prefetch=1,
            grid=(subs // tile, blocks),
            in_specs=[
                pl.BlockSpec(
                    (1, tile, rows), lambda m, s, place: (lax.rem(place[0] + blocks - s, blocks), m, 0)
                ),
                pl.BlockSpec((tile, width, centroids), lambda m, s, place: (m, 0, 0)),
            ],
            out_specs=pl.BlockSpec((tile * width, rows), lambda m, s, place: (m, s)),
            scratch_shapes=[pltpu.VMEM((tile, rows), jnp.int32)],
        ),
        out_shape=jax.ShapeDtypeStruct((subs * width, blocks * rows), jnp.bfloat16),
        compiler_params=pltpu.CompilerParams(vmem_limit_bytes=VMEM_BYTES),
        name="lookup",
    )(place, codes, table)


def load_panel(pieces, panel_ref, sems):
    dp, chunk, block = pieces[0].shape

    def copy(index, piece, owner):
        return pltpu.make_async_copy(
            piece.at[owner],
            panel_ref.at[
                pl.ds(pl.multiple_of(index * chunk, chunk), chunk),
                pl.ds(pl.multiple_of(owner * block, block), block),
            ],
            sems.at[index, owner],
        )

    for index, piece in enumerate(pieces):
        for owner in range(dp):
            copy(index, piece, owner).start()

    def wait(index):
        for owner in range(dp):
            copy(index, pieces[0], owner).wait()

    return chunk, wait


def times_panel(value_ref, panel_ref, out_ref):
    wide = min(512, panel_ref.shape[1])

    def body(step, carry):
        span = pl.ds(pl.multiple_of(step * wide, wide), wide)
        out_ref[:, span] = jnp.dot(
            value_ref[...], panel_ref[:, span], preferred_element_type=jnp.float32
        ).astype(out_ref.dtype)
        return carry

    lax.fori_loop(0, panel_ref.shape[1] // wide, body, 0)


def first_kernel(own_ref, *refs):
    count = len(refs) - 4
    pieces, (inner_ref, square_ref, panel_ref, sems) = refs[:count], refs[count:]
    chunk, wait = load_panel(pieces, panel_ref, sems)
    square_ref[...] = jnp.zeros_like(square_ref)
    wide = 512

    def body(index, carry):
        wait(index)
        span = pl.ds(pl.multiple_of(index * chunk, chunk), chunk)
        total = jnp.zeros(square_ref.shape, jnp.float32)
        for first in range(0, panel_ref.shape[1], wide):
            values = panel_ref[span, first : first + wide].astype(jnp.float32)
            total += jnp.sum((values * values).reshape(chunk // 8, 8, wide), axis=0)
        square_ref[...] += total
        return carry

    lax.fori_loop(0, len(pieces), body, 0)
    times_panel(own_ref, panel_ref, inner_ref)


def scale_of(model_width, mine_ref, other_ref):
    total = jnp.sum(mine_ref[...] + other_ref[...], axis=(0, 1), keepdims=True)
    return model_width / (1.96 * total)


def next_kernel(step, mine_ref, other_ref, mine_square_ref, other_square_ref, *refs):
    last = step == 3
    states = 2 if last else 1
    held, refs = refs[:states], refs[states:]
    count = len(refs) - (4 if last else 6)
    pieces, refs = refs[:count], refs[count:]
    if last:
        out_ref, panel_ref, sum_ref, sems = refs
    else:
        state_ref, inner_ref, panel_ref, sum_ref, value_ref, sems = refs
    chunk, wait = load_panel(pieces, panel_ref, sems)
    model_width = panel_ref.shape[1]
    scale = scale_of(model_width, mine_square_ref, other_square_ref)
    sum_ref[...] = (
        (mine_ref[...].astype(jnp.float32) + other_ref[...].astype(jnp.float32)) * scale
    ).astype(sum_ref.dtype)

    def body(index, carry):
        wait(index)
        span = pl.ds(pl.multiple_of(index * chunk, chunk), chunk)
        product = lax.dot_general(
            panel_ref[span, :], sum_ref[...], (((1,), (1,)), ((), ())),
            preferred_element_type=jnp.float32,
        )
        if step == 2:
            made = product
        else:
            made = 1.5 * held[0][span, :] - 0.5 * product
        if last:
            made = (1.5 * held[1][span, :] - 0.5 * made) * (math.sqrt(model_width) * jnp.sqrt(scale))
            out_ref[:, span] = made.T
        else:
            state_ref[span, :] = made
            value_ref[:, span] = made.T.astype(value_ref.dtype)
        return carry

    lax.fori_loop(0, len(pieces), body, 0)
    if not last:
        times_panel(value_ref, panel_ref, inner_ref)


def apply_first(own, pieces):
    dp, chunk, block = pieces[0].shape
    cols = chunk * len(pieces)
    return pl.pallas_call(
        first_kernel,
        in_specs=[VMEM] + [ANY] * len(pieces),
        out_specs=[VMEM, VMEM],
        out_shape=[
            jax.ShapeDtypeStruct((block, dp * block), jnp.bfloat16),
            jax.ShapeDtypeStruct((8, 512), jnp.float32),
        ],
        scratch_shapes=[
            pltpu.VMEM((cols, dp * block), jnp.bfloat16),
            pltpu.SemaphoreType.DMA((len(pieces), dp)),
        ],
        compiler_params=pltpu.CompilerParams(vmem_limit_bytes=VMEM_BYTES),
        name="first",
    )(own, *pieces)


def apply_next(step, inner, squares, held, pieces):
    dp, chunk, block = pieces[0].shape
    cols = chunk * len(pieces)
    last = step == 3
    if last:
        out_shape = jax.ShapeDtypeStruct((block, cols), jnp.float32)
        value = []
    else:
        out_shape = [
            jax.ShapeDtypeStruct((cols, block), jnp.float32),
            jax.ShapeDtypeStruct((block, dp * block), jnp.bfloat16),
        ]
        value = [pltpu.VMEM((block, cols), jnp.bfloat16)]
    return pl.pallas_call(
        functools.partial(next_kernel, step),
        in_specs=[VMEM] * (4 + len(held)) + [ANY] * len(pieces),
        out_specs=VMEM if last else [VMEM, VMEM],
        out_shape=out_shape,
        scratch_shapes=[
            pltpu.VMEM((cols, dp * block), jnp.bfloat16),
            pltpu.VMEM((block, dp * block), jnp.bfloat16),
        ]
        + value
        + [pltpu.SemaphoreType.DMA((len(pieces), dp))],
        compiler_params=pltpu.CompilerParams(vmem_limit_bytes=VMEM_BYTES),
        name="apply%d" % step,
    )(*inner, *squares, *held, *pieces)


def both_cores(value):
    if lax.axis_size("col") == 2:
        return value, lax.ppermute(value, "col", [(0, 1), (1, 0)])
    total = lax.psum(value.astype(jnp.float32), "col").astype(value.dtype)
    return total, jnp.zeros_like(total)


def columns_of_all(place, embeddings, dp, col):
    mine = split_blocks(place, embeddings, dp, col)
    parts = [mine[0]] + [
        lax.ppermute(mine[shift], "dp", [(i, (i + shift) % dp) for i in range(dp)])
        for shift in range(1, dp)
    ]
    share = jnp.stack(parts)
    if col == 2:
        other = lax.ppermute(share, "col", [(0, 1), (1, 0)])
        at_zero = place[1] == 0
        return jnp.concatenate(
            [jnp.where(at_zero, share, other), jnp.where(at_zero, other, share)], axis=1
        )
    return lax.all_gather(share, "col", axis=1, tiled=True)


def shards(embeddings, rotation, codes, codebooks):
    tok_rows, model_width = embeddings.shape
    sub_count = codes.shape[1]
    sub_width = codebooks.shape[2]
    dp, col = lax.axis_size("dp"), lax.axis_size("col")
    rows_total = tok_rows * dp
    block_rows = model_width // dp
    sub_chunk = sub_count // CHUNKS
    chunk = sub_chunk * sub_width
    place = jnp.stack([lax.axis_index("dp"), lax.axis_index("col")]).astype(jnp.int32)

    columns = columns_of_all(place, embeddings, dp, col)
    codes_t = codes.T.astype(jnp.bfloat16)
    all_codes = [
        lax.all_gather(codes_t[first : first + sub_chunk], "dp")
        for first in range(0, sub_count, sub_chunk)
    ]

    table = jnp.transpose(codebooks, (0, 2, 1)).astype(jnp.float32)
    own = rebuild_rows(place, codes_t[None], table)
    rotated = lax.dot_general(
        rotation, embeddings, (((0,), (1,)), ((), ())), preferred_element_type=jnp.float32
    )
    residue = rotated - own.astype(jnp.float32)
    row_error = lax.psum(jnp.sum(residue * residue, axis=0), "col")
    weights = lax.all_gather(1.0 / (1.0 + row_error / (2.0 * model_width)), "dp")
    order = lax.rem(place[0] + dp - jnp.arange(dp, dtype=jnp.int32), dp)
    weights = jnp.take(weights, order, axis=0, mode="clip")
    scaled = (weights[:, :, None] * columns.astype(jnp.float32)).astype(jnp.bfloat16)
    scaled = scaled.reshape(rows_total, block_rows)

    start_row = lax.axis_index("dp") * block_rows
    prior = lax.dynamic_slice_in_dim(rotation, start_row, block_rows, 0).T
    blocks, pieces = [], []
    for index in range(CHUNKS):
        table_part = table[index * sub_chunk : (index + 1) * sub_chunk]
        rebuilt = rebuild_rows(place, all_codes[index], table_part)
        cross = jnp.dot(rebuilt, scaled, preferred_element_type=jnp.float32)
        prior_part = prior[index * chunk : (index + 1) * chunk].astype(jnp.float32)
        blocks.append(cross + 0.2 * rows_total * prior_part)
        pieces.append(lax.all_gather(blocks[-1].astype(jnp.bfloat16), "dp"))

    start = jnp.concatenate(blocks, axis=0)
    inner, square = apply_first(start.T.astype(jnp.bfloat16), pieces)
    squares = both_cores(square)
    first, inner = apply_next(0, both_cores(inner), squares, [start], pieces)
    state, inner = apply_next(1, both_cores(inner), squares, [first], pieces)
    state, inner = apply_next(2, both_cores(inner), squares, [state], pieces)
    return apply_next(3, both_cores(inner), squares, [state, first], pieces)


def solution(mesh):
    placed = (P("dp", None), P(None, "col"), P("dp", "col"), P("col", None, None))
    return jax.shard_map(
        shards, mesh=mesh, in_specs=placed, out_specs=P("dp", "col"), check_vma=False
    )
```

```python
import functools
import math

import jax
import jax.numpy as jnp
from jax import lax
from jax.experimental import pallas as pl
from jax.experimental.pallas import tpu as pltpu
from jax.sharding import PartitionSpec as P

LANES = 128
GROUP = 8
CHUNKS = 4
INNER = 4
VMEM_BYTES = 52 * 1024 * 1024
ANY = pl.BlockSpec(memory_space=pl.ANY)
VMEM = pl.BlockSpec(memory_space=pltpu.VMEM)


def lookup_kernel(codes_ref, table_ref, out_ref, ids_ref):
    subs, rows = codes_ref.shape[1:]
    width = table_ref.shape[1]
    halves = table_ref.shape[2] // LANES
    ids_ref[...] = codes_ref[0].astype(jnp.float32).astype(jnp.int32)

    def body(step, carry):
        base = pl.multiple_of(step * GROUP, GROUP)
        for first in range(0, rows, LANES):
            ids_all = ids_ref[pl.ds(base, GROUP), first : first + LANES]
            for pair in range(0, GROUP, 2):
                both = []
                for sub in (pair, pair + 1):
                    ids = jnp.broadcast_to(ids_all[sub : sub + 1], (width, LANES))
                    lane = jnp.bitwise_and(ids, LANES - 1)
                    picked = None
                    for half in range(halves):
                        entries = table_ref[base + sub, :, half * LANES : (half + 1) * LANES]
                        got = jnp.take_along_axis(
                            entries, lane, axis=1, mode="promise_in_bounds"
                        )
                        picked = got if half == 0 else jnp.where(ids >= half * LANES, got, picked)
                    both.append(picked)
                out_ref[
                    pl.ds(pl.multiple_of((base + pair) * width, 2 * width), 2 * width),
                    first : first + LANES,
                ] = jnp.concatenate(both, axis=0).astype(out_ref.dtype)
        return carry

    lax.fori_loop(0, subs // GROUP, body, 0)


def rebuild_rows(codes, table):
    blocks, subs, rows = codes.shape
    width, centroids = table.shape[1:]
    tile = min(64, subs)
    return pl.pallas_call(
        lookup_kernel,
        grid=(subs // tile, blocks),
        in_specs=[
            pl.BlockSpec((1, tile, rows), lambda m, s: (s, m, 0)),
            pl.BlockSpec((tile, width, centroids), lambda m, s: (m, 0, 0)),
        ],
        out_specs=pl.BlockSpec((tile * width, rows), lambda m, s: (m, s)),
        scratch_shapes=[pltpu.VMEM((tile, rows), jnp.int32)],
        out_shape=jax.ShapeDtypeStruct((subs * width, blocks * rows), jnp.bfloat16),
        compiler_params=pltpu.CompilerParams(vmem_limit_bytes=VMEM_BYTES),
        name="lookup",
    )(codes, table)


def load_panel(gathered, panel_ref, sems):
    dp, cols, block = gathered.shape
    chunk = cols // CHUNKS

    def copy(index, owner):
        span = pl.ds(pl.multiple_of(index * chunk, chunk), chunk)
        return pltpu.make_async_copy(
            gathered.at[owner, span],
            panel_ref.at[span, pl.ds(pl.multiple_of(owner * block, block), block)],
            sems.at[index, owner],
        )

    def start(index, carry):
        for owner in range(dp):
            copy(index, owner).start()
        return carry

    def wait(index):
        for owner in range(dp):
            copy(index, owner).wait()

    lax.fori_loop(0, CHUNKS, start, 0)
    return chunk, wait


def first_kernel(own_ref, gathered_ref, inner_ref, square_ref, panel_ref, total_ref, sems):
    chunk, wait = load_panel(gathered_ref, panel_ref, sems)
    square_ref[...] = jnp.zeros_like(square_ref)
    total_ref[...] = jnp.zeros_like(total_ref)
    wide = square_ref.shape[1]

    def body(index, carry):
        wait(index)
        rows = pl.ds(pl.multiple_of(index * chunk, chunk), chunk)

        def part(step, carry):
            span = pl.ds(pl.multiple_of(step * wide, wide), wide)
            values = panel_ref[rows, span]
            total_ref[:, span] += jnp.dot(
                own_ref[:, rows], values, preferred_element_type=jnp.float32
            )
            values = values.astype(jnp.float32)
            square_ref[...] += jnp.sum((values * values).reshape(chunk // 8, 8, wide), axis=0)
            return carry

        return lax.fori_loop(0, panel_ref.shape[1] // wide, part, carry)

    lax.fori_loop(0, CHUNKS, body, 0)
    inner_ref[...] = total_ref[...].astype(inner_ref.dtype)


def next_kernel(step, mine_square_ref, other_square_ref, mine_any, other_any, *refs):
    last = step == 3
    states = 2 if last else 1
    held, refs = refs[:states], refs[states:]
    if last:
        gathered_ref, out_ref, panel_ref, mine_ref, other_ref, sum_ref, panel_sems, sems = refs
    else:
        (gathered_ref, state_ref, inner_ref, panel_ref, mine_ref, other_ref, sum_ref, value_ref,
         panel_sems, sems) = refs
    copies = [
        pltpu.make_async_copy(mine_any, mine_ref, sems.at[0]),
        pltpu.make_async_copy(other_any, other_ref, sems.at[1]),
    ]
    for copy in copies:
        copy.start()
    chunk, wait = load_panel(gathered_ref, panel_ref, panel_sems)
    model_width = panel_ref.shape[1]
    wide = 512
    total = jnp.sum(mine_square_ref[...] + other_square_ref[...], axis=(0, 1), keepdims=True)
    scale = model_width / (1.96 * total)
    for copy in copies:
        copy.wait()

    def turn(index, carry):
        span = pl.ds(pl.multiple_of(index * wide, wide), wide)
        both = mine_ref[:, span].astype(jnp.float32) + other_ref[:, span].astype(jnp.float32)
        sum_ref[span, :] = (both * scale).T.astype(sum_ref.dtype)
        return carry

    lax.fori_loop(0, model_width // wide, turn, 0)

    def body(index, carry):
        wait(index)
        span = pl.ds(pl.multiple_of(index * chunk, chunk), chunk)
        made = jnp.dot(panel_ref[span, :], sum_ref[...], preferred_element_type=jnp.float32)
        if step != 2:
            made = 1.5 * held[0][span, :] - 0.5 * made
        if last:
            made = (1.5 * held[1][span, :] - 0.5 * made) * (math.sqrt(model_width) * jnp.sqrt(scale))
            out_ref[:, span] = made.T
        else:
            state_ref[span, :] = made
            value_ref[:, span] = made.T.astype(value_ref.dtype)
        return carry

    lax.fori_loop(0, CHUNKS, body, 0)
    if last:
        return

    def product(index, carry):
        span = pl.ds(pl.multiple_of(index * wide, wide), wide)
        inner_ref[:, span] = jnp.dot(
            value_ref[...], panel_ref[:, span], preferred_element_type=jnp.float32
        ).astype(inner_ref.dtype)
        return carry

    lax.fori_loop(0, model_width // wide, product, 0)


def apply_first(own, gathered):
    dp, cols, block = gathered.shape
    return pl.pallas_call(
        first_kernel,
        in_specs=[VMEM, ANY],
        out_specs=[VMEM, VMEM],
        out_shape=[
            jax.ShapeDtypeStruct((block, dp * block), jnp.bfloat16),
            jax.ShapeDtypeStruct((8, 512), jnp.float32),
        ],
        scratch_shapes=[
            pltpu.VMEM((cols, dp * block), jnp.bfloat16),
            pltpu.VMEM((block, dp * block), jnp.float32),
            pltpu.SemaphoreType.DMA((CHUNKS, dp)),
        ],
        compiler_params=pltpu.CompilerParams(vmem_limit_bytes=VMEM_BYTES),
        name="first",
    )(own, gathered)


def apply_next(step, inner, squares, held, gathered):
    dp, cols, block = gathered.shape
    last = step == 3
    if last:
        out_shape = jax.ShapeDtypeStruct((block, cols), jnp.float32)
        value = []
    else:
        out_shape = [
            jax.ShapeDtypeStruct((cols, block), jnp.float32),
            jax.ShapeDtypeStruct((block, dp * block), jnp.bfloat16),
        ]
        value = [pltpu.VMEM((block, cols), jnp.bfloat16)]
    return pl.pallas_call(
        functools.partial(next_kernel, step),
        in_specs=[VMEM, VMEM, ANY, ANY] + [VMEM] * len(held) + [ANY],
        out_specs=VMEM if last else [VMEM, VMEM],
        out_shape=out_shape,
        scratch_shapes=[
            pltpu.VMEM((cols, dp * block), jnp.bfloat16),
            pltpu.VMEM((block, dp * block), jnp.bfloat16),
            pltpu.VMEM((block, dp * block), jnp.bfloat16),
            pltpu.VMEM((dp * block, block), jnp.bfloat16),
        ]
        + value
        + [pltpu.SemaphoreType.DMA((CHUNKS, dp)), pltpu.SemaphoreType.DMA((2,))],
        compiler_params=pltpu.CompilerParams(vmem_limit_bytes=VMEM_BYTES),
        name="apply%d" % step,
    )(*squares, *inner, *held, gathered)


def swap_cores(value):
    return lax.ppermute(value, "col", [(0, 1), (1, 0)])


def both_cores(value):
    if lax.axis_size("col") == 2:
        return value, swap_cores(value)
    total = lax.psum(value.astype(jnp.float32), "col").astype(value.dtype)
    return total, jnp.zeros_like(total)


def shards(embeddings, rotation, codes, codebooks):
    tok_rows, model_width = embeddings.shape
    dp, col = lax.axis_size("dp"), lax.axis_size("col")
    rows_total = tok_rows * dp
    block = model_width // dp
    inner_size = math.gcd(dp, INNER)
    outer_size = dp // inner_size
    wide = model_width // outer_size
    part_rows = tok_rows // col
    outer, inner = lax.axis_index("dp") // inner_size, lax.axis_index("dp") % inner_size
    core = lax.axis_index("col")

    def from_outer(value, step):
        pairs = [(i, (i // inner_size ^ step) * inner_size + i % inner_size) for i in range(dp)]
        return lax.ppermute(value, "dp", pairs)

    def from_inner(value, step):
        pairs = [(i, i // inner_size * inner_size + (i % inner_size ^ step)) for i in range(dp)]
        return lax.ppermute(value, "dp", pairs)

    steps = list(range(1, outer_size))
    shares = []
    for step in steps:
        send = lax.dynamic_slice(
            embeddings, (core * part_rows, (outer ^ step) * wide), (part_rows, wide)
        )
        shares.append(from_outer(send, step))
    codes_t = codes.T.astype(jnp.bfloat16)
    group_codes = jnp.stack([codes_t] + [from_outer(codes_t, step) for step in steps])
    columns = [lax.dynamic_slice_in_dim(embeddings, outer * wide, wide, 1)]
    for share in shares:
        if col == 2:
            other = swap_cores(share)
            pair = [jnp.where(core == 0, share, other), jnp.where(core == 0, other, share)]
            columns.append(jnp.concatenate(pair, axis=0))
        else:
            columns.append(lax.all_gather(share, "col", axis=0, tiled=True))

    table = jnp.transpose(codebooks, (0, 2, 1)).astype(jnp.float32)
    own = rebuild_rows(codes_t[None], table)
    rotated = lax.dot_general(
        rotation, embeddings, (((0,), (1,)), ((), ())), preferred_element_type=jnp.float32
    )
    residue = rotated - own.astype(jnp.float32)
    row_error = lax.psum(jnp.sum(residue * residue, axis=0), "col")
    weights = 1.0 / (1.0 + row_error / (2.0 * model_width))
    group_weights = [weights] + [from_outer(weights, step) for step in steps]
    scaled = jnp.concatenate(
        [
            (weight[:, None] * part.astype(jnp.float32)).astype(jnp.bfloat16)
            for weight, part in zip(group_weights, columns)
        ],
        axis=0,
    )

    rebuilt = rebuild_rows(group_codes, table)

    def group_block(step):
        part = lax.dynamic_slice_in_dim(scaled, (inner ^ step) * block, block, 1)
        return jnp.dot(rebuilt, part, preferred_element_type=jnp.float32)

    parts = [
        from_inner(group_block(step).astype(jnp.bfloat16), step)
        for step in reversed(range(1, inner_size))
    ]
    start_row = lax.axis_index("dp") * block
    prior = lax.dynamic_slice_in_dim(rotation, start_row, block, 0).T
    start = group_block(0) + 0.2 * rows_total * prior.astype(jnp.float32)
    for part in parts:
        start = start + part.astype(jnp.float32)
    narrow = start.astype(jnp.bfloat16)
    gathered = lax.all_gather(narrow, "dp")

    inner, square = apply_first(narrow.T, gathered)
    squares = both_cores(square)
    first, inner = apply_next(0, both_cores(inner), squares, [start], gathered)
    state, inner = apply_next(1, both_cores(inner), squares, [first], gathered)
    state, inner = apply_next(2, both_cores(inner), squares, [state], gathered)
    return apply_next(3, both_cores(inner), squares, [state, first], gathered)


def solution(mesh):
    placed = (P("dp", None), P(None, "col"), P("dp", "col"), P("col", None, None))
    return jax.shard_map(
        shards, mesh=mesh, in_specs=placed, out_specs=P("dp", "col"), check_vma=False
    )
```

```python
import functools
import math

import jax
import jax.numpy as jnp
from jax import lax
from jax.experimental import pallas as pl
from jax.experimental.pallas import tpu as pltpu
from jax.sharding import PartitionSpec as P

LANES = 128
GROUP = 8
CHUNKS = 4
INNER = 4
VMEM_BYTES = 24 * 1024 * 1024
ANY = pl.BlockSpec(memory_space=pl.ANY)
VMEM = pl.BlockSpec(memory_space=pltpu.VMEM)


def lookup_kernel(codes_ref, table_ref, out_ref, ids_ref):
    subs, rows = codes_ref.shape[1:]
    width = table_ref.shape[1]
    halves = table_ref.shape[2] // LANES
    ids_ref[...] = codes_ref[0].astype(jnp.float32).astype(jnp.int32)

    def body(step, carry):
        base = pl.multiple_of(step * GROUP, GROUP)
        for first in range(0, rows, LANES):
            ids_all = ids_ref[pl.ds(base, GROUP), first : first + LANES]
            for pair in range(0, GROUP, 2):
                both = []
                for sub in (pair, pair + 1):
                    ids = jnp.broadcast_to(ids_all[sub : sub + 1], (width, LANES))
                    lane = jnp.bitwise_and(ids, LANES - 1)
                    picked = None
                    for half in range(halves):
                        entries = table_ref[base + sub, :, half * LANES : (half + 1) * LANES]
                        got = jnp.take_along_axis(
                            entries, lane, axis=1, mode="promise_in_bounds"
                        )
                        picked = got if half == 0 else jnp.where(ids >= half * LANES, got, picked)
                    both.append(picked)
                out_ref[
                    pl.ds(pl.multiple_of((base + pair) * width, 2 * width), 2 * width),
                    first : first + LANES,
                ] = jnp.concatenate(both, axis=0).astype(out_ref.dtype)
        return carry

    lax.fori_loop(0, subs // GROUP, body, 0)


def rebuild_rows(codes, table):
    blocks, subs, rows = codes.shape
    width, centroids = table.shape[1:]
    tile = min(64, subs)
    return pl.pallas_call(
        lookup_kernel,
        grid=(subs // tile, blocks),
        in_specs=[
            pl.BlockSpec((1, tile, rows), lambda m, s: (s, m, 0)),
            pl.BlockSpec((tile, width, centroids), lambda m, s: (m, 0, 0)),
        ],
        out_specs=pl.BlockSpec((tile * width, rows), lambda m, s: (m, s)),
        scratch_shapes=[pltpu.VMEM((tile, rows), jnp.int32)],
        out_shape=jax.ShapeDtypeStruct((subs * width, blocks * rows), jnp.bfloat16),
        compiler_params=pltpu.CompilerParams(vmem_limit_bytes=VMEM_BYTES),
        name="lookup",
    )(codes, table)


def first_kernel(panel_ref, own_ref, inner_ref, square_ref):
    dp, cols, block = panel_ref.shape
    square_ref[...] = jnp.zeros_like(square_ref)

    def body(owner, carry):
        values = panel_ref[owner]
        inner_ref[:, pl.ds(pl.multiple_of(owner * block, block), block)] = jnp.dot(
            own_ref[...], values, preferred_element_type=jnp.float32
        ).astype(inner_ref.dtype)
        values = values.astype(jnp.float32)
        square_ref[...] += jnp.sum((values * values).reshape(cols // 8, 8, block), axis=0)
        return carry

    lax.fori_loop(0, dp, body, 0)


def next_kernel(step, panel_ref, mine_square_ref, other_square_ref, mine_ref, other_ref, *refs):
    last = step == 3
    states = 2 if last else 1
    held, refs = refs[:states], refs[states:]
    if last:
        out_ref, sum_ref = refs
    else:
        state_ref, inner_ref, sum_ref, value_ref = refs
    dp, cols, block = panel_ref.shape
    model_width = dp * block
    chunk = cols // CHUNKS
    total = jnp.sum(mine_square_ref[...] + other_square_ref[...], axis=(0, 1), keepdims=True)
    scale = model_width / (1.96 * total)

    def turn(owner, carry):
        span = pl.ds(pl.multiple_of(owner * block, block), block)
        both = mine_ref[:, span].astype(jnp.float32) + other_ref[:, span].astype(jnp.float32)
        sum_ref[owner] = (both * scale).T.astype(sum_ref.dtype)
        return carry

    lax.fori_loop(0, dp, turn, 0)

    def body(index, carry):
        span = pl.ds(pl.multiple_of(index * chunk, chunk), chunk)
        made = jnp.zeros((chunk, block), jnp.float32)
        for owner in range(dp):
            made += jnp.dot(
                panel_ref[owner, span, :], sum_ref[owner], preferred_element_type=jnp.float32
            )
        if step != 2:
            made = 1.5 * held[0][span, :] - 0.5 * made
        if last:
            made = (1.5 * held[1][span, :] - 0.5 * made) * (math.sqrt(model_width) * jnp.sqrt(scale))
            out_ref[:, span] = made.T
        else:
            state_ref[span, :] = made
            value_ref[:, span] = made.T.astype(value_ref.dtype)
        return carry

    lax.fori_loop(0, CHUNKS, body, 0)
    if last:
        return

    def product(owner, carry):
        inner_ref[:, pl.ds(pl.multiple_of(owner * block, block), block)] = jnp.dot(
            value_ref[...], panel_ref[owner], preferred_element_type=jnp.float32
        ).astype(inner_ref.dtype)
        return carry

    lax.fori_loop(0, dp, product, 0)


def in_vmem(*values):
    return [pltpu.with_memory_space_constraint(value, pltpu.VMEM) for value in values]


def apply_first(panel, own):
    dp, cols, block = panel.shape
    return pl.pallas_call(
        first_kernel,
        in_specs=[VMEM, VMEM],
        out_specs=[VMEM, VMEM],
        out_shape=[
            pltpu.VMEM((block, dp * block), jnp.bfloat16),
            pltpu.VMEM((8, block), jnp.float32),
        ],
        compiler_params=pltpu.CompilerParams(vmem_limit_bytes=VMEM_BYTES),
        name="first",
    )(*in_vmem(panel, own))


def apply_next(step, panel, inner, squares, held):
    dp, cols, block = panel.shape
    last = step == 3
    if last:
        out_shape = jax.ShapeDtypeStruct((block, cols), jnp.float32)
        value = []
    else:
        out_shape = [
            pltpu.VMEM((cols, block), jnp.float32),
            pltpu.VMEM((block, dp * block), jnp.bfloat16),
        ]
        value = [pltpu.VMEM((block, cols), jnp.bfloat16)]
    return pl.pallas_call(
        functools.partial(next_kernel, step),
        in_specs=[VMEM] * (5 + len(held)),
        out_specs=VMEM if last else [VMEM, VMEM],
        out_shape=out_shape,
        scratch_shapes=[pltpu.VMEM((dp, block, block), jnp.bfloat16)] + value,
        compiler_params=pltpu.CompilerParams(vmem_limit_bytes=VMEM_BYTES),
        name="apply%d" % step,
    )(*in_vmem(panel, *squares, *inner, *held))


def swap_cores(value):
    return lax.ppermute(value, "col", [(0, 1), (1, 0)])


def both_cores(value):
    if lax.axis_size("col") == 2:
        return value, swap_cores(value)
    total = lax.psum(value.astype(jnp.float32), "col").astype(value.dtype)
    return total, jnp.zeros_like(total)


def shards(embeddings, rotation, codes, codebooks):
    tok_rows, model_width = embeddings.shape
    dp, col = lax.axis_size("dp"), lax.axis_size("col")
    rows_total = tok_rows * dp
    block = model_width // dp
    inner_size = math.gcd(dp, INNER)
    outer_size = dp // inner_size
    wide = model_width // outer_size
    part_rows = tok_rows // col
    outer, inner = lax.axis_index("dp") // inner_size, lax.axis_index("dp") % inner_size
    core = lax.axis_index("col")

    def from_outer(value, step):
        pairs = [(i, (i // inner_size ^ step) * inner_size + i % inner_size) for i in range(dp)]
        return lax.ppermute(value, "dp", pairs)

    def from_inner(value, step):
        pairs = [(i, i // inner_size * inner_size + (i % inner_size ^ step)) for i in range(dp)]
        return lax.ppermute(value, "dp", pairs)

    steps = list(range(1, outer_size))
    shares = []
    for step in steps:
        send = lax.dynamic_slice(
            embeddings, (core * part_rows, (outer ^ step) * wide), (part_rows, wide)
        )
        shares.append(from_outer(send, step))
    codes_t = codes.T.astype(jnp.bfloat16)
    group_codes = jnp.stack([codes_t] + [from_outer(codes_t, step) for step in steps])
    columns = [lax.dynamic_slice_in_dim(embeddings, outer * wide, wide, 1)]
    for share in shares:
        if col == 2:
            other = swap_cores(share)
            pair = [jnp.where(core == 0, share, other), jnp.where(core == 0, other, share)]
            columns.append(jnp.concatenate(pair, axis=0))
        else:
            columns.append(lax.all_gather(share, "col", axis=0, tiled=True))

    table = jnp.transpose(codebooks, (0, 2, 1)).astype(jnp.float32)
    own = rebuild_rows(codes_t[None], table)
    rotated = lax.dot_general(
        rotation, embeddings, (((0,), (1,)), ((), ())), preferred_element_type=jnp.float32
    )
    residue = rotated - own.astype(jnp.float32)
    row_error = lax.psum(jnp.sum(residue * residue, axis=0), "col")
    weights = 1.0 / (1.0 + row_error / (2.0 * model_width))
    group_weights = [weights] + [from_outer(weights, step) for step in steps]
    scaled = jnp.concatenate(
        [
            (weight[:, None] * part.astype(jnp.float32)).astype(jnp.bfloat16)
            for weight, part in zip(group_weights, columns)
        ],
        axis=0,
    )

    rebuilt = rebuild_rows(group_codes, table)

    def group_block(step):
        part = lax.dynamic_slice_in_dim(scaled, (inner ^ step) * block, block, 1)
        return jnp.dot(rebuilt, part, preferred_element_type=jnp.float32)

    parts = [
        from_inner(group_block(step).astype(jnp.bfloat16), step)
        for step in reversed(range(1, inner_size))
    ]
    start_row = lax.axis_index("dp") * block
    prior = lax.dynamic_slice_in_dim(rotation, start_row, block, 0).T
    start = lax.optimization_barrier(group_block(0)) + 0.2 * rows_total * prior.astype(jnp.float32)
    for part in parts:
        start = start + part.astype(jnp.float32)
    narrow = start.astype(jnp.bfloat16)
    panel = lax.all_gather(narrow, "dp")

    inner, square = apply_first(panel, narrow.T)
    squares = both_cores(square)
    first, inner = apply_next(0, panel, both_cores(inner), squares, [start])
    state, inner = apply_next(1, panel, both_cores(inner), squares, [first])
    state, inner = apply_next(2, panel, both_cores(inner), squares, [state])
    return apply_next(3, panel, both_cores(inner), squares, [state, first])


def solution(mesh):
    placed = (P("dp", None), P(None, "col"), P("dp", "col"), P("col", None, None))
    return jax.shard_map(
        shards, mesh=mesh, in_specs=placed, out_specs=P("dp", "col"), check_vma=False
    )
```

```python
import functools
import math

import jax
import jax.numpy as jnp
from jax import lax
from jax.experimental import pallas as pl
from jax.experimental.pallas import tpu as pltpu
from jax.sharding import PartitionSpec as P

LANES = 128
GROUP = 8
CHUNKS = 4
INNER = 4
VMEM_BYTES = 24 * 1024 * 1024
ANY = pl.BlockSpec(memory_space=pl.ANY)
VMEM = pl.BlockSpec(memory_space=pltpu.VMEM)


def lookup_kernel(codes_ref, table_ref, out_ref, ids_ref):
    subs, rows = codes_ref.shape[1:]
    width = table_ref.shape[1]
    halves = table_ref.shape[2] // LANES
    ids_ref[...] = codes_ref[0].astype(jnp.float32).astype(jnp.int32)

    def body(step, carry):
        base = pl.multiple_of(step * GROUP, GROUP)
        for first in range(0, rows, LANES):
            ids_all = ids_ref[pl.ds(base, GROUP), first : first + LANES]
            for pair in range(0, GROUP, 2):
                both = []
                for sub in (pair, pair + 1):
                    ids = jnp.broadcast_to(ids_all[sub : sub + 1], (width, LANES))
                    lane = jnp.bitwise_and(ids, LANES - 1)
                    picked = None
                    for half in range(halves):
                        entries = table_ref[base + sub, :, half * LANES : (half + 1) * LANES]
                        got = jnp.take_along_axis(
                            entries, lane, axis=1, mode="promise_in_bounds"
                        )
                        picked = got if half == 0 else jnp.where(ids >= half * LANES, got, picked)
                    both.append(picked)
                out_ref[
                    pl.ds(pl.multiple_of((base + pair) * width, 2 * width), 2 * width),
                    first : first + LANES,
                ] = jnp.concatenate(both, axis=0).astype(out_ref.dtype)
        return carry

    lax.fori_loop(0, subs // GROUP, body, 0)


def rebuild_rows(codes, table):
    blocks, subs, rows = codes.shape
    width, centroids = table.shape[1:]
    tile = min(64, subs)
    return pl.pallas_call(
        lookup_kernel,
        grid=(subs // tile, blocks),
        in_specs=[
            pl.BlockSpec((1, tile, rows), lambda m, s: (s, m, 0)),
            pl.BlockSpec((tile, width, centroids), lambda m, s: (m, 0, 0)),
        ],
        out_specs=pl.BlockSpec((tile * width, rows), lambda m, s: (m, s)),
        scratch_shapes=[pltpu.VMEM((tile, rows), jnp.int32)],
        out_shape=jax.ShapeDtypeStruct((subs * width, blocks * rows), jnp.bfloat16),
        compiler_params=pltpu.CompilerParams(vmem_limit_bytes=VMEM_BYTES),
        name="lookup",
    )(codes, table)


def first_kernel(own_ref, before_ref, *refs):
    panel, (inner_ref, square_ref) = refs[:-2], refs[-2:]
    cols, block = panel[0].shape
    square = before_ref[...]
    for index, block_ref in enumerate(panel):
        values = block_ref[...]
        inner_ref[:, index * block : (index + 1) * block] = jnp.dot(
            own_ref[...], values, preferred_element_type=jnp.float32
        ).astype(inner_ref.dtype)
        values = values.astype(jnp.float32)
        square += jnp.sum((values * values).reshape(cols // 8, 8, block), axis=0)
    square_ref[...] = square


def next_kernel(step, blocks, parts, mine_square_ref, other_square_ref, *refs):
    last = step == 3
    states = 2 if last else 1
    panel, refs = refs[:blocks], refs[blocks:]
    mine, other, refs = refs[:parts], refs[parts : 2 * parts], refs[2 * parts :]
    held, refs = refs[:states], refs[states:]
    if last:
        out_ref, sum_ref = refs
    else:
        state_ref, inner_ref, sum_ref, value_ref = refs
    cols, block = panel[0].shape
    model_width = blocks * block
    chunk = cols // CHUNKS
    total = jnp.sum(mine_square_ref[...] + other_square_ref[...], axis=(0, 1), keepdims=True)
    scale = model_width / (1.96 * total)
    index = 0
    for mine_ref, other_ref in zip(mine, other):
        for first in range(0, mine_ref.shape[1], block):
            both = mine_ref[:, first : first + block].astype(jnp.float32)
            both += other_ref[:, first : first + block].astype(jnp.float32)
            sum_ref[index] = (both * scale).T.astype(sum_ref.dtype)
            index += 1

    def body(index, carry):
        span = pl.ds(pl.multiple_of(index * chunk, chunk), chunk)
        made = jnp.zeros((chunk, block), jnp.float32)
        for owner in range(blocks):
            made += jnp.dot(
                panel[owner][span, :], sum_ref[owner], preferred_element_type=jnp.float32
            )
        if step != 2:
            made = 1.5 * held[0][span, :] - 0.5 * made
        if last:
            made = (1.5 * held[1][span, :] - 0.5 * made) * (math.sqrt(model_width) * jnp.sqrt(scale))
            out_ref[:, span] = made.T
        else:
            state_ref[span, :] = made
            value_ref[:, span] = made.T.astype(value_ref.dtype)
        return carry

    lax.fori_loop(0, CHUNKS, body, 0)
    if last:
        return
    for index in range(blocks):
        inner_ref[:, index * block : (index + 1) * block] = jnp.dot(
            value_ref[...], panel[index][...], preferred_element_type=jnp.float32
        ).astype(inner_ref.dtype)


def in_vmem(*values):
    return [pltpu.with_memory_space_constraint(value, pltpu.VMEM) for value in values]


def apply_first(own, square, panel):
    block = panel[0].shape[1]
    return pl.pallas_call(
        first_kernel,
        in_specs=[VMEM] * (2 + len(panel)),
        out_specs=[VMEM, VMEM],
        out_shape=[
            pltpu.VMEM((block, len(panel) * block), jnp.bfloat16),
            pltpu.VMEM((8, block), jnp.float32),
        ],
        compiler_params=pltpu.CompilerParams(vmem_limit_bytes=VMEM_BYTES),
        name="first",
    )(*in_vmem(own, square, *panel))


def apply_next(step, panel, inner, squares, held):
    cols, block = panel[0].shape
    blocks = len(panel)
    last = step == 3
    if last:
        out_shape = jax.ShapeDtypeStruct((block, cols), jnp.float32)
        value = []
    else:
        out_shape = [
            pltpu.VMEM((cols, block), jnp.float32),
            pltpu.VMEM((block, blocks * block), jnp.bfloat16),
        ]
        value = [pltpu.VMEM((block, cols), jnp.bfloat16)]
    mine, other = zip(*inner)
    operands = in_vmem(*squares, *panel, *mine, *other, *held)
    return pl.pallas_call(
        functools.partial(next_kernel, step, blocks, len(inner)),
        in_specs=[VMEM] * len(operands),
        out_specs=VMEM if last else [VMEM, VMEM],
        out_shape=out_shape,
        scratch_shapes=[pltpu.VMEM((blocks, block, block), jnp.bfloat16)] + value,
        compiler_params=pltpu.CompilerParams(vmem_limit_bytes=VMEM_BYTES),
        name="apply%d" % step,
    )(*operands)


def swap_cores(value):
    return lax.ppermute(value, "col", [(0, 1), (1, 0)])


def both_cores(value):
    if lax.axis_size("col") == 2:
        return value, swap_cores(value)
    total = lax.psum(value.astype(jnp.float32), "col").astype(value.dtype)
    return total, jnp.zeros_like(total)


def gather_rounds(outer_size):
    held = {(0, 0)}
    last = outer_size - 1
    rounds = []
    for k in range(1, outer_size):
        rounds.append([((k, 0), (k - 1, 0)), ((k - 1, 1), (k - 1, 0)), ((k - 1, 2), (k - 1, 0))])
    held.update(key for moves in rounds for key, _ in moves)
    rest = [(last, 1), (last, 2)] + [(k, 3) for k in range(outer_size)]
    while rest:
        moves, taken = [], set()
        for key in rest:
            ways = [("y", (key[0], key[1] ^ 2)), ("x", (key[0], key[1] ^ 1)), ("z", (key[0] - 1, key[1]))]
            if key == (last, 1):
                ways.reverse()
            if key[1] == 3:
                ways = ways[::-1] if (key[0] - 1, 3) in held else ways
            for link, source in ways:
                if source in held and link not in taken:
                    taken.add(link)
                    moves.append((key, source))
                    break
        held.update(key for key, _ in moves)
        rest = [key for key in rest if key not in held]
        rounds.append(moves)
    return rounds


def shards(embeddings, rotation, codes, codebooks):
    tok_rows, model_width = embeddings.shape
    dp, col = lax.axis_size("dp"), lax.axis_size("col")
    rows_total = tok_rows * dp
    block = model_width // dp
    inner_size = math.gcd(dp, INNER)
    outer_size = dp // inner_size
    wide = model_width // outer_size
    part_rows = tok_rows // col
    outer, inner = lax.axis_index("dp") // inner_size, lax.axis_index("dp") % inner_size
    core = lax.axis_index("col")

    def from_outer(value, step):
        pairs = [(i, (i // inner_size ^ step) * inner_size + i % inner_size) for i in range(dp)]
        return lax.ppermute(value, "dp", pairs)

    def from_inner(value, step):
        pairs = [(i, i // inner_size * inner_size + (i % inner_size ^ step)) for i in range(dp)]
        return lax.ppermute(value, "dp", pairs)

    steps = list(range(1, outer_size))
    sends = [
        lax.dynamic_slice(embeddings, (core * part_rows, (outer ^ step) * wide), (part_rows, wide))
        for step in steps
    ]
    codes_t = codes.T.astype(jnp.bfloat16)
    group_codes = [codes_t] + [from_outer(codes_t, step) for step in steps]
    sends[0], group_codes = lax.optimization_barrier((sends[0], group_codes))
    shares = [from_outer(send, step) for send, step in zip(sends, steps)]
    table = jnp.transpose(codebooks, (0, 2, 1)).astype(jnp.float32)
    rebuilt = rebuild_rows(jnp.stack(group_codes), table)

    own = rebuild_rows(codes_t[None], table)
    rotated = lax.dot_general(
        rotation, embeddings, (((0,), (1,)), ((), ())), preferred_element_type=jnp.float32
    )
    residue = rotated - own.astype(jnp.float32)
    row_error = lax.psum(jnp.sum(residue * residue, axis=0), "col")
    weights = 1.0 / (1.0 + row_error / (2.0 * model_width))
    group_weights = [weights] + [from_outer(weights, step) for step in steps]

    shares, rebuilt, group_weights = lax.optimization_barrier((shares, rebuilt, group_weights))
    columns = [lax.dynamic_slice_in_dim(embeddings, outer * wide, wide, 1)]
    for share in shares:
        if col == 2:
            other = swap_cores(share)
            pair = [jnp.where(core == 0, share, other), jnp.where(core == 0, other, share)]
            columns.append(jnp.concatenate(pair, axis=0))
        else:
            columns.append(lax.all_gather(share, "col", axis=0, tiled=True))
    scaled = jnp.concatenate(
        [
            (weight[:, None] * part.astype(jnp.float32)).astype(jnp.bfloat16)
            for weight, part in zip(group_weights, columns)
        ],
        axis=0,
    )


    def group_block(step):
        part = lax.dynamic_slice_in_dim(scaled, (inner ^ step) * block, block, 1)
        return jnp.dot(rebuilt, part, preferred_element_type=jnp.float32)

    parts = [
        from_inner(group_block(step).astype(jnp.bfloat16), step)
        for step in reversed(range(1, inner_size))
    ]
    start_row = lax.axis_index("dp") * block
    prior = lax.dynamic_slice_in_dim(rotation, start_row, block, 0).T
    start = lax.optimization_barrier(group_block(0)) + 0.2 * rows_total * prior.astype(jnp.float32)
    for part in parts:
        start = start + part.astype(jnp.float32)
    narrow = start.astype(jnp.bfloat16)

    def ring(value):
        pairs = [(i, (i + inner_size) % dp) for i in range(dp)]
        return lax.ppermute(value, "dp", pairs)

    def move(key, source):
        if key[0] != source[0]:
            return ring(held[source])
        return from_inner(held[source], key[1] ^ source[1])

    own = narrow.T
    held = {(0, 0): narrow}
    order, products = [(0, 0)], []
    square = jnp.zeros((8, block), jnp.float32)
    fresh = [narrow]
    for moves in gather_rounds(outer_size):
        arrived = [move(key, source) for key, source in moves]
        product, square = apply_first(own, square, fresh)
        arrived, product, square = lax.optimization_barrier((arrived, product, square))
        held.update({key: value for (key, _), value in zip(moves, arrived)})
        order += [key for key, _ in moves]
        products.append(both_cores(product))
        fresh = arrived
    product, square = apply_first(own, square, fresh)
    products.append(both_cores(product))
    panel = [held[key] for key in order]
    squares = both_cores(square)
    first, product = apply_next(0, panel, products, squares, [start])
    state, product = apply_next(1, panel, [both_cores(product)], squares, [first])
    state, product = apply_next(2, panel, [both_cores(product)], squares, [state])
    return apply_next(3, panel, [both_cores(product)], squares, [state, first])


def solution(mesh):
    placed = (P("dp", None), P(None, "col"), P("dp", "col"), P("col", None, None))
    return jax.shard_map(
        shards, mesh=mesh, in_specs=placed, out_specs=P("dp", "col"), check_vma=False
    )
```

```python
import functools
import math

import jax
import jax.numpy as jnp
from jax import lax
from jax.experimental import pallas as pl
from jax.experimental.pallas import tpu as pltpu
from jax.sharding import PartitionSpec as P

LANES = 128
GROUP = 8
CHUNKS = 4
INNER = 4
VMEM_BYTES = 24 * 1024 * 1024
ANY = pl.BlockSpec(memory_space=pl.ANY)
VMEM = pl.BlockSpec(memory_space=pltpu.VMEM)


def lookup_kernel(codes_ref, table_ref, out_ref, ids_ref):
    subs, rows = codes_ref.shape[1:]
    width = table_ref.shape[1]
    halves = table_ref.shape[2] // LANES
    ids_ref[...] = codes_ref[0].astype(jnp.float32).astype(jnp.int32)

    def body(step, carry):
        base = pl.multiple_of(step * GROUP, GROUP)
        for first in range(0, rows, LANES):
            ids_all = ids_ref[pl.ds(base, GROUP), first : first + LANES]
            for pair in range(0, GROUP, 2):
                both = []
                for sub in (pair, pair + 1):
                    ids = jnp.broadcast_to(ids_all[sub : sub + 1], (width, LANES))
                    lane = jnp.bitwise_and(ids, LANES - 1)
                    picked = None
                    for half in range(halves):
                        entries = table_ref[base + sub, :, half * LANES : (half + 1) * LANES]
                        got = jnp.take_along_axis(
                            entries, lane, axis=1, mode="promise_in_bounds"
                        )
                        picked = got if half == 0 else jnp.where(ids >= half * LANES, got, picked)
                    both.append(picked)
                out_ref[
                    pl.ds(pl.multiple_of((base + pair) * width, 2 * width), 2 * width),
                    first : first + LANES,
                ] = jnp.concatenate(both, axis=0).astype(out_ref.dtype)
        return carry

    lax.fori_loop(0, subs // GROUP, body, 0)


def rebuild_rows(codes, table):
    blocks, subs, rows = codes.shape
    width, centroids = table.shape[1:]
    tile = min(64, subs)
    return pl.pallas_call(
        lookup_kernel,
        grid=(subs // tile, blocks),
        in_specs=[
            pl.BlockSpec((1, tile, rows), lambda m, s: (s, m, 0)),
            pl.BlockSpec((tile, width, centroids), lambda m, s: (m, 0, 0)),
        ],
        out_specs=pl.BlockSpec((tile * width, rows), lambda m, s: (m, s)),
        scratch_shapes=[pltpu.VMEM((tile, rows), jnp.int32)],
        out_shape=jax.ShapeDtypeStruct((subs * width, blocks * rows), jnp.bfloat16),
        compiler_params=pltpu.CompilerParams(vmem_limit_bytes=VMEM_BYTES),
        name="lookup",
    )(codes, table)


def product_of(value_ref, block_ref, inner_ref, index):
    block = block_ref.shape[1]
    product = jnp.dot(value_ref[...], block_ref[...], preferred_element_type=jnp.float32)
    inner_ref[index * block : (index + 1) * block, :] = product.T.astype(inner_ref.dtype)


def first_kernel(own_ref, before_ref, *refs):
    panel, (inner_ref, square_ref) = refs[:-2], refs[-2:]
    cols, block = panel[0].shape
    square = before_ref[...]
    for index, block_ref in enumerate(panel):
        product_of(own_ref, block_ref, inner_ref, index)
        values = block_ref[...].astype(jnp.float32)
        square += jnp.sum((values * values).reshape(cols // 8, 8, block), axis=0)
    square_ref[...] = square


def next_kernel(step, blocks, parts, mine_square_ref, other_square_ref, *refs):
    last = step == 3
    states = 2 if last else 1
    panel, refs = refs[:blocks], refs[blocks:]
    mine, other, refs = refs[:parts], refs[parts : 2 * parts], refs[2 * parts :]
    held, refs = refs[:states], refs[states:]
    if last:
        out_ref, sum_ref = refs
    else:
        state_ref, inner_ref, sum_ref, value_ref = refs
    cols, block = panel[0].shape
    model_width = blocks * block
    chunk = cols // CHUNKS
    total = jnp.sum(mine_square_ref[...] + other_square_ref[...], axis=(0, 1), keepdims=True)
    scale = model_width / (1.96 * total)
    first = 0
    for mine_ref, other_ref in zip(mine, other):
        sum_ref[first : first + mine_ref.shape[0], :] = mine_ref[...] + other_ref[...]
        first += mine_ref.shape[0]

    for index in range(CHUNKS):
        span = slice(index * chunk, (index + 1) * chunk)
        made = jnp.zeros((chunk, block), jnp.float32)
        for owner in range(blocks):
            made += jnp.dot(
                panel[owner][span, :],
                sum_ref[owner * block : (owner + 1) * block, :],
                preferred_element_type=jnp.float32,
            )
        if step == 2:
            made = made * scale
        else:
            made = 1.5 * held[0][span, :] - (0.5 * scale) * made
        if last:
            made = (1.5 * held[1][span, :] - 0.5 * made) * (math.sqrt(model_width) * jnp.sqrt(scale))
            out_ref[:, span] = made.T
        else:
            state_ref[span, :] = made
            value_ref[:, span] = made.T.astype(value_ref.dtype)
    if last:
        return
    for index in range(blocks):
        product_of(value_ref, panel[index], inner_ref, index)


def in_vmem(*values):
    return [pltpu.with_memory_space_constraint(value, pltpu.VMEM) for value in values]


def apply_first(own, square, panel):
    block = panel[0].shape[1]
    return pl.pallas_call(
        first_kernel,
        in_specs=[VMEM] * (2 + len(panel)),
        out_specs=[VMEM, VMEM],
        out_shape=[
            pltpu.VMEM((len(panel) * block, block), jnp.bfloat16),
            pltpu.VMEM((8, block), jnp.float32),
        ],
        compiler_params=pltpu.CompilerParams(vmem_limit_bytes=VMEM_BYTES),
        name="first",
    )(*in_vmem(own, square, *panel))


def apply_next(step, panel, inner, squares, held):
    cols, block = panel[0].shape
    blocks = len(panel)
    last = step == 3
    if last:
        out_shape = jax.ShapeDtypeStruct((block, cols), jnp.float32)
        value = []
    else:
        out_shape = [
            pltpu.VMEM((cols, block), jnp.float32),
            pltpu.VMEM((blocks * block, block), jnp.bfloat16),
        ]
        value = [pltpu.VMEM((block, cols), jnp.bfloat16)]
    mine, other = zip(*inner)
    operands = in_vmem(*squares, *panel, *mine, *other, *held)
    return pl.pallas_call(
        functools.partial(next_kernel, step, blocks, len(inner)),
        in_specs=[VMEM] * len(operands),
        out_specs=VMEM if last else [VMEM, VMEM],
        out_shape=out_shape,
        scratch_shapes=[pltpu.VMEM((blocks * block, block), jnp.bfloat16)] + value,
        compiler_params=pltpu.CompilerParams(vmem_limit_bytes=VMEM_BYTES),
        name="apply%d" % step,
    )(*operands)


def swap_cores(value):
    return lax.ppermute(value, "col", [(0, 1), (1, 0)])


def both_cores(value):
    if lax.axis_size("col") == 2:
        return value, swap_cores(value)
    total = lax.psum(value.astype(jnp.float32), "col").astype(value.dtype)
    return total, jnp.zeros_like(total)


def gather_rounds(outer_size):
    held = {(0, 0)}
    last = outer_size - 1
    rounds = []
    for k in range(1, outer_size):
        rounds.append([((k, 0), (k - 1, 0)), ((k - 1, 1), (k - 1, 0)), ((k - 1, 2), (k - 1, 0))])
    held.update(key for moves in rounds for key, _ in moves)
    rest = [(last, 1), (last, 2)] + [(k, 3) for k in range(outer_size)]
    while rest:
        moves, taken = [], set()
        for key in rest:
            ways = [("y", (key[0], key[1] ^ 2)), ("x", (key[0], key[1] ^ 1)), ("z", (key[0] - 1, key[1]))]
            if key == (last, 1):
                ways.reverse()
            if key[1] == 3:
                ways = ways[::-1] if (key[0] - 1, 3) in held else ways
            for link, source in ways:
                if source in held and link not in taken:
                    taken.add(link)
                    moves.append((key, source))
                    break
        held.update(key for key, _ in moves)
        rest = [key for key in rest if key not in held]
        rounds.append(moves)
    return rounds


def shards(embeddings, rotation, codes, codebooks):
    tok_rows, model_width = embeddings.shape
    dp, col = lax.axis_size("dp"), lax.axis_size("col")
    rows_total = tok_rows * dp
    block = model_width // dp
    inner_size = math.gcd(dp, INNER)
    outer_size = dp // inner_size
    wide = model_width // outer_size
    part_rows = tok_rows // col
    outer, inner = lax.axis_index("dp") // inner_size, lax.axis_index("dp") % inner_size
    core = lax.axis_index("col")

    def from_outer(value, step):
        pairs = [(i, (i // inner_size ^ step) * inner_size + i % inner_size) for i in range(dp)]
        return lax.ppermute(value, "dp", pairs)

    def from_inner(value, step):
        pairs = [(i, i // inner_size * inner_size + (i % inner_size ^ step)) for i in range(dp)]
        return lax.ppermute(value, "dp", pairs)

    steps = list(range(1, outer_size))
    sends = [
        lax.dynamic_slice(embeddings, (core * part_rows, (outer ^ step) * wide), (part_rows, wide))
        for step in steps
    ]
    codes_t = codes.T.astype(jnp.bfloat16)
    group_codes = [codes_t] + [from_outer(codes_t, step) for step in steps]

    table = jnp.transpose(codebooks, (0, 2, 1)).astype(jnp.float32)
    own = rebuild_rows(codes_t[None], table)
    sends[1:], own = lax.optimization_barrier((sends[1:], own))
    rotated = lax.dot_general(
        rotation, embeddings, (((0,), (1,)), ((), ())), preferred_element_type=jnp.float32
    )
    residue = rotated - own.astype(jnp.float32)
    row_error = lax.psum(jnp.sum(residue * residue, axis=0), "col")
    weights = 1.0 / (1.0 + row_error / (2.0 * model_width))
    sends[0], weights, group_codes = lax.optimization_barrier((sends[0], weights, group_codes))
    shares = [from_outer(send, step) for send, step in zip(sends, steps)]
    group_weights = [weights] + [from_outer(weights, step) for step in steps]
    rebuilt = rebuild_rows(jnp.stack(group_codes), table)

    shares, rebuilt, group_weights = lax.optimization_barrier((shares, rebuilt, group_weights))
    columns = [lax.dynamic_slice_in_dim(embeddings, outer * wide, wide, 1)]
    for share in shares:
        if col == 2:
            other = swap_cores(share)
            pair = [jnp.where(core == 0, share, other), jnp.where(core == 0, other, share)]
            columns.append(jnp.concatenate(pair, axis=0))
        else:
            columns.append(lax.all_gather(share, "col", axis=0, tiled=True))
    scaled = jnp.concatenate(
        [
            (weight[:, None] * part.astype(jnp.float32)).astype(jnp.bfloat16)
            for weight, part in zip(group_weights, columns)
        ],
        axis=0,
    )


    def group_block(step):
        part = lax.dynamic_slice_in_dim(scaled, (inner ^ step) * block, block, 1)
        return jnp.dot(rebuilt, part, preferred_element_type=jnp.float32)

    parts = [
        from_inner(group_block(step).astype(jnp.bfloat16), step)
        for step in reversed(range(1, inner_size))
    ]
    start_row = lax.axis_index("dp") * block
    prior = lax.dynamic_slice_in_dim(rotation, start_row, block, 0).T
    start = lax.optimization_barrier(group_block(0)) + 0.2 * rows_total * prior.astype(jnp.float32)
    for part in parts:
        start = start + part.astype(jnp.float32)
    narrow = start.astype(jnp.bfloat16)

    def ring(value):
        pairs = [(i, (i + inner_size) % dp) for i in range(dp)]
        return lax.ppermute(value, "dp", pairs)

    def move(key, source):
        if key[0] != source[0]:
            return ring(held[source])
        return from_inner(held[source], key[1] ^ source[1])

    own = narrow.T
    held = {(0, 0): narrow}
    order, products = [(0, 0)], []
    square = jnp.zeros((8, block), jnp.float32)
    fresh = [narrow]
    for moves in gather_rounds(outer_size):
        arrived = [move(key, source) for key, source in moves]
        product, square = apply_first(own, square, fresh)
        arrived, product, square = lax.optimization_barrier((arrived, product, square))
        held.update({key: value for (key, _), value in zip(moves, arrived)})
        order += [key for key, _ in moves]
        products.append(both_cores(product))
        fresh = arrived
    product, square = apply_first(own, square, fresh)
    products.append(both_cores(product))
    panel = [held[key] for key in order]
    squares = both_cores(square)
    first, product = apply_next(0, panel, products, squares, [start])
    state, product = apply_next(1, panel, [both_cores(product)], squares, [first])
    state, product = apply_next(2, panel, [both_cores(product)], squares, [state])
    return apply_next(3, panel, [both_cores(product)], squares, [state, first])


def solution(mesh):
    placed = (P("dp", None), P(None, "col"), P("dp", "col"), P("col", None, None))
    return jax.shard_map(
        shards, mesh=mesh, in_specs=placed, out_specs=P("dp", "col"), check_vma=False
    )
```

```python
import functools
import math

import jax
import jax.numpy as jnp
from jax import lax
from jax.experimental import pallas as pl
from jax.experimental.pallas import tpu as pltpu
from jax.sharding import PartitionSpec as P

LANES = 128
GROUP = 8
CHUNKS = 4
INNER = 4
VMEM_BYTES = 24 * 1024 * 1024
ANY = pl.BlockSpec(memory_space=pl.ANY)
VMEM = pl.BlockSpec(memory_space=pltpu.VMEM)


def lookup_kernel(codes_ref, table_ref, out_ref, ids_ref):
    subs, rows = codes_ref.shape[1:]
    width = table_ref.shape[1]
    halves = table_ref.shape[2] // LANES
    first_out = pl.program_id(0) * (subs * width)
    ids_ref[...] = codes_ref[0].astype(jnp.float32).astype(jnp.int32)

    def body(step, carry):
        base = pl.multiple_of(step * GROUP, GROUP)
        for first in range(0, rows, LANES):
            lanes = pl.ds(pl.multiple_of(pl.program_id(1) * rows + first, LANES), LANES)
            ids_all = ids_ref[pl.ds(base, GROUP), first : first + LANES]
            for pair in range(0, GROUP, 2):
                both = []
                for sub in (pair, pair + 1):
                    ids = jnp.broadcast_to(ids_all[sub : sub + 1], (width, LANES))
                    lane = jnp.bitwise_and(ids, LANES - 1)
                    picked = None
                    for half in range(halves):
                        entries = table_ref[base + sub, :, half * LANES : (half + 1) * LANES]
                        got = jnp.take_along_axis(
                            entries, lane, axis=1, mode="promise_in_bounds"
                        )
                        picked = got if half == 0 else jnp.where(ids >= half * LANES, got, picked)
                    both.append(picked)
                row = pl.multiple_of(first_out + (base + pair) * width, 2 * width)
                out_ref[pl.ds(row, 2 * width), lanes] = jnp.concatenate(both, axis=0).astype(
                    out_ref.dtype
                )
        return carry

    lax.fori_loop(0, subs // GROUP, body, 0)


def rebuild_rows(codes, table):
    blocks, subs, rows = codes.shape
    width, centroids = table.shape[1:]
    tile = min(64, subs)
    return pl.pallas_call(
        lookup_kernel,
        grid=(subs // tile, blocks),
        in_specs=[
            pl.BlockSpec((1, tile, rows), lambda m, s: (s, m, 0)),
            pl.BlockSpec((tile, width, centroids), lambda m, s: (m, 0, 0)),
        ],
        out_specs=VMEM,
        scratch_shapes=[pltpu.VMEM((tile, rows), jnp.int32)],
        out_shape=pltpu.VMEM((subs * width, blocks * rows), jnp.bfloat16),
        compiler_params=pltpu.CompilerParams(vmem_limit_bytes=VMEM_BYTES),
        name="lookup",
    )(codes, table)


def cross_kernel(targets, place_ref, rebuilt_ref, prior_ref, local_ref, *refs):
    pieces, outs = refs[: len(refs) - len(targets)], refs[len(refs) - len(targets) :]
    rows = local_ref.shape[0]
    block = outs[0].shape[1]
    part_rows, col = (pieces[0].shape[0], rows // pieces[0].shape[0]) if pieces else (rows, 1)
    for target, out_ref in zip(targets, outs):
        place = lax.bitwise_xor(place_ref[1], target)
        lanes = pl.ds(pl.multiple_of(place * block, block), block)
        total = jnp.dot(
            rebuilt_ref[:, :rows], local_ref[:, lanes], preferred_element_type=jnp.float32
        )
        for index, piece_ref in enumerate(pieces):
            step, turn = divmod(index, col)
            first = (step + 1) * rows + lax.rem(place_ref[0] + turn, col) * part_rows
            total += jnp.dot(
                rebuilt_ref[:, pl.ds(pl.multiple_of(first, part_rows), part_rows)],
                piece_ref[:, lanes],
                preferred_element_type=jnp.float32,
            )
        if target == 0:
            total += prior_ref[...]
        out_ref[...] = total.astype(out_ref.dtype)


def cross_blocks(targets, dtype, place, rebuilt, prior, local, pieces):
    operands = in_vmem(rebuilt, prior, local, *pieces)
    return pl.pallas_call(
        functools.partial(cross_kernel, targets),
        in_specs=[pl.BlockSpec(memory_space=pltpu.SMEM)] + [VMEM] * len(operands),
        out_specs=[VMEM] * len(targets),
        out_shape=[pltpu.VMEM(prior.shape, dtype) for _ in targets],
        compiler_params=pltpu.CompilerParams(vmem_limit_bytes=VMEM_BYTES),
        name="cross",
    )(place, *operands)


def product_of(value_ref, block_ref, inner_ref, index):
    block = block_ref.shape[1]
    product = jnp.dot(value_ref[...], block_ref[...], preferred_element_type=jnp.float32)
    inner_ref[index * block : (index + 1) * block, :] = product.T.astype(inner_ref.dtype)


def first_kernel(own_ref, before_ref, *refs):
    panel, (inner_ref, square_ref) = refs[:-2], refs[-2:]
    cols, block = panel[0].shape
    square = before_ref[...]
    for index, block_ref in enumerate(panel):
        product_of(own_ref, block_ref, inner_ref, index)
        values = block_ref[...].astype(jnp.float32)
        square += jnp.sum((values * values).reshape(cols // 8, 8, block), axis=0)
    square_ref[...] = square


def next_kernel(step, blocks, parts, mine_square_ref, other_square_ref, *refs):
    last = step == 3
    states = 2 if last else 1
    panel, refs = refs[:blocks], refs[blocks:]
    mine, other, refs = refs[:parts], refs[parts : 2 * parts], refs[2 * parts :]
    held, refs = refs[:states], refs[states:]
    if last:
        out_ref, sum_ref = refs
    else:
        state_ref, inner_ref, sum_ref, value_ref = refs
    cols, block = panel[0].shape
    model_width = blocks * block
    chunk = cols // CHUNKS
    total = jnp.sum(mine_square_ref[...] + other_square_ref[...], axis=(0, 1), keepdims=True)
    scale = model_width / (1.96 * total)
    first = 0
    for mine_ref, other_ref in zip(mine, other):
        sum_ref[first : first + mine_ref.shape[0], :] = mine_ref[...] + other_ref[...]
        first += mine_ref.shape[0]

    for index in range(CHUNKS):
        span = slice(index * chunk, (index + 1) * chunk)
        made = jnp.zeros((chunk, block), jnp.float32)
        for owner in range(blocks):
            made += jnp.dot(
                panel[owner][span, :],
                sum_ref[owner * block : (owner + 1) * block, :],
                preferred_element_type=jnp.float32,
            )
        if step == 2:
            made = made * scale
        else:
            made = 1.5 * held[0][span, :] - (0.5 * scale) * made
        if last:
            made = (1.5 * held[1][span, :] - 0.5 * made) * (math.sqrt(model_width) * jnp.sqrt(scale))
            out_ref[:, span] = made.T
        else:
            state_ref[span, :] = made
            value_ref[:, span] = made.T.astype(value_ref.dtype)
    if last:
        return
    for index in range(blocks):
        product_of(value_ref, panel[index], inner_ref, index)


def in_vmem(*values):
    return [pltpu.with_memory_space_constraint(value, pltpu.VMEM) for value in values]


def apply_first(own, square, panel):
    block = panel[0].shape[1]
    return pl.pallas_call(
        first_kernel,
        in_specs=[VMEM] * (2 + len(panel)),
        out_specs=[VMEM, VMEM],
        out_shape=[
            pltpu.VMEM((len(panel) * block, block), jnp.bfloat16),
            pltpu.VMEM((8, block), jnp.float32),
        ],
        compiler_params=pltpu.CompilerParams(vmem_limit_bytes=VMEM_BYTES),
        name="first",
    )(*in_vmem(own, square, *panel))


def apply_next(step, panel, inner, squares, held):
    cols, block = panel[0].shape
    blocks = len(panel)
    last = step == 3
    if last:
        out_shape = jax.ShapeDtypeStruct((block, cols), jnp.float32)
        value = []
    else:
        out_shape = [
            pltpu.VMEM((cols, block), jnp.float32),
            pltpu.VMEM((blocks * block, block), jnp.bfloat16),
        ]
        value = [pltpu.VMEM((block, cols), jnp.bfloat16)]
    mine, other = zip(*inner)
    operands = in_vmem(*squares, *panel, *mine, *other, *held)
    return pl.pallas_call(
        functools.partial(next_kernel, step, blocks, len(inner)),
        in_specs=[VMEM] * len(operands),
        out_specs=VMEM if last else [VMEM, VMEM],
        out_shape=out_shape,
        scratch_shapes=[pltpu.VMEM((blocks * block, block), jnp.bfloat16)] + value,
        compiler_params=pltpu.CompilerParams(vmem_limit_bytes=VMEM_BYTES),
        name="apply%d" % step,
    )(*operands)


def swap_cores(value):
    return lax.ppermute(value, "col", [(0, 1), (1, 0)])


def both_cores(value):
    if lax.axis_size("col") == 2:
        return value, swap_cores(value)
    total = lax.psum(value.astype(jnp.float32), "col").astype(value.dtype)
    return total, jnp.zeros_like(total)


def gather_rounds(outer_size):
    held = {(0, 0)}
    last = outer_size - 1
    rounds = []
    for k in range(1, outer_size):
        rounds.append([((k, 0), (k - 1, 0)), ((k - 1, 1), (k - 1, 0)), ((k - 1, 2), (k - 1, 0))])
    held.update(key for moves in rounds for key, _ in moves)
    rest = [(last, 1), (last, 2)] + [(k, 3) for k in range(outer_size)]
    while rest:
        moves, taken = [], set()
        for key in rest:
            ways = [("y", (key[0], key[1] ^ 2)), ("x", (key[0], key[1] ^ 1)), ("z", (key[0] - 1, key[1]))]
            if key == (last, 1):
                ways.reverse()
            if key[1] == 3:
                ways = ways[::-1] if (key[0] - 1, 3) in held else ways
            for link, source in ways:
                if source in held and link not in taken:
                    taken.add(link)
                    moves.append((key, source))
                    break
        held.update(key for key, _ in moves)
        rest = [key for key in rest if key not in held]
        rounds.append(moves)
    return rounds


def shards(embeddings, rotation, codes, codebooks):
    tok_rows, model_width = embeddings.shape
    dp, col = lax.axis_size("dp"), lax.axis_size("col")
    rows_total = tok_rows * dp
    block = model_width // dp
    inner_size = math.gcd(dp, INNER)
    outer_size = dp // inner_size
    wide = model_width // outer_size
    part_rows = tok_rows // col
    outer, inner = lax.axis_index("dp") // inner_size, lax.axis_index("dp") % inner_size
    core = lax.axis_index("col")

    def from_outer(value, step):
        pairs = [(i, (i // inner_size ^ step) * inner_size + i % inner_size) for i in range(dp)]
        return lax.ppermute(value, "dp", pairs)

    def from_inner(value, step):
        pairs = [(i, i // inner_size * inner_size + (i % inner_size ^ step)) for i in range(dp)]
        return lax.ppermute(value, "dp", pairs)

    steps = list(range(1, outer_size))
    codes_t = codes.T.astype(jnp.bfloat16)
    group_codes = [codes_t] + [from_outer(codes_t, step) for step in steps]

    table = jnp.transpose(codebooks, (0, 2, 1)).astype(jnp.float32)
    own = rebuild_rows(codes_t[None], table)
    rotated = lax.dot_general(
        rotation, embeddings, (((0,), (1,)), ((), ())), preferred_element_type=jnp.float32
    )
    residue = rotated - own.astype(jnp.float32)
    row_error = lax.psum(jnp.sum(residue * residue, axis=0), "col")
    weights = 1.0 / (1.0 + row_error / (2.0 * model_width))
    scaled = (weights[:, None] * embeddings.astype(jnp.float32)).astype(jnp.bfloat16)

    sends = [
        lax.dynamic_slice(scaled, (core * part_rows, (outer ^ step) * wide), (part_rows, wide))
        for step in steps
    ]
    shares = [from_outer(send, step) for send, step in zip(sends, steps)]
    local = lax.dynamic_slice_in_dim(scaled, outer * wide, wide, 1)
    rebuilt = rebuild_rows(jnp.stack(group_codes), table)
    shares, rebuilt = lax.optimization_barrier((shares, rebuilt))
    pieces = []
    for share in shares:
        if part_rows % LANES:
            pieces.append(lax.all_gather(share, "col", axis=0, tiled=True))
            continue
        pieces.append(share)
        for turn in range(1, col):
            pairs = [(i, (i - turn) % col) for i in range(col)]
            pieces.append(lax.ppermute(share, "col", pairs))

    place = jnp.stack([core, inner]).astype(jnp.int32)
    start_row = lax.axis_index("dp") * block
    prior = lax.dynamic_slice_in_dim(rotation, start_row, block, 0).T
    prior = 0.2 * rows_total * prior.astype(jnp.float32)
    targets = list(reversed(range(1, inner_size)))
    parts = cross_blocks(targets, jnp.bfloat16, place, rebuilt, prior, local, pieces)
    parts = [from_inner(part, target) for part, target in zip(parts, targets)]
    (start,) = cross_blocks([0], jnp.float32, place, rebuilt, prior, local, pieces)
    for part in parts:
        start = start + part.astype(jnp.float32)
    narrow = start.astype(jnp.bfloat16)

    def ring(value):
        pairs = [(i, (i + inner_size) % dp) for i in range(dp)]
        return lax.ppermute(value, "dp", pairs)

    def move(key, source):
        if key[0] != source[0]:
            return ring(held[source])
        return from_inner(held[source], key[1] ^ source[1])

    own = narrow.T
    held = {(0, 0): narrow}
    order, products = [(0, 0)], []
    square = jnp.zeros((8, block), jnp.float32)
    fresh = [narrow]
    for moves in gather_rounds(outer_size):
        arrived = [move(key, source) for key, source in moves]
        product, square = apply_first(own, square, fresh)
        arrived, product, square = lax.optimization_barrier((arrived, product, square))
        held.update({key: value for (key, _), value in zip(moves, arrived)})
        order += [key for key, _ in moves]
        products.append(both_cores(product))
        fresh = arrived
    product, square = apply_first(own, square, fresh)
    products.append(both_cores(product))
    panel = [held[key] for key in order]
    squares = both_cores(square)
    first, product = apply_next(0, panel, products, squares, [start])
    state, product = apply_next(1, panel, [both_cores(product)], squares, [first])
    state, product = apply_next(2, panel, [both_cores(product)], squares, [state])
    return apply_next(3, panel, [both_cores(product)], squares, [state, first])


def solution(mesh):
    placed = (P("dp", None), P(None, "col"), P("dp", "col"), P("col", None, None))
    return jax.shard_map(
        shards, mesh=mesh, in_specs=placed, out_specs=P("dp", "col"), check_vma=False
    )
```

```python
import functools
import math

import jax
import jax.numpy as jnp
from jax import lax
from jax.experimental import pallas as pl
from jax.experimental.pallas import tpu as pltpu
from jax.sharding import PartitionSpec as P

LANES = 128
GROUP = 8
CHUNKS = 4
INNER = 4
VMEM_BYTES = 24 * 1024 * 1024
ANY = pl.BlockSpec(memory_space=pl.ANY)
VMEM = pl.BlockSpec(memory_space=pltpu.VMEM)


def lookup_kernel(codes_ref, table_ref, out_ref, ids_ref):
    subs, rows = codes_ref.shape[1:]
    width = table_ref.shape[1]
    halves = table_ref.shape[2] // LANES
    first_out = pl.program_id(0) * (subs * width)
    ids_ref[...] = codes_ref[0].astype(jnp.float32).astype(jnp.int32)

    def body(step, carry):
        base = pl.multiple_of(step * GROUP, GROUP)
        for first in range(0, rows, LANES):
            lanes = pl.ds(pl.multiple_of(pl.program_id(1) * rows + first, LANES), LANES)
            ids_all = ids_ref[pl.ds(base, GROUP), first : first + LANES]
            for pair in range(0, GROUP, 2):
                both = []
                for sub in (pair, pair + 1):
                    ids = jnp.broadcast_to(ids_all[sub : sub + 1], (width, LANES))
                    lane = jnp.bitwise_and(ids, LANES - 1)
                    picked = None
                    for half in range(halves):
                        entries = table_ref[base + sub, :, half * LANES : (half + 1) * LANES]
                        got = jnp.take_along_axis(
                            entries, lane, axis=1, mode="promise_in_bounds"
                        )
                        picked = got if half == 0 else jnp.where(ids >= half * LANES, got, picked)
                    both.append(picked)
                row = pl.multiple_of(first_out + (base + pair) * width, 2 * width)
                out_ref[pl.ds(row, 2 * width), lanes] = jnp.concatenate(both, axis=0).astype(
                    out_ref.dtype
                )
        return carry

    lax.fori_loop(0, subs // GROUP, body, 0)


def rebuild_rows(codes, table):
    blocks, subs, rows = codes.shape
    width, centroids = table.shape[1:]
    tile = min(64, subs)
    return pl.pallas_call(
        lookup_kernel,
        grid=(subs // tile, blocks),
        in_specs=[
            pl.BlockSpec((1, tile, rows), lambda m, s: (s, m, 0)),
            pl.BlockSpec((tile, width, centroids), lambda m, s: (m, 0, 0)),
        ],
        out_specs=VMEM,
        scratch_shapes=[pltpu.VMEM((tile, rows), jnp.int32)],
        out_shape=pltpu.VMEM((subs * width, blocks * rows), jnp.bfloat16),
        compiler_params=pltpu.CompilerParams(vmem_limit_bytes=VMEM_BYTES),
        name="lookup",
    )(codes, table)


def cross_kernel(plan, place_ref, rebuilt_ref, prior_ref, local_ref, *refs):
    pieces, outs = refs[: len(refs) - len(plan)], refs[len(refs) - len(plan) :]
    rows = local_ref.shape[0]
    part_rows, col = (pieces[0].shape[0], rows // pieces[0].shape[0]) if pieces else (rows, 1)
    for (targets, first_row), out_ref in zip(plan, outs):
        height, block = out_ref.shape[0] // len(targets), out_ref.shape[1]
        span = slice(first_row, first_row + height)
        for slot, target in enumerate(targets):
            place = lax.bitwise_xor(place_ref[1], target)
            lanes = pl.ds(pl.multiple_of(place * block, block), block)
            total = jnp.dot(
                rebuilt_ref[span, :rows], local_ref[:, lanes], preferred_element_type=jnp.float32
            )
            for index, piece_ref in enumerate(pieces):
                step, turn = divmod(index, col)
                first = (step + 1) * rows + lax.rem(place_ref[0] + turn, col) * part_rows
                total += jnp.dot(
                    rebuilt_ref[span, pl.ds(pl.multiple_of(first, part_rows), part_rows)],
                    piece_ref[:, lanes],
                    preferred_element_type=jnp.float32,
                )
            if target == 0:
                total += prior_ref[span, :]
            out_ref[slot * height : (slot + 1) * height, :] = total.astype(out_ref.dtype)


def cross_blocks(plan, dtype, place, rebuilt, prior, local, pieces):
    operands = in_vmem(rebuilt, prior, local, *pieces)
    half, block = prior.shape[0] // 2, prior.shape[1]
    return pl.pallas_call(
        functools.partial(cross_kernel, plan),
        in_specs=[pl.BlockSpec(memory_space=pltpu.SMEM)] + [VMEM] * len(operands),
        out_specs=[VMEM] * len(plan),
        out_shape=[pltpu.VMEM((len(targets) * half, block), dtype) for targets, _ in plan],
        compiler_params=pltpu.CompilerParams(vmem_limit_bytes=VMEM_BYTES),
        name="cross",
    )(place, *operands)


def product_of(value_ref, halves, inner_ref, index):
    half, block = halves[0].shape
    product = jnp.zeros((value_ref.shape[0], block), jnp.float32)
    for first, half_ref in enumerate(halves):
        product += jnp.dot(
            value_ref[:, first * half : (first + 1) * half], half_ref[...],
            preferred_element_type=jnp.float32,
        )
    inner_ref[index * block : (index + 1) * block, :] = product.T.astype(inner_ref.dtype)


def first_kernel(own_ref, before_ref, *refs):
    panel, (inner_ref, square_ref) = refs[:-2], refs[-2:]
    half, block = panel[0].shape
    square = before_ref[...]
    for index in range(len(panel) // 2):
        halves = panel[2 * index : 2 * index + 2]
        product_of(own_ref, halves, inner_ref, index)
        for half_ref in halves:
            values = half_ref[...].astype(jnp.float32)
            square += jnp.sum((values * values).reshape(half // 8, 8, block), axis=0)
    square_ref[...] = square


def next_kernel(step, blocks, parts, mine_square_ref, other_square_ref, *refs):
    last = step == 3
    states = 2 if last else 1
    panel, refs = refs[: 2 * blocks], refs[2 * blocks :]
    mine, other, refs = refs[:parts], refs[parts : 2 * parts], refs[2 * parts :]
    held, refs = refs[:states], refs[states:]
    if last:
        out_ref, sum_ref = refs
    else:
        state_ref, inner_ref, sum_ref, value_ref = refs
    half, block = panel[0].shape
    model_width = blocks * block
    chunk = 2 * half // CHUNKS
    total = jnp.sum(mine_square_ref[...] + other_square_ref[...], axis=(0, 1), keepdims=True)
    scale = model_width / (1.96 * total)
    first = 0
    for mine_ref, other_ref in zip(mine, other):
        sum_ref[first : first + mine_ref.shape[0], :] = mine_ref[...] + other_ref[...]
        first += mine_ref.shape[0]

    for index in range(CHUNKS):
        span = slice(index * chunk, (index + 1) * chunk)
        side, first = divmod(index * chunk, half)
        made = jnp.zeros((chunk, block), jnp.float32)
        for owner in range(blocks):
            made += jnp.dot(
                panel[2 * owner + side][first : first + chunk, :],
                sum_ref[owner * block : (owner + 1) * block, :],
                preferred_element_type=jnp.float32,
            )
        if step == 2:
            made = made * scale
        else:
            made = 1.5 * held[0][span, :] - (0.5 * scale) * made
        if last:
            made = (1.5 * held[1][span, :] - 0.5 * made) * (math.sqrt(model_width) * jnp.sqrt(scale))
            out_ref[:, span] = made.T
        else:
            state_ref[span, :] = made
            value_ref[:, span] = made.T.astype(value_ref.dtype)
    if last:
        return
    for index in range(blocks):
        product_of(value_ref, panel[2 * index : 2 * index + 2], inner_ref, index)


def in_vmem(*values):
    return [pltpu.with_memory_space_constraint(value, pltpu.VMEM) for value in values]


def apply_first(own, square, panel):
    block = panel[0].shape[1]
    return pl.pallas_call(
        first_kernel,
        in_specs=[VMEM] * (2 + len(panel)),
        out_specs=[VMEM, VMEM],
        out_shape=[
            pltpu.VMEM((len(panel) // 2 * block, block), jnp.bfloat16),
            pltpu.VMEM((8, block), jnp.float32),
        ],
        compiler_params=pltpu.CompilerParams(vmem_limit_bytes=VMEM_BYTES),
        name="first",
    )(*in_vmem(own, square, *panel))


def apply_next(step, panel, inner, squares, held):
    half, block = panel[0].shape
    blocks, cols = len(panel) // 2, 2 * half
    last = step == 3
    if last:
        out_shape = jax.ShapeDtypeStruct((block, cols), jnp.float32)
        value = []
    else:
        out_shape = [
            pltpu.VMEM((cols, block), jnp.float32),
            pltpu.VMEM((blocks * block, block), jnp.bfloat16),
        ]
        value = [pltpu.VMEM((block, cols), jnp.bfloat16)]
    mine, other = zip(*inner)
    operands = in_vmem(*squares, *panel, *mine, *other, *held)
    return pl.pallas_call(
        functools.partial(next_kernel, step, blocks, len(inner)),
        in_specs=[VMEM] * len(operands),
        out_specs=VMEM if last else [VMEM, VMEM],
        out_shape=out_shape,
        scratch_shapes=[pltpu.VMEM((blocks * block, block), jnp.bfloat16)] + value,
        compiler_params=pltpu.CompilerParams(vmem_limit_bytes=VMEM_BYTES),
        name="apply%d" % step,
    )(*operands)


def swap_cores(value):
    return lax.ppermute(value, "col", [(0, 1), (1, 0)])


def both_cores(value):
    if lax.axis_size("col") == 2:
        return value, swap_cores(value)
    total = lax.psum(value.astype(jnp.float32), "col").astype(value.dtype)
    return total, jnp.zeros_like(total)


def gather_rounds(outer_size):
    held = {(0, 0)}
    last = outer_size - 1
    rounds = []
    for k in range(1, outer_size):
        rounds.append([((k, 0), (k - 1, 0)), ((k - 1, 1), (k - 1, 0)), ((k - 1, 2), (k - 1, 0))])
    held.update(key for moves in rounds for key, _ in moves)
    rest = [(last, 1), (last, 2)] + [(k, 3) for k in range(outer_size)]
    while rest:
        moves, taken = [], set()
        for key in rest:
            ways = [("y", (key[0], key[1] ^ 2)), ("x", (key[0], key[1] ^ 1)), ("z", (key[0] - 1, key[1]))]
            if key == (last, 1):
                ways.reverse()
            if key[1] == 3:
                ways = ways[::-1] if (key[0] - 1, 3) in held else ways
            for link, source in ways:
                if source in held and link not in taken:
                    taken.add(link)
                    moves.append((key, source))
                    break
        held.update(key for key, _ in moves)
        rest = [key for key in rest if key not in held]
        rounds.append(moves)
    return rounds


def shards(embeddings, rotation, codes, codebooks):
    tok_rows, model_width = embeddings.shape
    dp, col = lax.axis_size("dp"), lax.axis_size("col")
    rows_total = tok_rows * dp
    block = model_width // dp
    inner_size = math.gcd(dp, INNER)
    outer_size = dp // inner_size
    wide = model_width // outer_size
    part_rows = tok_rows // col
    outer, inner = lax.axis_index("dp") // inner_size, lax.axis_index("dp") % inner_size
    core = lax.axis_index("col")

    def from_outer(value, step):
        pairs = [(i, (i // inner_size ^ step) * inner_size + i % inner_size) for i in range(dp)]
        return lax.ppermute(value, "dp", pairs)

    def from_inner(value, step):
        pairs = [(i, i // inner_size * inner_size + (i % inner_size ^ step)) for i in range(dp)]
        return lax.ppermute(value, "dp", pairs)

    steps = list(range(1, outer_size))
    codes_t = codes.T.astype(jnp.bfloat16)
    group_codes = [codes_t] + [from_outer(codes_t, step) for step in steps]

    table = jnp.transpose(codebooks, (0, 2, 1)).astype(jnp.float32)
    own = rebuild_rows(codes_t[None], table)
    rotated = lax.dot_general(
        rotation, embeddings, (((0,), (1,)), ((), ())), preferred_element_type=jnp.float32
    )
    residue = rotated - own.astype(jnp.float32)
    row_error = lax.psum(jnp.sum(residue * residue, axis=0), "col")
    weights = 1.0 / (1.0 + row_error / (2.0 * model_width))
    scaled = (weights[:, None] * embeddings.astype(jnp.float32)).astype(jnp.bfloat16)

    sends = [
        lax.dynamic_slice(scaled, (core * part_rows, (outer ^ step) * wide), (part_rows, wide))
        for step in steps
    ]
    shares = [from_outer(send, step) for send, step in zip(sends, steps)]
    local = lax.dynamic_slice_in_dim(scaled, outer * wide, wide, 1)
    rebuilt = rebuild_rows(jnp.stack(group_codes), table)
    shares, rebuilt = lax.optimization_barrier((shares, rebuilt))
    pieces = []
    for share in shares:
        if part_rows % LANES:
            pieces.append(lax.all_gather(share, "col", axis=0, tiled=True))
            continue
        pieces.append(share)
        for turn in range(1, col):
            pairs = [(i, (i - turn) % col) for i in range(col)]
            pieces.append(lax.ppermute(share, "col", pairs))

    place = jnp.stack([core, inner]).astype(jnp.int32)
    start_row = lax.axis_index("dp") * block
    prior = lax.dynamic_slice_in_dim(rotation, start_row, block, 0).T
    prior = 0.2 * rows_total * prior.astype(jnp.float32)
    half = prior.shape[0] // 2
    blocks_for = functools.partial(
        cross_blocks, place=place, rebuilt=rebuilt, prior=prior, local=local, pieces=pieces
    )
    near = [(1, 2), (2, 1)]
    sent = blocks_for([((one, 3), side * half) for side, (one, _) in enumerate(near)], jnp.bfloat16)
    came = [from_inner(value, one) for value, (one, _) in zip(sent, near)]
    kept = blocks_for(
        [((0,), side * half) for side in range(2)]
        + [((two,), side * half) for side, (_, two) in enumerate(near)],
        jnp.float32,
    )
    starts = []
    for side, (_, two) in enumerate(near):
        passed = kept[2 + side] + came[side][half:].astype(jnp.float32)
        last = from_inner(passed.astype(jnp.bfloat16), two)
        starts.append(kept[side] + came[side][:half].astype(jnp.float32) + last.astype(jnp.float32))
    narrow = [value.astype(jnp.bfloat16) for value in starts]
    start = jnp.concatenate(starts, axis=0)

    def ring(value):
        pairs = [(i, (i + inner_size) % dp) for i in range(dp)]
        return lax.ppermute(value, "dp", pairs)

    own = jnp.concatenate(narrow, axis=0).T
    held = [{(0, 0): value} for value in narrow]

    def move(side, key, source):
        value = held[side][source]
        return ring(value) if key[0] != source[0] else from_inner(value, key[1] ^ source[1])

    def halves(keys):
        return [held[side][key] for key in keys for side in range(2)]

    order, products = [(0, 0)], []
    square = jnp.zeros((8, block), jnp.float32)
    fresh = [(0, 0)]
    for moves in gather_rounds(outer_size):
        arrived = [[move(side, key, source) for key, source in moves] for side in range(2)]
        product, square = apply_first(own, square, halves(fresh))
        arrived[0], product, square = lax.optimization_barrier((arrived[0], product, square))
        arrived[1] = lax.optimization_barrier(arrived[1])
        fresh = [key for key, _ in moves]
        for side in range(2):
            held[side].update(zip(fresh, arrived[side]))
        order += fresh
        products.append(both_cores(product))
    product, square = apply_first(own, square, halves(fresh))
    products.append(both_cores(product))
    panel = halves(order)
    squares = both_cores(square)
    first, product = apply_next(0, panel, products, squares, [start])
    state, product = apply_next(1, panel, [both_cores(product)], squares, [first])
    state, product = apply_next(2, panel, [both_cores(product)], squares, [state])
    return apply_next(3, panel, [both_cores(product)], squares, [state, first])


def solution(mesh):
    placed = (P("dp", None), P(None, "col"), P("dp", "col"), P("col", None, None))
    return jax.shard_map(
        shards, mesh=mesh, in_specs=placed, out_specs=P("dp", "col"), check_vma=False
    )
```

```python
import functools
import math

import jax
import jax.numpy as jnp
from jax import lax
from jax.experimental import pallas as pl
from jax.experimental.pallas import tpu as pltpu
from jax.sharding import PartitionSpec as P

LANES = 128
GROUP = 8
CHUNKS = 4
INNER = 4
VMEM_BYTES = 24 * 1024 * 1024
ANY = pl.BlockSpec(memory_space=pl.ANY)
VMEM = pl.BlockSpec(memory_space=pltpu.VMEM)


def lookup_kernel(codes_ref, table_ref, out_ref, ids_ref):
    subs, rows = codes_ref.shape[1:]
    width = table_ref.shape[1]
    halves = table_ref.shape[2] // LANES
    first_out = pl.program_id(0) * (subs * width)
    ids_ref[...] = codes_ref[0].astype(jnp.float32).astype(jnp.int32)

    def body(step, carry):
        base = pl.multiple_of(step * GROUP, GROUP)
        for first in range(0, rows, LANES):
            lanes = pl.ds(pl.multiple_of(pl.program_id(1) * rows + first, LANES), LANES)
            ids_all = ids_ref[pl.ds(base, GROUP), first : first + LANES]
            for pair in range(0, GROUP, 2):
                both = []
                for sub in (pair, pair + 1):
                    ids = jnp.broadcast_to(ids_all[sub : sub + 1], (width, LANES))
                    lane = jnp.bitwise_and(ids, LANES - 1)
                    picked = None
                    for half in range(halves):
                        entries = table_ref[base + sub, :, half * LANES : (half + 1) * LANES]
                        got = jnp.take_along_axis(
                            entries, lane, axis=1, mode="promise_in_bounds"
                        )
                        picked = got if half == 0 else jnp.where(ids >= half * LANES, got, picked)
                    both.append(picked)
                row = pl.multiple_of(first_out + (base + pair) * width, 2 * width)
                out_ref[pl.ds(row, 2 * width), lanes] = jnp.concatenate(both, axis=0).astype(
                    out_ref.dtype
                )
        return carry

    lax.fori_loop(0, subs // GROUP, body, 0)


def rebuild_rows(codes, table):
    blocks, subs, rows = codes.shape
    width, centroids = table.shape[1:]
    tile = min(64, subs)
    return pl.pallas_call(
        lookup_kernel,
        grid=(subs // tile, blocks),
        in_specs=[
            pl.BlockSpec((1, tile, rows), lambda m, s: (s, m, 0)),
            pl.BlockSpec((tile, width, centroids), lambda m, s: (m, 0, 0)),
        ],
        out_specs=VMEM,
        scratch_shapes=[pltpu.VMEM((tile, rows), jnp.int32)],
        out_shape=pltpu.VMEM((subs * width, blocks * rows), jnp.bfloat16),
        compiler_params=pltpu.CompilerParams(vmem_limit_bytes=VMEM_BYTES),
        name="lookup",
    )(codes, table)


def cross_kernel(plan, place_ref, rebuilt_ref, prior_ref, local_ref, *refs):
    pieces, outs = refs[: len(refs) - len(plan)], refs[len(refs) - len(plan) :]
    rows = local_ref.shape[0]
    part_rows, col = (pieces[0].shape[0], rows // pieces[0].shape[0]) if pieces else (rows, 1)
    for (targets, first_row), out_ref in zip(plan, outs):
        height, block = out_ref.shape[0] // len(targets), out_ref.shape[1]
        span = slice(first_row, first_row + height)
        for slot, target in enumerate(targets):
            place = lax.bitwise_xor(place_ref[1], target)
            lanes = pl.ds(pl.multiple_of(place * block, block), block)
            total = jnp.dot(
                rebuilt_ref[span, :rows], local_ref[:, lanes], preferred_element_type=jnp.float32
            )
            for index, piece_ref in enumerate(pieces):
                step, turn = divmod(index, col)
                first = (step + 1) * rows + lax.rem(place_ref[0] + turn, col) * part_rows
                total += jnp.dot(
                    rebuilt_ref[span, pl.ds(pl.multiple_of(first, part_rows), part_rows)],
                    piece_ref[:, lanes],
                    preferred_element_type=jnp.float32,
                )
            if target == 0:
                total += prior_ref[span, :]
            out_ref[slot * height : (slot + 1) * height, :] = total.astype(out_ref.dtype)


def cross_blocks(plan, dtype, place, rebuilt, prior, local, pieces):
    operands = in_vmem(rebuilt, prior, local, *pieces)
    half, block = prior.shape[0] // 2, prior.shape[1]
    return pl.pallas_call(
        functools.partial(cross_kernel, plan),
        in_specs=[pl.BlockSpec(memory_space=pltpu.SMEM)] + [VMEM] * len(operands),
        out_specs=[VMEM] * len(plan),
        out_shape=[pltpu.VMEM((len(targets) * half, block), dtype) for targets, _ in plan],
        compiler_params=pltpu.CompilerParams(vmem_limit_bytes=VMEM_BYTES),
        name="cross",
    )(place, *operands)


def product_of(value_ref, halves, inner_ref, index):
    half, block = halves[0].shape
    product = jnp.zeros((value_ref.shape[0], block), jnp.float32)
    for first, half_ref in enumerate(halves):
        product += jnp.dot(
            value_ref[:, first * half : (first + 1) * half], half_ref[...],
            preferred_element_type=jnp.float32,
        )
    inner_ref[index * block : (index + 1) * block, :] = product.T.astype(inner_ref.dtype)


def first_kernel(own_ref, before_ref, *refs):
    panel, (inner_ref, square_ref) = refs[:-2], refs[-2:]
    half, block = panel[0].shape
    square = before_ref[...]
    for index in range(len(panel) // 2):
        halves = panel[2 * index : 2 * index + 2]
        product_of(own_ref, halves, inner_ref, index)
        for half_ref in halves:
            values = half_ref[...].astype(jnp.float32)
            square += jnp.sum((values * values).reshape(half // 8, 8, block), axis=0)
    square_ref[...] = square


def add_up(mine, other, sum_ref):
    first = 0
    for mine_ref, other_ref in zip(mine, other):
        sum_ref[first : first + mine_ref.shape[0], :] = mine_ref[...] + other_ref[...]
        first += mine_ref.shape[0]


def gram_rows(panel, sum_ref, index):
    half, block = panel[0].shape
    chunk = 2 * half // CHUNKS
    side, first = divmod(index * chunk, half)
    made = jnp.zeros((chunk, block), jnp.float32)
    for owner in range(len(panel) // 2):
        made += jnp.dot(
            panel[2 * owner + side][first : first + chunk, :],
            sum_ref[owner * block : (owner + 1) * block, :],
            preferred_element_type=jnp.float32,
        )
    return slice(index * chunk, (index + 1) * chunk), made


def early_kernel(blocks, parts, *refs):
    panel, refs = refs[: 2 * blocks], refs[2 * blocks :]
    mine, other, (out_ref, sum_ref) = refs[:parts], refs[parts : 2 * parts], refs[2 * parts :]
    add_up(mine, other, sum_ref)
    for index in range(CHUNKS):
        span, made = gram_rows(panel, sum_ref, index)
        out_ref[span, :] = made


def late_kernel(step, blocks, parts, mine_square_ref, other_square_ref, *refs):
    last = step == 3
    states = 2 if last else 1
    first_late, late = blocks
    panel, refs = refs[: 2 * (first_late + late)], refs[2 * (first_late + late) :]
    mine, other, refs = refs[:parts], refs[parts : 2 * parts], refs[2 * parts :]
    early_ref, held, refs = refs[0], refs[1 : 1 + states], refs[1 + states :]
    if last:
        out_ref, sum_ref = refs
    else:
        state_ref, value_ref, inner_ref, sum_ref = refs
    half, block = panel[0].shape
    model_width = (first_late + late) * block
    total = jnp.sum(mine_square_ref[...] + other_square_ref[...], axis=(0, 1), keepdims=True)
    scale = model_width / (1.96 * total)
    add_up(mine, other, sum_ref)
    for index in range(CHUNKS):
        span, made = gram_rows(panel[2 * first_late :], sum_ref, index)
        made += early_ref[span, :]
        if step == 2:
            made = made * scale
        else:
            made = 1.5 * held[0][span, :] - (0.5 * scale) * made
        if last:
            made = (1.5 * held[1][span, :] - 0.5 * made) * (math.sqrt(model_width) * jnp.sqrt(scale))
            out_ref[:, span] = made.T
        else:
            state_ref[span, :] = made
            value_ref[:, span] = made.T.astype(value_ref.dtype)
    if last:
        return
    for index in range(inner_ref.shape[0] // block):
        product_of(value_ref, panel[2 * index : 2 * index + 2], inner_ref, index)


def rest_kernel(value_ref, *refs):
    panel, inner_ref = refs[:-1], refs[-1]
    for index in range(len(panel) // 2):
        product_of(value_ref, panel[2 * index : 2 * index + 2], inner_ref, index)


def in_vmem(*values):
    return [pltpu.with_memory_space_constraint(value, pltpu.VMEM) for value in values]


def apply_first(own, square, panel):
    block = panel[0].shape[1]
    return pl.pallas_call(
        first_kernel,
        in_specs=[VMEM] * (2 + len(panel)),
        out_specs=[VMEM, VMEM],
        out_shape=[
            pltpu.VMEM((len(panel) // 2 * block, block), jnp.bfloat16),
            pltpu.VMEM((8, block), jnp.float32),
        ],
        compiler_params=pltpu.CompilerParams(vmem_limit_bytes=VMEM_BYTES),
        name="first",
    )(*in_vmem(own, square, *panel))


def apply_early(panel, inner):
    half, block = panel[0].shape
    blocks = len(panel) // 2
    mine, other = zip(*inner)
    operands = in_vmem(*panel, *mine, *other)
    return pl.pallas_call(
        functools.partial(early_kernel, blocks, len(inner)),
        in_specs=[VMEM] * len(operands),
        out_specs=VMEM,
        out_shape=pltpu.VMEM((2 * half, block), jnp.float32),
        scratch_shapes=[pltpu.VMEM((blocks * block, block), jnp.bfloat16)],
        compiler_params=pltpu.CompilerParams(vmem_limit_bytes=VMEM_BYTES),
        name="early",
    )(*operands)


def apply_late(step, early, panel, inner, squares, held):
    half, block = panel[0].shape
    blocks, cols = len(panel) // 2, 2 * half
    late = sum(mine.shape[0] for mine, _ in inner) // block
    last = step == 3
    if last:
        out_shape = jax.ShapeDtypeStruct((block, cols), jnp.float32)
    else:
        out_shape = [
            pltpu.VMEM((cols, block), jnp.float32),
            pltpu.VMEM((block, cols), jnp.bfloat16),
            pltpu.VMEM((blocks // 2 * block, block), jnp.bfloat16),
        ]
    mine, other = zip(*inner)
    operands = in_vmem(*squares, *panel, *mine, *other, early, *held)
    return pl.pallas_call(
        functools.partial(late_kernel, step, (blocks - late, late), len(inner)),
        in_specs=[VMEM] * len(operands),
        out_specs=VMEM if last else [VMEM] * 3,
        out_shape=out_shape,
        scratch_shapes=[pltpu.VMEM((late * block, block), jnp.bfloat16)],
        compiler_params=pltpu.CompilerParams(vmem_limit_bytes=VMEM_BYTES),
        name="late%d" % step,
    )(*operands)


def apply_rest(value, panel):
    block = panel[0].shape[1]
    operands = in_vmem(value, *panel)
    return pl.pallas_call(
        rest_kernel,
        in_specs=[VMEM] * len(operands),
        out_specs=VMEM,
        out_shape=pltpu.VMEM((len(panel) // 2 * block, block), jnp.bfloat16),
        compiler_params=pltpu.CompilerParams(vmem_limit_bytes=VMEM_BYTES),
        name="rest",
    )(*operands)


def swap_cores(value):
    return lax.ppermute(value, "col", [(0, 1), (1, 0)])


def both_cores(value):
    if lax.axis_size("col") == 2:
        return value, swap_cores(value)
    total = lax.psum(value.astype(jnp.float32), "col").astype(value.dtype)
    return total, jnp.zeros_like(total)


def gather_rounds(outer_size):
    held = {(0, 0)}
    last = outer_size - 1
    rounds = []
    for k in range(1, outer_size):
        rounds.append([((k, 0), (k - 1, 0)), ((k - 1, 1), (k - 1, 0)), ((k - 1, 2), (k - 1, 0))])
    held.update(key for moves in rounds for key, _ in moves)
    rest = [(last, 1), (last, 2)] + [(k, 3) for k in range(outer_size)]
    while rest:
        moves, taken = [], set()
        for key in rest:
            ways = [("y", (key[0], key[1] ^ 2)), ("x", (key[0], key[1] ^ 1)), ("z", (key[0] - 1, key[1]))]
            if key == (last, 1):
                ways.reverse()
            if key[1] == 3:
                ways = ways[::-1] if (key[0] - 1, 3) in held else ways
            for link, source in ways:
                if source in held and link not in taken:
                    taken.add(link)
                    moves.append((key, source))
                    break
        held.update(key for key, _ in moves)
        rest = [key for key in rest if key not in held]
        rounds.append(moves)
    return rounds


def shards(embeddings, rotation, codes, codebooks):
    tok_rows, model_width = embeddings.shape
    dp, col = lax.axis_size("dp"), lax.axis_size("col")
    rows_total = tok_rows * dp
    block = model_width // dp
    inner_size = math.gcd(dp, INNER)
    outer_size = dp // inner_size
    wide = model_width // outer_size
    part_rows = tok_rows // col
    outer, inner = lax.axis_index("dp") // inner_size, lax.axis_index("dp") % inner_size
    core = lax.axis_index("col")

    def from_outer(value, step):
        pairs = [(i, (i // inner_size ^ step) * inner_size + i % inner_size) for i in range(dp)]
        return lax.ppermute(value, "dp", pairs)

    def from_inner(value, step):
        pairs = [(i, i // inner_size * inner_size + (i % inner_size ^ step)) for i in range(dp)]
        return lax.ppermute(value, "dp", pairs)

    steps = list(range(1, outer_size))
    codes_t = codes.T.astype(jnp.bfloat16)
    group_codes = [codes_t] + [from_outer(codes_t, step) for step in steps]

    table = jnp.transpose(codebooks, (0, 2, 1)).astype(jnp.float32)
    own = rebuild_rows(codes_t[None], table)
    rotated = lax.dot_general(
        rotation, embeddings, (((0,), (1,)), ((), ())), preferred_element_type=jnp.float32
    )
    residue = rotated - own.astype(jnp.float32)
    row_error = lax.psum(jnp.sum(residue * residue, axis=0), "col")
    weights = 1.0 / (1.0 + row_error / (2.0 * model_width))
    scaled = (weights[:, None] * embeddings.astype(jnp.float32)).astype(jnp.bfloat16)

    sends = [
        lax.dynamic_slice(scaled, (core * part_rows, (outer ^ step) * wide), (part_rows, wide))
        for step in steps
    ]
    shares = [from_outer(send, step) for send, step in zip(sends, steps)]
    local = lax.dynamic_slice_in_dim(scaled, outer * wide, wide, 1)
    rebuilt = rebuild_rows(jnp.stack(group_codes), table)
    shares, rebuilt = lax.optimization_barrier((shares, rebuilt))
    pieces = []
    for share in shares:
        if part_rows % LANES:
            pieces.append(lax.all_gather(share, "col", axis=0, tiled=True))
            continue
        pieces.append(share)
        for turn in range(1, col):
            pairs = [(i, (i - turn) % col) for i in range(col)]
            pieces.append(lax.ppermute(share, "col", pairs))

    place = jnp.stack([core, inner]).astype(jnp.int32)
    start_row = lax.axis_index("dp") * block
    prior = lax.dynamic_slice_in_dim(rotation, start_row, block, 0).T
    prior = 0.2 * rows_total * prior.astype(jnp.float32)
    half = prior.shape[0] // 2
    blocks_for = functools.partial(
        cross_blocks, place=place, rebuilt=rebuilt, prior=prior, local=local, pieces=pieces
    )
    near = [(1, 2), (2, 1)]
    sent = blocks_for([((one, 3), side * half) for side, (one, _) in enumerate(near)], jnp.bfloat16)
    came = [from_inner(value, one) for value, (one, _) in zip(sent, near)]
    kept = blocks_for(
        [((0,), side * half) for side in range(2)]
        + [((two,), side * half) for side, (_, two) in enumerate(near)],
        jnp.float32,
    )
    starts = []
    for side, (_, two) in enumerate(near):
        passed = kept[2 + side] + came[side][half:].astype(jnp.float32)
        last = from_inner(passed.astype(jnp.bfloat16), two)
        starts.append(kept[side] + came[side][:half].astype(jnp.float32) + last.astype(jnp.float32))
    narrow = [value.astype(jnp.bfloat16) for value in starts]
    start = jnp.concatenate(starts, axis=0)

    def ring(value):
        pairs = [(i, (i + inner_size) % dp) for i in range(dp)]
        return lax.ppermute(value, "dp", pairs)

    own = jnp.concatenate(narrow, axis=0).T
    held = [{(0, 0): value} for value in narrow]

    def move(side, key, source):
        value = held[side][source]
        return ring(value) if key[0] != source[0] else from_inner(value, key[1] ^ source[1])

    def halves(keys):
        return [held[side][key] for key in keys for side in range(2)]

    order, products = [(0, 0)], []
    square = jnp.zeros((8, block), jnp.float32)
    fresh = [(0, 0)]
    for moves in gather_rounds(outer_size):
        arrived = [[move(side, key, source) for key, source in moves] for side in range(2)]
        product, square = apply_first(own, square, halves(fresh))
        arrived[0], product, square = lax.optimization_barrier((arrived[0], product, square))
        arrived[1] = lax.optimization_barrier(arrived[1])
        fresh = [key for key, _ in moves]
        for side in range(2):
            held[side].update(zip(fresh, arrived[side]))
        order += fresh
        products.append(both_cores(product))
    product, square = apply_first(own, square, halves(fresh))
    products.append(both_cores(product))
    panel = halves(order)
    squares = both_cores(square)

    first_late = sum(mine.shape[0] for mine, _ in products[:-2]) // block
    early = apply_early(panel[: 2 * first_late], products[:-2])
    inner = products[-2:]
    states = [start]
    middle = len(panel) // 2
    for step in range(3):
        state, value, product = apply_late(step, early, panel, inner, squares, states[-1:])
        states.append(state)
        product = both_cores(product)
        inner = [both_cores(apply_rest(value, panel[middle:]))]
        early = apply_early(panel[:middle], [product])
    return apply_late(3, early, panel, inner, squares, [states[3], states[1]])


def solution(mesh):
    placed = (P("dp", None), P(None, "col"), P("dp", "col"), P("col", None, None))
    return jax.shard_map(
        shards, mesh=mesh, in_specs=placed, out_specs=P("dp", "col"), check_vma=False
    )
```

```python
import functools
import math

import jax
import jax.numpy as jnp
from jax import lax
from jax.experimental import pallas as pl
from jax.experimental.pallas import tpu as pltpu
from jax.sharding import PartitionSpec as P

LANES = 128
GROUP = 8
CHUNKS = 4
INNER = 4
VMEM_BYTES = 24 * 1024 * 1024
ANY = pl.BlockSpec(memory_space=pl.ANY)
VMEM = pl.BlockSpec(memory_space=pltpu.VMEM)


def lookup_kernel(codes_ref, table_ref, weights_ref, out_ref, ids_ref):
    subs, rows = codes_ref.shape[1:]
    width = table_ref.shape[1]
    halves = table_ref.shape[2] // LANES
    first_out = pl.program_id(0) * (subs * width)
    ids_ref[...] = codes_ref[0].astype(jnp.float32).astype(jnp.int32)

    def body(step, carry):
        base = pl.multiple_of(step * GROUP, GROUP)
        for first in range(0, rows, LANES):
            lanes = pl.ds(pl.multiple_of(pl.program_id(1) * rows + first, LANES), LANES)
            ids_all = ids_ref[pl.ds(base, GROUP), first : first + LANES]
            scale = jnp.broadcast_to(weights_ref[0, :, first : first + LANES], (width, LANES))
            for pair in range(0, GROUP, 2):
                both = []
                for sub in (pair, pair + 1):
                    ids = jnp.broadcast_to(ids_all[sub : sub + 1], (width, LANES))
                    lane = jnp.bitwise_and(ids, LANES - 1)
                    picked = None
                    for half in range(halves):
                        entries = table_ref[base + sub, :, half * LANES : (half + 1) * LANES]
                        got = jnp.take_along_axis(
                            entries, lane, axis=1, mode="promise_in_bounds"
                        )
                        picked = got if half == 0 else jnp.where(ids >= half * LANES, got, picked)
                    both.append(picked * scale)
                row = pl.multiple_of(first_out + (base + pair) * width, 2 * width)
                out_ref[pl.ds(row, 2 * width), lanes] = jnp.concatenate(both, axis=0).astype(
                    out_ref.dtype
                )
        return carry

    lax.fori_loop(0, subs // GROUP, body, 0)


def rebuild_rows(codes, table, weights):
    blocks, subs, rows = codes.shape
    width, centroids = table.shape[1:]
    tile = min(64, subs)
    return pl.pallas_call(
        lookup_kernel,
        grid=(subs // tile, blocks),
        in_specs=[
            pl.BlockSpec((1, tile, rows), lambda m, s: (s, m, 0)),
            pl.BlockSpec((tile, width, centroids), lambda m, s: (m, 0, 0)),
            pl.BlockSpec((1, 1, rows), lambda m, s: (s, 0, 0)),
        ],
        out_specs=VMEM,
        scratch_shapes=[pltpu.VMEM((tile, rows), jnp.int32)],
        out_shape=pltpu.VMEM((subs * width, blocks * rows), jnp.bfloat16),
        compiler_params=pltpu.CompilerParams(vmem_limit_bytes=VMEM_BYTES),
        name="lookup",
    )(codes, table, weights[:, None, :])


def cross_kernel(plan, place_ref, own_ref, rebuilt_ref, prior_ref, local_ref, *refs):
    pieces, outs = refs[: len(refs) - len(plan)], refs[len(refs) - len(plan) :]
    rows = local_ref.shape[0]
    part_rows, col = (pieces[0].shape[0], rows // pieces[0].shape[0]) if pieces else (rows, 1)
    for (targets, first_row), out_ref in zip(plan, outs):
        height, block = out_ref.shape[0] // len(targets), out_ref.shape[1]
        span = slice(first_row, first_row + height)
        left = [own_ref[span, :]]
        for index in range(len(pieces)):
            step, turn = divmod(index, col)
            first = step * rows + lax.rem(place_ref[0] + turn, col) * part_rows
            left.append(rebuilt_ref[span, pl.ds(pl.multiple_of(first, part_rows), part_rows)])
        left = jnp.concatenate(left, axis=1)
        for slot, target in enumerate(targets):
            place = lax.bitwise_xor(place_ref[1], target)
            lanes = pl.ds(pl.multiple_of(place * block, block), block)
            right = [local_ref[:, lanes]] + [piece_ref[:, lanes] for piece_ref in pieces]
            total = jnp.dot(
                left, jnp.concatenate(right, axis=0), preferred_element_type=jnp.float32
            )
            if target == 0:
                total += prior_ref[span, :]
            out_ref[slot * height : (slot + 1) * height, :] = total.astype(out_ref.dtype)


def cross_blocks(plan, dtype, place, own, rebuilt, prior, local, pieces):
    operands = in_vmem(own, rebuilt, prior, local, *pieces)
    half, block = prior.shape[0] // 2, prior.shape[1]
    return pl.pallas_call(
        functools.partial(cross_kernel, plan),
        in_specs=[pl.BlockSpec(memory_space=pltpu.SMEM)] + [VMEM] * len(operands),
        out_specs=[VMEM] * len(plan),
        out_shape=[pltpu.VMEM((len(targets) * half, block), dtype) for targets, _ in plan],
        compiler_params=pltpu.CompilerParams(vmem_limit_bytes=VMEM_BYTES),
        name="cross",
    )(place, *operands)


def product_of(value_ref, halves, inner_ref, index):
    half, block = halves[0].shape
    product = jnp.zeros((value_ref.shape[0], block), jnp.float32)
    for first, half_ref in enumerate(halves):
        product += jnp.dot(
            value_ref[:, first * half : (first + 1) * half], half_ref[...],
            preferred_element_type=jnp.float32,
        )
    inner_ref[index * block : (index + 1) * block, :] = product.T.astype(inner_ref.dtype)


def first_kernel(own_ref, before_ref, *refs):
    panel, (inner_ref, square_ref) = refs[:-2], refs[-2:]
    half, block = panel[0].shape
    square = before_ref[...]
    for index in range(len(panel) // 2):
        halves = panel[2 * index : 2 * index + 2]
        product_of(own_ref, halves, inner_ref, index)
        for half_ref in halves:
            values = half_ref[...].astype(jnp.float32)
            square += jnp.sum((values * values).reshape(half // 8, 8, block), axis=0)
    square_ref[...] = square


def add_up(mine, other, sum_ref):
    first = 0
    for mine_ref, other_ref in zip(mine, other):
        sum_ref[first : first + mine_ref.shape[0], :] = mine_ref[...] + other_ref[...]
        first += mine_ref.shape[0]


def gram_rows(panel, sum_ref, index):
    half = panel[0].shape[0]
    chunk = 2 * half // CHUNKS
    side, first = divmod(index * chunk, half)
    rows = [half_ref[first : first + chunk, :] for half_ref in panel[side::2]]
    made = jnp.dot(
        jnp.concatenate(rows, axis=1), sum_ref[...], preferred_element_type=jnp.float32
    )
    return slice(index * chunk, (index + 1) * chunk), made


def early_kernel(blocks, parts, *refs):
    panel, refs = refs[: 2 * blocks], refs[2 * blocks :]
    mine, other, (out_ref, sum_ref) = refs[:parts], refs[parts : 2 * parts], refs[2 * parts :]
    add_up(mine, other, sum_ref)
    for index in range(CHUNKS):
        span, made = gram_rows(panel, sum_ref, index)
        out_ref[span, :] = made


def late_kernel(step, blocks, parts, mine_square_ref, other_square_ref, *refs):
    last = step == 3
    states = 2 if last else 1
    first_late, late = blocks
    panel, refs = refs[: 2 * (first_late + late)], refs[2 * (first_late + late) :]
    mine, other, refs = refs[:parts], refs[parts : 2 * parts], refs[2 * parts :]
    early_ref, held, refs = refs[0], refs[1 : 1 + states], refs[1 + states :]
    if last:
        out_ref, sum_ref = refs
    else:
        state_ref, value_ref, inner_ref, sum_ref = refs
    half, block = panel[0].shape
    model_width = (first_late + late) * block
    total = jnp.sum(mine_square_ref[...] + other_square_ref[...], axis=(0, 1), keepdims=True)
    scale = model_width / (1.96 * total)
    add_up(mine, other, sum_ref)
    for index in range(CHUNKS):
        span, made = gram_rows(panel[2 * first_late :], sum_ref, index)
        made += early_ref[span, :]
        if step == 2:
            made = made * scale
        else:
            made = 1.5 * held[0][span, :] - (0.5 * scale) * made
        if last:
            made = (1.5 * held[1][span, :] - 0.5 * made) * (math.sqrt(model_width) * jnp.sqrt(scale))
            out_ref[:, span] = made.T
        else:
            state_ref[span, :] = made
            value_ref[:, span] = made.T.astype(value_ref.dtype)
    if last:
        return
    for index in range(inner_ref.shape[0] // block):
        product_of(value_ref, panel[2 * index : 2 * index + 2], inner_ref, index)


def rest_kernel(value_ref, *refs):
    panel, inner_ref = refs[:-1], refs[-1]
    for index in range(len(panel) // 2):
        product_of(value_ref, panel[2 * index : 2 * index + 2], inner_ref, index)


def in_vmem(*values):
    return [pltpu.with_memory_space_constraint(value, pltpu.VMEM) for value in values]


def apply_first(own, square, panel):
    block = panel[0].shape[1]
    return pl.pallas_call(
        first_kernel,
        in_specs=[VMEM] * (2 + len(panel)),
        out_specs=[VMEM, VMEM],
        out_shape=[
            pltpu.VMEM((len(panel) // 2 * block, block), jnp.bfloat16),
            pltpu.VMEM((8, block), jnp.float32),
        ],
        compiler_params=pltpu.CompilerParams(vmem_limit_bytes=VMEM_BYTES),
        name="first",
    )(*in_vmem(own, square, *panel))


def apply_early(panel, inner):
    half, block = panel[0].shape
    blocks = len(panel) // 2
    mine, other = zip(*inner)
    operands = in_vmem(*panel, *mine, *other)
    return pl.pallas_call(
        functools.partial(early_kernel, blocks, len(inner)),
        in_specs=[VMEM] * len(operands),
        out_specs=VMEM,
        out_shape=pltpu.VMEM((2 * half, block), jnp.float32),
        scratch_shapes=[pltpu.VMEM((blocks * block, block), jnp.bfloat16)],
        compiler_params=pltpu.CompilerParams(vmem_limit_bytes=VMEM_BYTES),
        name="early",
    )(*operands)


def apply_late(step, early, panel, inner, squares, held):
    half, block = panel[0].shape
    blocks, cols = len(panel) // 2, 2 * half
    late = sum(mine.shape[0] for mine, _ in inner) // block
    last = step == 3
    if last:
        out_shape = jax.ShapeDtypeStruct((block, cols), jnp.float32)
    else:
        out_shape = [
            pltpu.VMEM((cols, block), jnp.float32),
            pltpu.VMEM((block, cols), jnp.bfloat16),
            pltpu.VMEM((blocks // 2 * block, block), jnp.bfloat16),
        ]
    mine, other = zip(*inner)
    operands = in_vmem(*squares, *panel, *mine, *other, early, *held)
    return pl.pallas_call(
        functools.partial(late_kernel, step, (blocks - late, late), len(inner)),
        in_specs=[VMEM] * len(operands),
        out_specs=VMEM if last else [VMEM] * 3,
        out_shape=out_shape,
        scratch_shapes=[pltpu.VMEM((late * block, block), jnp.bfloat16)],
        compiler_params=pltpu.CompilerParams(vmem_limit_bytes=VMEM_BYTES),
        name="late%d" % step,
    )(*operands)


def apply_rest(value, panel):
    block = panel[0].shape[1]
    operands = in_vmem(value, *panel)
    return pl.pallas_call(
        rest_kernel,
        in_specs=[VMEM] * len(operands),
        out_specs=VMEM,
        out_shape=pltpu.VMEM((len(panel) // 2 * block, block), jnp.bfloat16),
        compiler_params=pltpu.CompilerParams(vmem_limit_bytes=VMEM_BYTES),
        name="rest",
    )(*operands)


def swap_cores(value):
    return lax.ppermute(value, "col", [(0, 1), (1, 0)])


def both_cores(value):
    if lax.axis_size("col") == 2:
        return value, swap_cores(value)
    total = lax.psum(value.astype(jnp.float32), "col").astype(value.dtype)
    return total, jnp.zeros_like(total)


def gather_rounds(outer_size):
    held = {(0, 0)}
    last = outer_size - 1
    rounds = []
    for k in range(1, outer_size):
        rounds.append([((k, 0), (k - 1, 0)), ((k - 1, 1), (k - 1, 0)), ((k - 1, 2), (k - 1, 0))])
    held.update(key for moves in rounds for key, _ in moves)
    rest = [(last, 1), (last, 2)] + [(k, 3) for k in range(outer_size)]
    while rest:
        moves, taken = [], set()
        for key in rest:
            ways = [("y", (key[0], key[1] ^ 2)), ("x", (key[0], key[1] ^ 1)), ("z", (key[0] - 1, key[1]))]
            if key == (last, 1):
                ways.reverse()
            if key[1] == 3:
                ways = ways[::-1] if (key[0] - 1, 3) in held else ways
            for link, source in ways:
                if source in held and link not in taken:
                    taken.add(link)
                    moves.append((key, source))
                    break
        held.update(key for key, _ in moves)
        rest = [key for key in rest if key not in held]
        rounds.append(moves)
    return rounds


def shards(embeddings, rotation, codes, codebooks):
    tok_rows, model_width = embeddings.shape
    dp, col = lax.axis_size("dp"), lax.axis_size("col")
    rows_total = tok_rows * dp
    block = model_width // dp
    inner_size = math.gcd(dp, INNER)
    outer_size = dp // inner_size
    wide = model_width // outer_size
    part_rows = tok_rows // col
    outer, inner = lax.axis_index("dp") // inner_size, lax.axis_index("dp") % inner_size
    core = lax.axis_index("col")

    def from_outer(value, step):
        pairs = [(i, (i // inner_size ^ step) * inner_size + i % inner_size) for i in range(dp)]
        return lax.ppermute(value, "dp", pairs)

    def from_inner(value, step):
        pairs = [(i, i // inner_size * inner_size + (i % inner_size ^ step)) for i in range(dp)]
        return lax.ppermute(value, "dp", pairs)

    steps = list(range(1, outer_size))
    codes_t = codes.T.astype(jnp.bfloat16)
    group_codes = [from_outer(codes_t, step) for step in steps]

    table = jnp.transpose(codebooks, (0, 2, 1)).astype(jnp.float32)
    own = rebuild_rows(codes_t[None], table, jnp.ones((1, tok_rows), jnp.float32))
    rotated = lax.dot_general(
        rotation, embeddings, (((0,), (1,)), ((), ())), preferred_element_type=jnp.float32
    )
    residue = rotated - own.astype(jnp.float32)
    row_error = jnp.sum(residue * residue, axis=0)

    sends = [
        lax.dynamic_slice(embeddings, (core * part_rows, (outer ^ step) * wide), (part_rows, wide))
        for step in steps
    ]
    sends[:-1], row_error, group_codes = lax.optimization_barrier(
        (sends[:-1], row_error, group_codes)
    )
    shares = [from_outer(send, step) for send, step in zip(sends[:-1], steps)]
    weights = 1.0 / (1.0 + lax.psum(row_error, "col") / (2.0 * model_width))
    weights, shares = lax.optimization_barrier((weights, shares))
    group_weights = [from_outer(weights, step) for step in steps]
    sends[-1:], group_weights = lax.optimization_barrier((sends[-1:], group_weights))
    rebuilt = rebuild_rows(jnp.stack(group_codes), table, jnp.stack(group_weights))
    own = (own.astype(jnp.float32) * weights[None, :]).astype(jnp.bfloat16)
    late = [from_outer(send, step) for send, step in zip(sends[-1:], steps[-1:])]
    late, rebuilt = lax.optimization_barrier((late, rebuilt))
    local = lax.dynamic_slice_in_dim(embeddings, outer * wide, wide, 1)
    pieces = []
    for share in shares + late:
        if part_rows % LANES:
            pieces.append(lax.all_gather(share, "col", axis=0, tiled=True))
            continue
        pieces.append(share)
        for turn in range(1, col):
            pairs = [(i, (i - turn) % col) for i in range(col)]
            pieces.append(lax.ppermute(share, "col", pairs))

    place = jnp.stack([core, inner]).astype(jnp.int32)
    start_row = lax.axis_index("dp") * block
    prior = lax.dynamic_slice_in_dim(rotation, start_row, block, 0).T
    prior = 0.2 * rows_total * prior.astype(jnp.float32)
    half = prior.shape[0] // 2
    blocks_for = functools.partial(
        cross_blocks, place=place, own=own, rebuilt=rebuilt, prior=prior, local=local, pieces=pieces
    )
    near = [(1, 2), (2, 1)]
    sent = blocks_for([((one, 3), side * half) for side, (one, _) in enumerate(near)], jnp.bfloat16)
    came = [from_inner(value, one) for value, (one, _) in zip(sent, near)]
    kept = blocks_for(
        [((0,), side * half) for side in range(2)]
        + [((two,), side * half) for side, (_, two) in enumerate(near)],
        jnp.float32,
    )
    starts = []
    for side, (_, two) in enumerate(near):
        passed = kept[2 + side] + came[side][half:].astype(jnp.float32)
        last = from_inner(passed.astype(jnp.bfloat16), two)
        starts.append(kept[side] + came[side][:half].astype(jnp.float32) + last.astype(jnp.float32))
    narrow = [value.astype(jnp.bfloat16) for value in starts]
    start = jnp.concatenate(starts, axis=0)

    def ring(value):
        pairs = [(i, (i + inner_size) % dp) for i in range(dp)]
        return lax.ppermute(value, "dp", pairs)

    own = jnp.concatenate(narrow, axis=0).T
    held = [{(0, 0): value} for value in narrow]

    def move(side, key, source):
        value = held[side][source]
        return ring(value) if key[0] != source[0] else from_inner(value, key[1] ^ source[1])

    def halves(keys):
        return [held[side][key] for key in keys for side in range(2)]

    order, products = [(0, 0)], []
    square = jnp.zeros((8, block), jnp.float32)
    fresh = [(0, 0)]
    for moves in gather_rounds(outer_size):
        arrived = [[move(side, key, source) for key, source in moves] for side in range(2)]
        product, square = apply_first(own, square, halves(fresh))
        arrived[0], product, square = lax.optimization_barrier((arrived[0], product, square))
        arrived[1] = lax.optimization_barrier(arrived[1])
        fresh = [key for key, _ in moves]
        for side in range(2):
            held[side].update(zip(fresh, arrived[side]))
        order += fresh
        products.append(both_cores(product))
    product, square = apply_first(own, square, halves(fresh))
    products.append(both_cores(product))
    panel = halves(order)
    squares = both_cores(square)

    first_late = sum(mine.shape[0] for mine, _ in products[:-2]) // block
    early = apply_early(panel[: 2 * first_late], products[:-2])
    inner = products[-2:]
    states = [start]
    middle = len(panel) // 2
    for step in range(3):
        state, value, product = apply_late(step, early, panel, inner, squares, states[-1:])
        states.append(state)
        product = both_cores(product)
        inner = [both_cores(apply_rest(value, panel[middle:]))]
        early = apply_early(panel[:middle], [product])
    return apply_late(3, early, panel, inner, squares, [states[3], states[1]])


def solution(mesh):
    placed = (P("dp", None), P(None, "col"), P("dp", "col"), P("col", None, None))
    return jax.shard_map(
        shards, mesh=mesh, in_specs=placed, out_specs=P("dp", "col"), check_vma=False
    )
```

```python
import functools
import math

import jax
import jax.numpy as jnp
from jax import lax
from jax.experimental import pallas as pl
from jax.experimental.pallas import tpu as pltpu
from jax.sharding import PartitionSpec as P

LANES = 128
GROUP = 8
CHUNKS = 4
INNER = 4
VMEM_BYTES = 22 * 1024 * 1024
ANY = pl.BlockSpec(memory_space=pl.ANY)
VMEM = pl.BlockSpec(memory_space=pltpu.VMEM)


def lookup_kernel(codes_ref, table_ref, out_ref, ids_ref):
    subs, rows = codes_ref.shape[1:]
    width = table_ref.shape[1]
    halves = table_ref.shape[2] // LANES
    first_out = pl.program_id(0) * (subs * width)
    ids_ref[...] = codes_ref[0].astype(jnp.float32).astype(jnp.int32)

    def body(step, carry):
        base = pl.multiple_of(step * GROUP, GROUP)
        for first in range(0, rows, LANES):
            lanes = pl.ds(pl.multiple_of(pl.program_id(1) * rows + first, LANES), LANES)
            ids_all = ids_ref[pl.ds(base, GROUP), first : first + LANES]
            for pair in range(0, GROUP, 2):
                both = []
                for sub in (pair, pair + 1):
                    ids = jnp.broadcast_to(ids_all[sub : sub + 1], (width, LANES))
                    lane = jnp.bitwise_and(ids, LANES - 1)
                    picked = None
                    for half in range(halves):
                        entries = table_ref[base + sub, :, half * LANES : (half + 1) * LANES]
                        got = jnp.take_along_axis(
                            entries, lane, axis=1, mode="promise_in_bounds"
                        )
                        picked = got if half == 0 else jnp.where(ids >= half * LANES, got, picked)
                    both.append(picked)
                row = pl.multiple_of(first_out + (base + pair) * width, 2 * width)
                out_ref[pl.ds(row, 2 * width), lanes] = jnp.concatenate(both, axis=0).astype(
                    out_ref.dtype
                )
        return carry

    lax.fori_loop(0, subs // GROUP, body, 0)


def rebuild_rows(codes, table):
    blocks, subs, rows = codes.shape
    width, centroids = table.shape[1:]
    tile = min(64, subs)
    return pl.pallas_call(
        lookup_kernel,
        grid=(subs // tile, blocks),
        in_specs=[
            pl.BlockSpec((1, tile, rows), lambda m, s: (s, m, 0)),
            pl.BlockSpec((tile, width, centroids), lambda m, s: (m, 0, 0)),
        ],
        out_specs=VMEM,
        scratch_shapes=[pltpu.VMEM((tile, rows), jnp.int32)],
        out_shape=pltpu.VMEM((subs * width, blocks * rows), jnp.bfloat16),
        compiler_params=pltpu.CompilerParams(vmem_limit_bytes=VMEM_BYTES),
        name="lookup",
    )(codes, table)


def slices_kernel(steps, place_ref, weights_ref, rows_ref, local_ref, *sends):
    part_rows, wide = sends[0].shape

    def scaled(first, rows, step):
        lanes = pl.ds(pl.multiple_of(lax.bitwise_xor(place_ref[2], step) * wide, wide), wide)
        column = jnp.broadcast_to(weights_ref[:, pl.ds(first, rows)], (LANES, rows)).T
        values = rows_ref[pl.ds(first, rows), lanes].astype(jnp.float32)
        column = jnp.concatenate([column] * (wide // LANES), axis=1)
        return (values * column).astype(local_ref.dtype)

    first = pl.multiple_of(place_ref[0] * part_rows, part_rows)
    for step, send_ref in zip(steps, sends):
        send_ref[...] = scaled(first, part_rows, step)
    for first in range(0, local_ref.shape[0], part_rows):
        local_ref[first : first + part_rows, :] = scaled(first, part_rows, 0)


def weighted_slices(place, weights, embeddings, part_rows, wide, steps):
    rows = embeddings.shape[0]
    if part_rows % LANES:
        scaled = (weights[:, None] * embeddings.astype(jnp.float32)).astype(jnp.bfloat16)
        first = place[0] * part_rows
        return [lax.dynamic_slice_in_dim(scaled, place[2] * wide, wide, 1)] + [
            lax.dynamic_slice(scaled, (first, (place[2] ^ step) * wide), (part_rows, wide))
            for step in steps
        ]
    return pl.pallas_call(
        functools.partial(slices_kernel, steps),
        in_specs=[pl.BlockSpec(memory_space=pltpu.SMEM), VMEM, VMEM],
        out_specs=[VMEM] * (1 + len(steps)),
        out_shape=[pltpu.VMEM((rows, wide), jnp.bfloat16)]
        + [pltpu.VMEM((part_rows, wide), jnp.bfloat16)] * len(steps),
        compiler_params=pltpu.CompilerParams(vmem_limit_bytes=VMEM_BYTES),
        name="slices",
    )(place, *in_vmem(weights[None, :], embeddings))


def cross_kernel(plan, place_ref, rebuilt_ref, prior_ref, local_ref, *refs):
    pieces, outs = refs[: len(refs) - len(plan)], refs[len(refs) - len(plan) :]
    rows = local_ref.shape[0]
    part_rows, col = (pieces[0].shape[0], rows // pieces[0].shape[0]) if pieces else (rows, 1)
    for (targets, first_row), out_ref in zip(plan, outs):
        height, block = out_ref.shape[0] // len(targets), out_ref.shape[1]
        span = slice(first_row, first_row + height)
        for slot, target in enumerate(targets):
            place = lax.bitwise_xor(place_ref[1], target)
            lanes = pl.ds(pl.multiple_of(place * block, block), block)
            total = jnp.dot(
                rebuilt_ref[span, :rows], local_ref[:, lanes], preferred_element_type=jnp.float32
            )
            for index, piece_ref in enumerate(pieces):
                step, turn = divmod(index, col)
                first = (step + 1) * rows + lax.rem(place_ref[0] + turn, col) * part_rows
                total += jnp.dot(
                    rebuilt_ref[span, pl.ds(pl.multiple_of(first, part_rows), part_rows)],
                    piece_ref[:, lanes],
                    preferred_element_type=jnp.float32,
                )
            if target == 0:
                total += prior_ref[span, :]
            out_ref[slot * height : (slot + 1) * height, :] = total.astype(out_ref.dtype)


def cross_blocks(plan, dtype, place, rebuilt, prior, local, pieces):
    operands = in_vmem(rebuilt, prior, local, *pieces)
    half, block = prior.shape[0] // 2, prior.shape[1]
    return pl.pallas_call(
        functools.partial(cross_kernel, plan),
        in_specs=[pl.BlockSpec(memory_space=pltpu.SMEM)] + [VMEM] * len(operands),
        out_specs=[VMEM] * len(plan),
        out_shape=[pltpu.VMEM((len(targets) * half, block), dtype) for targets, _ in plan],
        compiler_params=pltpu.CompilerParams(vmem_limit_bytes=VMEM_BYTES),
        name="cross",
    )(place, *operands)


def product_of(value_ref, halves, inner_ref, index):
    half, block = halves[0].shape
    product = jnp.zeros((value_ref.shape[0], block), jnp.float32)
    for first, half_ref in enumerate(halves):
        product += jnp.dot(
            value_ref[:, first * half : (first + 1) * half], half_ref[...],
            preferred_element_type=jnp.float32,
        )
    inner_ref[:, index * block : (index + 1) * block] = product.astype(inner_ref.dtype)


def first_kernel(own_ref, before_ref, *refs):
    panel, (inner_ref, square_ref) = refs[:-2], refs[-2:]
    half, block = panel[0].shape
    square = before_ref[...]
    for index in range(len(panel) // 2):
        halves = panel[2 * index : 2 * index + 2]
        product_of(own_ref, halves, inner_ref, index)
        for half_ref in halves:
            values = half_ref[...].astype(jnp.float32)
            square += jnp.sum((values * values).reshape(half // 8, 8, block), axis=0)
    square_ref[...] = square


def add_up(mine, other, sum_ref):
    first = 0
    for mine_ref, other_ref in zip(mine, other):
        width = mine_ref.shape[1]
        sum_ref[:, first : first + width] = mine_ref[...] + other_ref[...]
        first += width


def gram_columns(panel, sum_ref, index):
    half = panel[0].shape[0]
    chunk = 2 * half // CHUNKS
    side, first = divmod(index * chunk, half)
    rows = [half_ref[first : first + chunk, :] for half_ref in panel[side::2]]
    made = lax.dot_general(
        sum_ref[...], jnp.concatenate(rows, axis=1), (((1,), (1,)), ((), ())),
        preferred_element_type=jnp.float32,
    )
    return slice(index * chunk, (index + 1) * chunk), made


def early_kernel(blocks, parts, *refs):
    panel, refs = refs[: 2 * blocks], refs[2 * blocks :]
    mine, other, (out_ref, sum_ref) = refs[:parts], refs[parts : 2 * parts], refs[2 * parts :]
    add_up(mine, other, sum_ref)
    for index in range(CHUNKS):
        span, made = gram_columns(panel, sum_ref, index)
        out_ref[:, span] = made


def late_kernel(step, blocks, parts, mine_square_ref, other_square_ref, *refs):
    last = step == 3
    states = 2 if last else 1
    first_late, late = blocks
    panel, refs = refs[: 2 * (first_late + late)], refs[2 * (first_late + late) :]
    mine, other, refs = refs[:parts], refs[parts : 2 * parts], refs[2 * parts :]
    early_ref, held, refs = refs[0], refs[1 : 1 + states], refs[1 + states :]
    if last:
        out_ref, sum_ref = refs
    else:
        state_ref, value_ref, inner_ref, sum_ref = refs
    half, block = panel[0].shape
    model_width = (first_late + late) * block
    total = jnp.sum(mine_square_ref[...] + other_square_ref[...], axis=(0, 1), keepdims=True)
    scale = model_width / (1.96 * total)
    add_up(mine, other, sum_ref)
    for index in range(CHUNKS):
        span, made = gram_columns(panel[2 * first_late :], sum_ref, index)
        made += early_ref[:, span]
        if step == 2:
            made = made * scale
        else:
            made = 1.5 * held[0][:, span] - (0.5 * scale) * made
        if last:
            made = (1.5 * held[1][:, span] - 0.5 * made) * (math.sqrt(model_width) * jnp.sqrt(scale))
            out_ref[:, span] = made
        else:
            state_ref[:, span] = made
            value_ref[:, span] = made.astype(value_ref.dtype)
    if last:
        return
    for index in range(inner_ref.shape[1] // block):
        product_of(value_ref, panel[2 * index : 2 * index + 2], inner_ref, index)


def rest_kernel(value_ref, *refs):
    panel, inner_ref = refs[:-1], refs[-1]
    for index in range(len(panel) // 2):
        product_of(value_ref, panel[2 * index : 2 * index + 2], inner_ref, index)


def in_vmem(*values):
    return [pltpu.with_memory_space_constraint(value, pltpu.VMEM) for value in values]


def apply_first(own, square, panel):
    block = panel[0].shape[1]
    return pl.pallas_call(
        first_kernel,
        in_specs=[VMEM] * (2 + len(panel)),
        out_specs=[VMEM, VMEM],
        out_shape=[
            pltpu.VMEM((block, len(panel) // 2 * block), jnp.bfloat16),
            pltpu.VMEM((8, block), jnp.float32),
        ],
        compiler_params=pltpu.CompilerParams(vmem_limit_bytes=VMEM_BYTES),
        name="first",
    )(*in_vmem(own, square, *panel))


def apply_early(panel, inner):
    half, block = panel[0].shape
    blocks = len(panel) // 2
    mine, other = zip(*inner)
    operands = in_vmem(*panel, *mine, *other)
    return pl.pallas_call(
        functools.partial(early_kernel, blocks, len(inner)),
        in_specs=[VMEM] * len(operands),
        out_specs=VMEM,
        out_shape=pltpu.VMEM((block, 2 * half), jnp.float32),
        scratch_shapes=[pltpu.VMEM((block, blocks * block), jnp.bfloat16)],
        compiler_params=pltpu.CompilerParams(vmem_limit_bytes=VMEM_BYTES),
        name="early",
    )(*operands)


def apply_late(step, early, panel, inner, squares, held):
    half, block = panel[0].shape
    blocks, cols = len(panel) // 2, 2 * half
    late = sum(mine.shape[1] for mine, _ in inner) // block
    last = step == 3
    if last:
        out_shape = jax.ShapeDtypeStruct((block, cols), jnp.float32)
    else:
        out_shape = [
            pltpu.VMEM((block, cols), jnp.float32),
            pltpu.VMEM((block, cols), jnp.bfloat16),
            pltpu.VMEM((block, blocks // 2 * block), jnp.bfloat16),
        ]
    mine, other = zip(*inner)
    operands = in_vmem(*squares, *panel, *mine, *other, early, *held)
    return pl.pallas_call(
        functools.partial(late_kernel, step, (blocks - late, late), len(inner)),
        in_specs=[VMEM] * len(operands),
        out_specs=VMEM if last else [VMEM] * 3,
        out_shape=out_shape,
        scratch_shapes=[pltpu.VMEM((block, late * block), jnp.bfloat16)],
        compiler_params=pltpu.CompilerParams(vmem_limit_bytes=VMEM_BYTES),
        name="late%d" % step,
    )(*operands)


def apply_rest(value, panel):
    block = panel[0].shape[1]
    operands = in_vmem(value, *panel)
    return pl.pallas_call(
        rest_kernel,
        in_specs=[VMEM] * len(operands),
        out_specs=VMEM,
        out_shape=pltpu.VMEM((block, len(panel) // 2 * block), jnp.bfloat16),
        compiler_params=pltpu.CompilerParams(vmem_limit_bytes=VMEM_BYTES),
        name="rest",
    )(*operands)


def swap_cores(value):
    return lax.ppermute(value, "col", [(0, 1), (1, 0)])


def both_cores(value):
    if lax.axis_size("col") == 2:
        return value, swap_cores(value)
    total = lax.psum(value.astype(jnp.float32), "col").astype(value.dtype)
    return total, jnp.zeros_like(total)


def gather_rounds(outer_size):
    held = {(0, 0)}
    last = outer_size - 1
    rounds = []
    for k in range(1, outer_size):
        rounds.append([((k, 0), (k - 1, 0)), ((k - 1, 1), (k - 1, 0)), ((k - 1, 2), (k - 1, 0))])
    held.update(key for moves in rounds for key, _ in moves)
    rest = [(last, 1), (last, 2)] + [(k, 3) for k in range(outer_size)]
    while rest:
        moves, taken = [], set()
        for key in rest:
            ways = [("y", (key[0], key[1] ^ 2)), ("x", (key[0], key[1] ^ 1)), ("z", (key[0] - 1, key[1]))]
            if key == (last, 1):
                ways.reverse()
            if key[1] == 3:
                ways = ways[::-1] if (key[0] - 1, 3) in held else ways
            for link, source in ways:
                if source in held and link not in taken:
                    taken.add(link)
                    moves.append((key, source))
                    break
        held.update(key for key, _ in moves)
        rest = [key for key in rest if key not in held]
        rounds.append(moves)
    return rounds


def shards(embeddings, rotation, codes, codebooks):
    tok_rows, model_width = embeddings.shape
    dp, col = lax.axis_size("dp"), lax.axis_size("col")
    rows_total = tok_rows * dp
    block = model_width // dp
    inner_size = math.gcd(dp, INNER)
    outer_size = dp // inner_size
    wide = model_width // outer_size
    part_rows = tok_rows // col
    outer, inner = lax.axis_index("dp") // inner_size, lax.axis_index("dp") % inner_size
    core = lax.axis_index("col")

    def from_outer(value, step):
        pairs = [(i, (i // inner_size ^ step) * inner_size + i % inner_size) for i in range(dp)]
        return lax.ppermute(value, "dp", pairs)

    def from_inner(value, step):
        pairs = [(i, i // inner_size * inner_size + (i % inner_size ^ step)) for i in range(dp)]
        return lax.ppermute(value, "dp", pairs)

    steps = list(range(1, outer_size))
    codes_t = codes.T.astype(jnp.bfloat16)
    group_codes = [codes_t] + [from_outer(codes_t, step) for step in steps]

    table = jnp.transpose(codebooks, (0, 2, 1)).astype(jnp.float32)
    own = rebuild_rows(codes_t[None], table)
    rotated = lax.dot_general(
        rotation, embeddings, (((0,), (1,)), ((), ())), preferred_element_type=jnp.float32
    )
    residue = rotated - own.astype(jnp.float32)
    row_error = lax.psum(jnp.sum(residue * residue, axis=0), "col")
    weights = 1.0 / (1.0 + row_error / (2.0 * model_width))

    place = jnp.stack([core, inner, outer]).astype(jnp.int32)
    weights, group_codes = lax.optimization_barrier((weights, group_codes))
    local, *sends = weighted_slices(place, weights, embeddings, part_rows, wide, steps)
    shares = [from_outer(send, step) for send, step in zip(sends, steps)]
    rebuilt = rebuild_rows(jnp.stack(group_codes), table)
    shares, rebuilt = lax.optimization_barrier((shares, rebuilt))
    pieces = []
    for share in shares:
        if part_rows % LANES:
            pieces.append(lax.all_gather(share, "col", axis=0, tiled=True))
            continue
        pieces.append(share)
        for turn in range(1, col):
            pairs = [(i, (i - turn) % col) for i in range(col)]
            pieces.append(lax.ppermute(share, "col", pairs))

    start_row = lax.axis_index("dp") * block
    prior = lax.dynamic_slice_in_dim(rotation, start_row, block, 0).T
    prior = 0.2 * rows_total * prior.astype(jnp.float32)
    half = prior.shape[0] // 2
    blocks_for = functools.partial(
        cross_blocks, place=place, rebuilt=rebuilt, prior=prior, local=local, pieces=pieces
    )
    near = [(1, 2), (2, 1)]
    sent = blocks_for([((one, 3), side * half) for side, (one, _) in enumerate(near)], jnp.bfloat16)
    came = [from_inner(value, one) for value, (one, _) in zip(sent, near)]
    kept = blocks_for(
        [((0,), side * half) for side in range(2)]
        + [((two,), side * half) for side, (_, two) in enumerate(near)],
        jnp.float32,
    )
    starts = []
    for side, (_, two) in enumerate(near):
        passed = kept[2 + side] + came[side][half:].astype(jnp.float32)
        last = from_inner(passed.astype(jnp.bfloat16), two)
        starts.append(kept[side] + came[side][:half].astype(jnp.float32) + last.astype(jnp.float32))
    narrow = [value.astype(jnp.bfloat16) for value in starts]
    start = jnp.concatenate(starts, axis=0).T

    def ring(value):
        pairs = [(i, (i + inner_size) % dp) for i in range(dp)]
        return lax.ppermute(value, "dp", pairs)

    own = start.astype(jnp.bfloat16)
    held = [{(0, 0): value} for value in narrow]

    def move(side, key, source):
        value = held[side][source]
        return ring(value) if key[0] != source[0] else from_inner(value, key[1] ^ source[1])

    def halves(keys):
        return [held[side][key] for key in keys for side in range(2)]

    order, products = [(0, 0)], []
    square = jnp.zeros((8, block), jnp.float32)
    fresh = [(0, 0)]
    rounds = gather_rounds(outer_size)
    for moves in rounds:
        arrived = [[move(side, key, source) for key, source in moves] for side in range(2)]
        product, square = apply_first(own, square, halves(fresh))
        arrived[0], product, square = lax.optimization_barrier((arrived[0], product, square))
        beside = [products[-1]] if products else []
        if moves is rounds[-1]:
            beside = [apply_early(halves(order[: -len(fresh)]), products)]
        arrived[1], beside = lax.optimization_barrier((arrived[1], beside))
        if moves is rounds[-1]:
            early = beside[0]
        elif products:
            products[-1] = beside[0]
        fresh = [key for key, _ in moves]
        for side in range(2):
            held[side].update(zip(fresh, arrived[side]))
        order += fresh
        products.append(both_cores(product))
    product, square = apply_first(own, square, halves(fresh))
    products.append(both_cores(product))
    panel = halves(order)
    squares = both_cores(square)

    inner = products[-2:]
    states = [start]
    middle = len(panel) // 2
    for step in range(3):
        state, value, product = apply_late(step, early, panel, inner, squares, states[-1:])
        states.append(state)
        product = both_cores(product)
        inner = [both_cores(apply_rest(value, panel[middle:]))]
        early = apply_early(panel[:middle], [product])
    return apply_late(3, early, panel, inner, squares, [states[3], states[1]])


def solution(mesh):
    placed = (P("dp", None), P(None, "col"), P("dp", "col"), P("col", None, None))
    return jax.shard_map(
        shards, mesh=mesh, in_specs=placed, out_specs=P("dp", "col"), check_vma=False
    )
```

```python
import functools
import math

import jax
import jax.numpy as jnp
from jax import lax
from jax.experimental import pallas as pl
from jax.experimental.pallas import tpu as pltpu
from jax.sharding import PartitionSpec as P

LANES = 128
GROUP = 8
CHUNKS = 4
INNER = 4
VMEM_BYTES = 24 * 1024 * 1024
ANY = pl.BlockSpec(memory_space=pl.ANY)
VMEM = pl.BlockSpec(memory_space=pltpu.VMEM)


def lookup_kernel(codes_ref, table_ref, out_ref, ids_ref):
    subs, rows = codes_ref.shape[1:]
    width = table_ref.shape[1]
    halves = table_ref.shape[2] // LANES
    first_out = pl.program_id(0) * (subs * width)
    ids_ref[...] = codes_ref[0].astype(jnp.float32).astype(jnp.int32)

    def body(step, carry):
        base = pl.multiple_of(step * GROUP, GROUP)
        for first in range(0, rows, LANES):
            lanes = pl.ds(pl.multiple_of(pl.program_id(1) * rows + first, LANES), LANES)
            ids_all = ids_ref[pl.ds(base, GROUP), first : first + LANES]
            for pair in range(0, GROUP, 2):
                both = []
                for sub in (pair, pair + 1):
                    ids = jnp.broadcast_to(ids_all[sub : sub + 1], (width, LANES))
                    lane = jnp.bitwise_and(ids, LANES - 1)
                    picked = None
                    for half in range(halves):
                        entries = table_ref[base + sub, :, half * LANES : (half + 1) * LANES]
                        got = jnp.take_along_axis(
                            entries, lane, axis=1, mode="promise_in_bounds"
                        )
                        picked = got if half == 0 else jnp.where(ids >= half * LANES, got, picked)
                    both.append(picked)
                row = pl.multiple_of(first_out + (base + pair) * width, 2 * width)
                out_ref[pl.ds(row, 2 * width), lanes] = jnp.concatenate(both, axis=0).astype(
                    out_ref.dtype
                )
        return carry

    lax.fori_loop(0, subs // GROUP, body, 0)


def rebuild_rows(codes, table):
    blocks, subs, rows = codes.shape
    width, centroids = table.shape[1:]
    tile = min(64, subs)
    return pl.pallas_call(
        lookup_kernel,
        grid=(subs // tile, blocks),
        in_specs=[
            pl.BlockSpec((1, tile, rows), lambda m, s: (s, m, 0)),
            pl.BlockSpec((tile, width, centroids), lambda m, s: (m, 0, 0)),
        ],
        out_specs=VMEM,
        scratch_shapes=[pltpu.VMEM((tile, rows), jnp.int32)],
        out_shape=pltpu.VMEM((subs * width, blocks * rows), jnp.bfloat16),
        compiler_params=pltpu.CompilerParams(vmem_limit_bytes=VMEM_BYTES),
        name="lookup",
    )(codes, table)


def slices_kernel(steps, streams, inner_size, place_ref, weights_ref, rows_ref, *outs):
    width = outs[0].shape[1] // inner_size
    wide = width * streams * inner_size
    rows, part_rows = outs[0].shape[0], outs[-1].shape[0]

    def scaled(first, step, stream):
        base = lax.bitwise_xor(place_ref[2], step) * wide + stream * width
        column = jnp.broadcast_to(weights_ref[:, pl.ds(first, part_rows)], (LANES, part_rows)).T
        for index in range(inner_size):
            lanes = pl.ds(pl.multiple_of(base + index * width * streams, LANES), width)
            values = rows_ref[pl.ds(first, part_rows), lanes].astype(jnp.float32)
            yield slice(index * width, (index + 1) * width), (values * column).astype(outs[0].dtype)

    for index, out_ref in enumerate(outs):
        stream, slot = divmod(index, 1 + len(steps))
        if slot:
            first = pl.multiple_of(place_ref[0] * part_rows, part_rows)
            for span, values in scaled(first, steps[slot - 1], stream):
                out_ref[:, span] = values
        else:
            for first in range(0, rows, part_rows):
                for span, values in scaled(first, 0, stream):
                    out_ref[first : first + part_rows, span] = values


def weighted_slices(place, weights, embeddings, part_rows, steps, streams, inner_size, wide):
    rows = embeddings.shape[0]
    count = 1 + len(steps)
    if part_rows % LANES or wide // streams // inner_size != LANES:
        scaled = (weights[:, None] * embeddings.astype(jnp.float32)).astype(jnp.bfloat16)
        parts = [lax.dynamic_slice_in_dim(scaled, place[2] * wide, wide, 1)]
        for step in steps:
            start = (place[0] * part_rows, (place[2] ^ step) * wide)
            parts.append(lax.dynamic_slice(scaled, start, (part_rows, wide)))
        split = [part.reshape(part.shape[0], inner_size, streams, -1) for part in parts]
        return [
            [part[:, :, stream].reshape(part.shape[0], -1) for part in split]
            for stream in range(streams)
        ]
    shapes = [(rows, wide // streams)] + [(part_rows, wide // streams)] * len(steps)
    outs = pl.pallas_call(
        functools.partial(slices_kernel, steps, streams, inner_size),
        in_specs=[pl.BlockSpec(memory_space=pltpu.SMEM), VMEM, VMEM],
        out_specs=[VMEM] * (count * streams),
        out_shape=[pltpu.VMEM(shape, jnp.bfloat16) for shape in shapes] * streams,
        compiler_params=pltpu.CompilerParams(vmem_limit_bytes=VMEM_BYTES),
        name="slices",
    )(place, *in_vmem(weights[None, :], embeddings))
    return [list(outs[first : first + count]) for first in range(0, count * streams, count)]


def cross_kernel(plan, place_ref, own_ref, rebuilt_ref, prior_ref, local_ref, *refs):
    pieces, outs = refs[: len(refs) - len(plan)], refs[len(refs) - len(plan) :]
    rows = local_ref.shape[0]
    part_rows, col = (pieces[0].shape[0], rows // pieces[0].shape[0]) if pieces else (rows, 1)
    for (targets, first_row), out_ref in zip(plan, outs):
        span = slice(first_row, first_row + out_ref.shape[0])
        width = out_ref.shape[1] // len(targets)
        left = [own_ref[span, :]]
        for index in range(len(pieces)):
            step, turn = divmod(index, col)
            first = step * rows + lax.rem(place_ref[0] + turn, col) * part_rows
            left.append(rebuilt_ref[span, pl.ds(pl.multiple_of(first, part_rows), part_rows)])
        right = []
        for target in targets:
            place = lax.bitwise_xor(place_ref[1], target)
            lanes = pl.ds(pl.multiple_of(place * width, width), width)
            right.append(
                jnp.concatenate([part[:, lanes] for part in (local_ref, *pieces)], axis=0)
            )
        total = jnp.dot(
            jnp.concatenate(left, axis=1), jnp.concatenate(right, axis=1),
            preferred_element_type=jnp.float32,
        )
        if targets[0] == 0:
            out_ref[:, :width] = (total[:, :width] + prior_ref[span, :]).astype(out_ref.dtype)
            out_ref[:, width:] = total[:, width:].astype(out_ref.dtype)
        else:
            out_ref[...] = total.astype(out_ref.dtype)


def cross_blocks(plan, dtype, place, own, rebuilt, prior, local, pieces):
    operands = in_vmem(own, rebuilt, prior, local, *pieces)
    half, width = prior.shape[0] // 2, prior.shape[1]
    return pl.pallas_call(
        functools.partial(cross_kernel, plan),
        in_specs=[pl.BlockSpec(memory_space=pltpu.SMEM)] + [VMEM] * len(operands),
        out_specs=[VMEM] * len(plan),
        out_shape=[pltpu.VMEM((half, len(targets) * width), dtype) for targets, _ in plan],
        compiler_params=pltpu.CompilerParams(vmem_limit_bytes=VMEM_BYTES),
        name="cross",
    )(place, *operands)


def product_of(value_ref, pieces, inner_ref, index):
    block_values = jnp.concatenate([piece_ref[...] for piece_ref in pieces], axis=1)
    block = block_values.shape[1]
    product = jnp.dot(value_ref[...], block_values, preferred_element_type=jnp.float32)
    inner_ref[index * block : (index + 1) * block, :] = product.T.astype(inner_ref.dtype)


def first_kernel(streams, own_ref, before_ref, *refs):
    panel, (inner_ref, square_ref) = refs[:-2], refs[-2:]
    cols, width = panel[0].shape
    square = before_ref[...]
    for index in range(len(panel) // streams):
        pieces = panel[streams * index : streams * (index + 1)]
        product_of(own_ref, pieces, inner_ref, index)
        for piece_ref in pieces:
            values = piece_ref[...].astype(jnp.float32)
            square += jnp.sum((values * values).reshape(cols // 8, 8, width), axis=0)
    square_ref[...] = square


def add_up(mine, other, sum_ref):
    first = 0
    for mine_ref, other_ref in zip(mine, other):
        sum_ref[first : first + mine_ref.shape[0], :] = mine_ref[...] + other_ref[...]
        first += mine_ref.shape[0]


def gram_rows(panel, sum_ref, index):
    chunk = panel[0].shape[0] // CHUNKS
    span = slice(index * chunk, (index + 1) * chunk)
    rows = jnp.concatenate([piece_ref[span, :] for piece_ref in panel], axis=1)
    return span, jnp.dot(rows, sum_ref[...], preferred_element_type=jnp.float32)


def early_kernel(count, parts, *refs):
    panel, refs = refs[:count], refs[count:]
    mine, other, (out_ref, sum_ref) = refs[:parts], refs[parts : 2 * parts], refs[2 * parts :]
    add_up(mine, other, sum_ref)
    for index in range(CHUNKS):
        span, made = gram_rows(panel, sum_ref, index)
        out_ref[span, :] = made


def late_kernel(step, streams, counts, parts, mine_square_ref, other_square_ref, *refs):
    last = step == 3
    states = 2 if last else 1
    first_late, late = counts
    panel, refs = refs[: first_late + late], refs[first_late + late :]
    mine, other, refs = refs[:parts], refs[parts : 2 * parts], refs[2 * parts :]
    early_ref, held, refs = refs[0], refs[1 : 1 + states], refs[1 + states :]
    if last:
        out_ref, sum_ref = refs
    else:
        state_ref, value_ref, inner_ref, sum_ref = refs
    width = panel[0].shape[1]
    model_width = len(panel) * width
    total = jnp.sum(mine_square_ref[...] + other_square_ref[...], axis=(0, 1), keepdims=True)
    scale = model_width / (1.96 * total)
    add_up(mine, other, sum_ref)
    for index in range(CHUNKS):
        span, made = gram_rows(panel[first_late:], sum_ref, index)
        made += early_ref[span, :]
        if step == 2:
            made = made * scale
        else:
            made = 1.5 * held[0][span, :] - (0.5 * scale) * made
        if last:
            made = (1.5 * held[1][span, :] - 0.5 * made) * (math.sqrt(model_width) * jnp.sqrt(scale))
            out_ref[:, span] = made.T
        else:
            state_ref[span, :] = made
            value_ref[:, span] = made.T.astype(value_ref.dtype)
    if last:
        return
    for index in range(inner_ref.shape[0] // (streams * width)):
        product_of(value_ref, panel[streams * index : streams * (index + 1)], inner_ref, index)


def rest_kernel(streams, value_ref, *refs):
    panel, inner_ref = refs[:-1], refs[-1]
    for index in range(len(panel) // streams):
        product_of(value_ref, panel[streams * index : streams * (index + 1)], inner_ref, index)


def in_vmem(*values):
    return [pltpu.with_memory_space_constraint(value, pltpu.VMEM) for value in values]


def apply_first(own, square, panel):
    block = own.shape[0]
    streams = block // panel[0].shape[1]
    return pl.pallas_call(
        functools.partial(first_kernel, streams),
        in_specs=[VMEM] * (2 + len(panel)),
        out_specs=[VMEM, VMEM],
        out_shape=[
            pltpu.VMEM((len(panel) // streams * block, block), jnp.bfloat16),
            pltpu.VMEM(square.shape, jnp.float32),
        ],
        compiler_params=pltpu.CompilerParams(vmem_limit_bytes=VMEM_BYTES),
        name="first",
    )(*in_vmem(own, square, *panel))


def apply_early(panel, inner):
    cols, width = panel[0].shape
    mine, other = zip(*inner)
    operands = in_vmem(*panel, *mine, *other)
    return pl.pallas_call(
        functools.partial(early_kernel, len(panel), len(inner)),
        in_specs=[VMEM] * len(operands),
        out_specs=VMEM,
        out_shape=pltpu.VMEM((cols, mine[0].shape[1]), jnp.float32),
        scratch_shapes=[pltpu.VMEM((len(panel) * width, mine[0].shape[1]), jnp.bfloat16)],
        compiler_params=pltpu.CompilerParams(vmem_limit_bytes=VMEM_BYTES),
        name="early",
    )(*operands)


def apply_late(step, early, panel, inner, squares, held):
    mine, other = zip(*inner)
    cols, width = panel[0].shape
    block = mine[0].shape[1]
    late = sum(part.shape[0] for part in mine) // width
    last = step == 3
    if last:
        out_shape = jax.ShapeDtypeStruct((block, cols), jnp.float32)
    else:
        out_shape = [
            pltpu.VMEM((cols, block), jnp.float32),
            pltpu.VMEM((block, cols), jnp.bfloat16),
            pltpu.VMEM((len(panel) // 2 * width, block), jnp.bfloat16),
        ]
    operands = in_vmem(*squares, *panel, *mine, *other, early, *held)
    return pl.pallas_call(
        functools.partial(late_kernel, step, block // width, (len(panel) - late, late), len(inner)),
        in_specs=[VMEM] * len(operands),
        out_specs=VMEM if last else [VMEM] * 3,
        out_shape=out_shape,
        scratch_shapes=[pltpu.VMEM((late * width, block), jnp.bfloat16)],
        compiler_params=pltpu.CompilerParams(vmem_limit_bytes=VMEM_BYTES),
        name="late%d" % step,
    )(*operands)


def apply_rest(value, panel):
    block = value.shape[0]
    width = panel[0].shape[1]
    operands = in_vmem(value, *panel)
    return pl.pallas_call(
        functools.partial(rest_kernel, block // width),
        in_specs=[VMEM] * len(operands),
        out_specs=VMEM,
        out_shape=pltpu.VMEM((len(panel) * width, block), jnp.bfloat16),
        compiler_params=pltpu.CompilerParams(vmem_limit_bytes=VMEM_BYTES),
        name="rest",
    )(*operands)


def swap_cores(value):
    return lax.ppermute(value, "col", [(0, 1), (1, 0)])


def both_cores(value):
    if lax.axis_size("col") == 2:
        return value, swap_cores(value)
    total = lax.psum(value.astype(jnp.float32), "col").astype(value.dtype)
    return total, jnp.zeros_like(total)


def gather_rounds(outer_size):
    held = {(0, 0)}
    last = outer_size - 1
    rounds = []
    for k in range(1, outer_size):
        rounds.append([((k, 0), (k - 1, 0)), ((k - 1, 1), (k - 1, 0)), ((k - 1, 2), (k - 1, 0))])
    held.update(key for moves in rounds for key, _ in moves)
    rest = [(last, 1), (last, 2)] + [(k, 3) for k in range(outer_size)]
    while rest:
        moves, taken = [], set()
        for key in rest:
            ways = [("y", (key[0], key[1] ^ 2)), ("x", (key[0], key[1] ^ 1)), ("z", (key[0] - 1, key[1]))]
            if key == (last, 1):
                ways.reverse()
            if key[1] == 3:
                ways = ways[::-1] if (key[0] - 1, 3) in held else ways
            for link, source in ways:
                if source in held and link not in taken:
                    taken.add(link)
                    moves.append((key, source))
                    break
        held.update(key for key, _ in moves)
        rest = [key for key in rest if key not in held]
        rounds.append(moves)
    return rounds


def shards(embeddings, rotation, codes, codebooks):
    tok_rows, model_width = embeddings.shape
    dp, col = lax.axis_size("dp"), lax.axis_size("col")
    rows_total = tok_rows * dp
    block = model_width // dp
    inner_size = math.gcd(dp, INNER)
    outer_size = dp // inner_size
    wide = model_width // outer_size
    part_rows = tok_rows // col
    outer, inner = lax.axis_index("dp") // inner_size, lax.axis_index("dp") % inner_size
    core = lax.axis_index("col")

    def from_outer(value, step):
        pairs = [(i, (i // inner_size ^ step) * inner_size + i % inner_size) for i in range(dp)]
        return lax.ppermute(value, "dp", pairs)

    def from_inner(value, step):
        pairs = [(i, i // inner_size * inner_size + (i % inner_size ^ step)) for i in range(dp)]
        return lax.ppermute(value, "dp", pairs)

    steps = list(range(1, outer_size))
    codes_t = codes.T.astype(jnp.bfloat16)
    group_codes = [from_outer(codes_t, step) for step in steps]

    table = jnp.transpose(codebooks, (0, 2, 1)).astype(jnp.float32)
    own = rebuild_rows(codes_t[None], table)
    rotated = lax.dot_general(
        rotation, embeddings, (((0,), (1,)), ((), ())), preferred_element_type=jnp.float32
    )
    residue = rotated - own.astype(jnp.float32)
    row_error = lax.psum(jnp.sum(residue * residue, axis=0), "col")
    weights = 1.0 / (1.0 + row_error / (2.0 * model_width))
    weights, group_codes = lax.optimization_barrier((weights, group_codes))

    streams = 2 if block % (2 * LANES) == 0 else 1
    width = block // streams
    place = jnp.stack([core, inner, outer]).astype(jnp.int32)
    slices = weighted_slices(
        place, weights, embeddings, part_rows, steps, streams, inner_size, wide
    )
    rebuilt = rebuild_rows(jnp.stack(group_codes), table)
    start_row = lax.axis_index("dp") * block
    prior = lax.dynamic_slice_in_dim(rotation, start_row, block, 0).T
    prior = 0.2 * rows_total * prior.astype(jnp.float32)
    half = prior.shape[0] // 2
    near = [(1, 2), (2, 1)]
    fetched, shares = [], []
    for stream, (_, *sends) in enumerate(slices):
        if stream:
            sends, rebuilt, shares = lax.optimization_barrier((sends, rebuilt, shares))
            fetched.append(shares)
        shares = [from_outer(send, step) for send, step in zip(sends, steps)]
    fetched.append(shares)
    starts, narrow = [], []
    for stream in range(streams):
        pieces = []
        for share in fetched[stream]:
            if part_rows % LANES:
                pieces.append(lax.all_gather(share, "col", axis=0, tiled=True))
                continue
            pieces.append(share)
            for turn in range(1, col):
                pairs = [(i, (i - turn) % col) for i in range(col)]
                pieces.append(lax.ppermute(share, "col", pairs))
        if stream:
            pieces, narrow = lax.optimization_barrier((pieces, narrow))
        blocks_for = functools.partial(
            cross_blocks,
            place=place,
            own=own,
            rebuilt=rebuilt,
            prior=prior[:, stream * width : (stream + 1) * width],
            local=slices[stream][0],
            pieces=pieces,
        )
        sent = blocks_for([((one, 3), side * half) for side, (one, _) in enumerate(near)], jnp.bfloat16)
        came = [from_inner(value, one) for value, (one, _) in zip(sent, near)]
        kept = blocks_for([((0, two), side * half) for side, (_, two) in enumerate(near)], jnp.float32)
        if stream + 1 < streams:
            fetched[stream + 1], came = lax.optimization_barrier((fetched[stream + 1], came))
        sums = []
        for side, (_, two) in enumerate(near):
            total = kept[side] + came[side].astype(jnp.float32)
            last = from_inner(total[:, width:].astype(jnp.bfloat16), two)
            sums.append(total[:, :width] + last.astype(jnp.float32))
        starts.append(jnp.concatenate(sums, axis=0))
        narrow.append(starts[-1].astype(jnp.bfloat16))
    start = jnp.concatenate(starts, axis=1)

    def ring(value):
        pairs = [(i, (i + inner_size) % dp) for i in range(dp)]
        return lax.ppermute(value, "dp", pairs)

    own = jnp.concatenate(narrow, axis=1).T
    held = [{(0, 0): value} for value in narrow]

    def move(stream, key, source):
        value = held[stream][source]
        return ring(value) if key[0] != source[0] else from_inner(value, key[1] ^ source[1])

    def pieces_of(keys):
        return [held[stream][key] for key in keys for stream in range(streams)]

    order, products = [(0, 0)], []
    square = jnp.zeros((8, width), jnp.float32)
    fresh = [(0, 0)]
    for moves in gather_rounds(outer_size):
        arrived = [
            [move(stream, key, source) for key, source in moves] for stream in range(streams)
        ]
        product, square = apply_first(own, square, pieces_of(fresh))
        for stream in range(streams - 1):
            arrived[stream] = lax.optimization_barrier(arrived[stream])
        arrived[-1], product, square = lax.optimization_barrier((arrived[-1], product, square))
        fresh = [key for key, _ in moves]
        for stream in range(streams):
            held[stream].update(zip(fresh, arrived[stream]))
        order += fresh
        products.append(both_cores(product))
    product, square = apply_first(own, square, pieces_of(fresh))
    products.append(both_cores(product))
    panel = pieces_of(order)
    squares = both_cores(square)

    first_late = sum(mine.shape[0] for mine, _ in products[:-2]) // width
    early = apply_early(panel[:first_late], products[:-2])
    inner = products[-2:]
    states = [start]
    middle = len(panel) // 2
    for step in range(3):
        state, value, product = apply_late(step, early, panel, inner, squares, states[-1:])
        states.append(state)
        product = both_cores(product)
        inner = [both_cores(apply_rest(value, panel[middle:]))]
        early = apply_early(panel[:middle], [product])
    return apply_late(3, early, panel, inner, squares, [states[3], states[1]])


def solution(mesh):
    placed = (P("dp", None), P(None, "col"), P("dp", "col"), P("col", None, None))
    return jax.shard_map(
        shards, mesh=mesh, in_specs=placed, out_specs=P("dp", "col"), check_vma=False
    )
```

```python
import functools
import math

import jax
import jax.numpy as jnp
from jax import lax
from jax.experimental import pallas as pl
from jax.experimental.pallas import tpu as pltpu
from jax.sharding import PartitionSpec as P

LANES = 128
GROUP = 8
CHUNKS = 4
INNER = 4
VMEM_BYTES = 24 * 1024 * 1024
ANY = pl.BlockSpec(memory_space=pl.ANY)
VMEM = pl.BlockSpec(memory_space=pltpu.VMEM)


def lookup_kernel(codes_ref, table_ref, out_ref, ids_ref):
    subs, rows = codes_ref.shape[1:]
    width = table_ref.shape[1]
    halves = table_ref.shape[2] // LANES
    first_out = pl.program_id(0) * (subs * width)
    ids_ref[...] = codes_ref[0].astype(jnp.float32).astype(jnp.int32)

    def body(step, carry):
        base = pl.multiple_of(step * GROUP, GROUP)
        for first in range(0, rows, LANES):
            lanes = pl.ds(pl.multiple_of(pl.program_id(1) * rows + first, LANES), LANES)
            ids_all = ids_ref[pl.ds(base, GROUP), first : first + LANES]
            for pair in range(0, GROUP, 2):
                both = []
                for sub in (pair, pair + 1):
                    ids = jnp.broadcast_to(ids_all[sub : sub + 1], (width, LANES))
                    lane = jnp.bitwise_and(ids, LANES - 1)
                    picked = None
                    for half in range(halves):
                        entries = table_ref[base + sub, :, half * LANES : (half + 1) * LANES]
                        got = jnp.take_along_axis(
                            entries, lane, axis=1, mode="promise_in_bounds"
                        )
                        picked = got if half == 0 else jnp.where(ids >= half * LANES, got, picked)
                    both.append(picked)
                row = pl.multiple_of(first_out + (base + pair) * width, 2 * width)
                out_ref[pl.ds(row, 2 * width), lanes] = jnp.concatenate(both, axis=0).astype(
                    out_ref.dtype
                )
        return carry

    lax.fori_loop(0, subs // GROUP, body, 0)


def rebuild_rows(codes, table):
    blocks, subs, rows = codes.shape
    width, centroids = table.shape[1:]
    tile = min(64, subs)
    return pl.pallas_call(
        lookup_kernel,
        grid=(subs // tile, blocks),
        in_specs=[
            pl.BlockSpec((1, tile, rows), lambda m, s: (s, m, 0)),
            pl.BlockSpec((tile, width, centroids), lambda m, s: (m, 0, 0)),
        ],
        out_specs=VMEM,
        scratch_shapes=[pltpu.VMEM((tile, rows), jnp.int32)],
        out_shape=pltpu.VMEM((subs * width, blocks * rows), jnp.bfloat16),
        compiler_params=pltpu.CompilerParams(vmem_limit_bytes=VMEM_BYTES),
        name="lookup",
    )(codes, table)


def slices_kernel(steps, streams, inner_size, place_ref, weights_ref, rows_ref, *outs):
    width = outs[0].shape[1] // inner_size
    wide = width * streams * inner_size
    rows, part_rows = outs[0].shape[0], outs[-1].shape[0]

    def scaled(first, step, stream):
        base = lax.bitwise_xor(place_ref[2], step) * wide + stream * width
        column = jnp.broadcast_to(weights_ref[:, pl.ds(first, part_rows)], (LANES, part_rows)).T
        for index in range(inner_size):
            lanes = pl.ds(pl.multiple_of(base + index * width * streams, LANES), width)
            values = rows_ref[pl.ds(first, part_rows), lanes].astype(jnp.float32)
            yield slice(index * width, (index + 1) * width), (values * column).astype(outs[0].dtype)

    for index, out_ref in enumerate(outs):
        stream, slot = divmod(index, 1 + len(steps))
        if slot:
            first = pl.multiple_of(place_ref[0] * part_rows, part_rows)
            for span, values in scaled(first, steps[slot - 1], stream):
                out_ref[:, span] = values
        else:
            for first in range(0, rows, part_rows):
                for span, values in scaled(first, 0, stream):
                    out_ref[first : first + part_rows, span] = values


def weighted_slices(place, weights, embeddings, part_rows, steps, streams, inner_size, wide):
    rows = embeddings.shape[0]
    count = 1 + len(steps)
    if part_rows % LANES or wide // streams // inner_size != LANES:
        scaled = (weights[:, None] * embeddings.astype(jnp.float32)).astype(jnp.bfloat16)
        parts = [lax.dynamic_slice_in_dim(scaled, place[2] * wide, wide, 1)]
        for step in steps:
            start = (place[0] * part_rows, (place[2] ^ step) * wide)
            parts.append(lax.dynamic_slice(scaled, start, (part_rows, wide)))
        split = [part.reshape(part.shape[0], inner_size, streams, -1) for part in parts]
        return [
            [part[:, :, stream].reshape(part.shape[0], -1) for part in split]
            for stream in range(streams)
        ]
    shapes = [(rows, wide // streams)] + [(part_rows, wide // streams)] * len(steps)
    outs = pl.pallas_call(
        functools.partial(slices_kernel, steps, streams, inner_size),
        in_specs=[pl.BlockSpec(memory_space=pltpu.SMEM), VMEM, VMEM],
        out_specs=[VMEM] * (count * streams),
        out_shape=[pltpu.VMEM(shape, jnp.bfloat16) for shape in shapes] * streams,
        compiler_params=pltpu.CompilerParams(vmem_limit_bytes=VMEM_BYTES),
        name="slices",
    )(place, *in_vmem(weights[None, :], embeddings))
    return [list(outs[first : first + count]) for first in range(0, count * streams, count)]


def cross_kernel(plan, place_ref, own_ref, rebuilt_ref, prior_ref, local_ref, *refs):
    pieces, outs = refs[: len(refs) - len(plan)], refs[len(refs) - len(plan) :]
    rows = local_ref.shape[0]
    part_rows, col = (pieces[0].shape[0], rows // pieces[0].shape[0]) if pieces else (rows, 1)
    for (targets, first_row), out_ref in zip(plan, outs):
        span = slice(first_row, first_row + out_ref.shape[0])
        width = out_ref.shape[1] // len(targets)
        left = [own_ref[span, :]]
        for index in range(len(pieces)):
            step, turn = divmod(index, col)
            first = step * rows + lax.rem(place_ref[0] + turn, col) * part_rows
            left.append(rebuilt_ref[span, pl.ds(pl.multiple_of(first, part_rows), part_rows)])
        right = []
        for target in targets:
            place = lax.bitwise_xor(place_ref[1], target)
            lanes = pl.ds(pl.multiple_of(place * width, width), width)
            right.append(
                jnp.concatenate([part[:, lanes] for part in (local_ref, *pieces)], axis=0)
            )
        total = jnp.dot(
            jnp.concatenate(left, axis=1), jnp.concatenate(right, axis=1),
            preferred_element_type=jnp.float32,
        )
        if targets[0] == 0:
            out_ref[:, :width] = (total[:, :width] + prior_ref[span, :]).astype(out_ref.dtype)
            out_ref[:, width:] = total[:, width:].astype(out_ref.dtype)
        else:
            out_ref[...] = total.astype(out_ref.dtype)


def cross_blocks(plan, dtype, place, own, rebuilt, prior, local, pieces):
    operands = in_vmem(own, rebuilt, prior, local, *pieces)
    half, width = prior.shape[0] // 2, prior.shape[1]
    return pl.pallas_call(
        functools.partial(cross_kernel, plan),
        in_specs=[pl.BlockSpec(memory_space=pltpu.SMEM)] + [VMEM] * len(operands),
        out_specs=[VMEM] * len(plan),
        out_shape=[pltpu.VMEM((half, len(targets) * width), dtype) for targets, _ in plan],
        compiler_params=pltpu.CompilerParams(vmem_limit_bytes=VMEM_BYTES),
        name="cross",
    )(place, *operands)


def product_of(value_ref, pieces, inner_ref, index):
    block_values = jnp.concatenate([piece_ref[...] for piece_ref in pieces], axis=1)
    block = block_values.shape[1]
    product = jnp.dot(value_ref[...], block_values, preferred_element_type=jnp.float32)
    inner_ref[index * block : (index + 1) * block, :] = product.T.astype(inner_ref.dtype)


def first_kernel(streams, own_ref, before_ref, *refs):
    panel, (inner_ref, square_ref) = refs[:-2], refs[-2:]
    cols, width = panel[0].shape
    square = before_ref[...]
    for index in range(len(panel) // streams):
        pieces = panel[streams * index : streams * (index + 1)]
        product_of(own_ref, pieces, inner_ref, index)
        for piece_ref in pieces:
            values = piece_ref[...].astype(jnp.float32)
            square += jnp.sum((values * values).reshape(cols // 8, 8, width), axis=0)
    square_ref[...] = square


def add_up(mine, other, sum_ref):
    first = 0
    for mine_ref, other_ref in zip(mine, other):
        sum_ref[first : first + mine_ref.shape[0], :] = mine_ref[...] + other_ref[...]
        first += mine_ref.shape[0]


def gram_rows(panel, sum_ref, index):
    chunk = panel[0].shape[0] // CHUNKS
    span = slice(index * chunk, (index + 1) * chunk)
    rows = jnp.concatenate([piece_ref[span, :] for piece_ref in panel], axis=1)
    return span, jnp.dot(rows, sum_ref[...], preferred_element_type=jnp.float32)


def apply_kernel(step, streams, count, parts, mine_square_ref, other_square_ref, *refs):
    last = step == 3
    states = 2 if last else 1
    panel, refs = refs[:count], refs[count:]
    mine, other, refs = refs[:parts], refs[parts : 2 * parts], refs[2 * parts :]
    held, refs = refs[:states], refs[states:]
    if last:
        out_ref, sum_ref = refs
    else:
        state_ref, value_ref, inner_ref, sum_ref = refs
    width = panel[0].shape[1]
    model_width = count * width
    total = jnp.sum(mine_square_ref[...] + other_square_ref[...], axis=(0, 1), keepdims=True)
    scale = model_width / (1.96 * total)
    add_up(mine, other, sum_ref)
    for index in range(CHUNKS):
        span, made = gram_rows(panel, sum_ref, index)
        if step == 2:
            made = made * scale
        else:
            made = 1.5 * held[0][span, :] - (0.5 * scale) * made
        if last:
            made = (1.5 * held[1][span, :] - 0.5 * made) * (math.sqrt(model_width) * jnp.sqrt(scale))
            out_ref[:, span] = made.T
        else:
            state_ref[span, :] = made
            value_ref[:, span] = made.T.astype(value_ref.dtype)
    if last:
        return
    for index in range(inner_ref.shape[0] // (streams * width)):
        product_of(value_ref, panel[streams * index : streams * (index + 1)], inner_ref, index)


def rest_kernel(streams, value_ref, *refs):
    panel, inner_ref = refs[:-1], refs[-1]
    for index in range(len(panel) // streams):
        product_of(value_ref, panel[streams * index : streams * (index + 1)], inner_ref, index)


def in_vmem(*values):
    return [pltpu.with_memory_space_constraint(value, pltpu.VMEM) for value in values]


def apply_first(own, square, panel):
    block = own.shape[0]
    streams = block // panel[0].shape[1]
    return pl.pallas_call(
        functools.partial(first_kernel, streams),
        in_specs=[VMEM] * (2 + len(panel)),
        out_specs=[VMEM, VMEM],
        out_shape=[
            pltpu.VMEM((len(panel) // streams * block, block), jnp.bfloat16),
            pltpu.VMEM(square.shape, jnp.float32),
        ],
        compiler_params=pltpu.CompilerParams(vmem_limit_bytes=VMEM_BYTES),
        name="first",
    )(*in_vmem(own, square, *panel))


def apply_gram(step, panel, inner, squares, held):
    mine, other = zip(*inner)
    cols, width = panel[0].shape
    block = mine[0].shape[1]
    last = step == 3
    if last:
        out_shape = jax.ShapeDtypeStruct((block, cols), jnp.float32)
    else:
        out_shape = [
            pltpu.VMEM((cols, block), jnp.float32),
            pltpu.VMEM((block, cols), jnp.bfloat16),
            pltpu.VMEM((len(panel) // 2 * width, block), jnp.bfloat16),
        ]
    operands = in_vmem(*squares, *panel, *mine, *other, *held)
    return pl.pallas_call(
        functools.partial(apply_kernel, step, block // width, len(panel), len(inner)),
        in_specs=[VMEM] * len(operands),
        out_specs=VMEM if last else [VMEM] * 3,
        out_shape=out_shape,
        scratch_shapes=[pltpu.VMEM((len(panel) * width, block), jnp.bfloat16)],
        compiler_params=pltpu.CompilerParams(vmem_limit_bytes=VMEM_BYTES),
        name="apply%d" % step,
    )(*operands)


def apply_rest(value, panel):
    block = value.shape[0]
    width = panel[0].shape[1]
    operands = in_vmem(value, *panel)
    return pl.pallas_call(
        functools.partial(rest_kernel, block // width),
        in_specs=[VMEM] * len(operands),
        out_specs=VMEM,
        out_shape=pltpu.VMEM((len(panel) * width, block), jnp.bfloat16),
        compiler_params=pltpu.CompilerParams(vmem_limit_bytes=VMEM_BYTES),
        name="rest",
    )(*operands)


def swap_cores(value):
    return lax.ppermute(value, "col", [(0, 1), (1, 0)])


def both_cores(value):
    if lax.axis_size("col") == 2:
        return value, swap_cores(value)
    total = lax.psum(value.astype(jnp.float32), "col").astype(value.dtype)
    return total, jnp.zeros_like(total)


def gather_rounds(outer_size):
    held = {(0, 0)}
    last = outer_size - 1
    rounds = []
    for k in range(1, outer_size):
        rounds.append([((k, 0), (k - 1, 0)), ((k - 1, 1), (k - 1, 0)), ((k - 1, 2), (k - 1, 0))])
    held.update(key for moves in rounds for key, _ in moves)
    rest = [(last, 1), (last, 2)] + [(k, 3) for k in range(outer_size)]
    while rest:
        moves, taken = [], set()
        for key in rest:
            ways = [("y", (key[0], key[1] ^ 2)), ("x", (key[0], key[1] ^ 1)), ("z", (key[0] - 1, key[1]))]
            if key == (last, 1):
                ways.reverse()
            if key[1] == 3:
                ways = ways[::-1] if (key[0] - 1, 3) in held else ways
            for link, source in ways:
                if source in held and link not in taken:
                    taken.add(link)
                    moves.append((key, source))
                    break
        held.update(key for key, _ in moves)
        rest = [key for key in rest if key not in held]
        rounds.append(moves)
    return rounds


def shards(embeddings, rotation, codes, codebooks):
    tok_rows, model_width = embeddings.shape
    dp, col = lax.axis_size("dp"), lax.axis_size("col")
    rows_total = tok_rows * dp
    block = model_width // dp
    inner_size = math.gcd(dp, INNER)
    outer_size = dp // inner_size
    wide = model_width // outer_size
    part_rows = tok_rows // col
    outer, inner = lax.axis_index("dp") // inner_size, lax.axis_index("dp") % inner_size
    core = lax.axis_index("col")

    def from_outer(value, step):
        pairs = [(i, (i // inner_size ^ step) * inner_size + i % inner_size) for i in range(dp)]
        return lax.ppermute(value, "dp", pairs)

    def from_inner(value, step):
        pairs = [(i, i // inner_size * inner_size + (i % inner_size ^ step)) for i in range(dp)]
        return lax.ppermute(value, "dp", pairs)

    steps = list(range(1, outer_size))
    codes_t = codes.T.astype(jnp.bfloat16)
    group_codes = [from_outer(codes_t, step) for step in steps]

    table = jnp.transpose(codebooks, (0, 2, 1)).astype(jnp.float32)
    own = rebuild_rows(codes_t[None], table)
    rotated = lax.dot_general(
        rotation, embeddings, (((0,), (1,)), ((), ())), preferred_element_type=jnp.float32
    )
    residue = rotated - own.astype(jnp.float32)
    row_error = lax.psum(jnp.sum(residue * residue, axis=0), "col")
    weights = 1.0 / (1.0 + row_error / (2.0 * model_width))
    weights, group_codes = lax.optimization_barrier((weights, group_codes))

    streams = 2 if block % (2 * LANES) == 0 else 1
    width = block // streams
    place = jnp.stack([core, inner, outer]).astype(jnp.int32)
    slices = weighted_slices(
        place, weights, embeddings, part_rows, steps, streams, inner_size, wide
    )
    rebuilt = rebuild_rows(jnp.stack(group_codes), table)
    start_row, rebuilt = lax.optimization_barrier((lax.axis_index("dp") * block, rebuilt))
    prior = lax.dynamic_slice_in_dim(rotation, start_row, block, 0).T
    prior = 0.2 * rows_total * prior.astype(jnp.float32)
    half = prior.shape[0] // 2
    near = [(1, 2), (2, 1)]
    fetched, shares = [], []
    for stream, (_, *sends) in enumerate(slices):
        if stream:
            sends, rebuilt, shares = lax.optimization_barrier((sends, rebuilt, shares))
            fetched.append(shares)
        shares = [from_outer(send, step) for send, step in zip(sends, steps)]
    fetched.append(shares)
    starts, narrow = [], []
    for stream in range(streams):
        pieces = []
        for share in fetched[stream]:
            if part_rows % LANES:
                pieces.append(lax.all_gather(share, "col", axis=0, tiled=True))
                continue
            pieces.append(share)
            for turn in range(1, col):
                pairs = [(i, (i - turn) % col) for i in range(col)]
                pieces.append(lax.ppermute(share, "col", pairs))
        if stream:
            pieces, narrow = lax.optimization_barrier((pieces, narrow))
        blocks_for = functools.partial(
            cross_blocks,
            place=place,
            own=own,
            rebuilt=rebuilt,
            prior=prior[:, stream * width : (stream + 1) * width],
            local=slices[stream][0],
            pieces=pieces,
        )
        sent = blocks_for([((one, 3), side * half) for side, (one, _) in enumerate(near)], jnp.bfloat16)
        came = [from_inner(value, one) for value, (one, _) in zip(sent, near)]
        kept = blocks_for([((0, two), side * half) for side, (_, two) in enumerate(near)], jnp.float32)
        if stream + 1 < streams:
            fetched[stream + 1], came = lax.optimization_barrier((fetched[stream + 1], came))
        sums = []
        for side, (_, two) in enumerate(near):
            total = kept[side] + came[side].astype(jnp.float32)
            last = from_inner(total[:, width:].astype(jnp.bfloat16), two)
            sums.append(total[:, :width] + last.astype(jnp.float32))
        starts.append(jnp.concatenate(sums, axis=0))
        narrow.append(starts[-1].astype(jnp.bfloat16))
    start = jnp.concatenate(starts, axis=1)

    def ring(value):
        pairs = [(i, (i + inner_size) % dp) for i in range(dp)]
        return lax.ppermute(value, "dp", pairs)

    own = jnp.concatenate(narrow, axis=1).T
    held = [{(0, 0): value} for value in narrow]

    def move(stream, key, source):
        value = held[stream][source]
        return ring(value) if key[0] != source[0] else from_inner(value, key[1] ^ source[1])

    def pieces_of(keys):
        return [held[stream][key] for key in keys for stream in range(streams)]

    order, products = [(0, 0)], []
    square = jnp.zeros((8, width), jnp.float32)
    fresh = [(0, 0)]
    for moves in gather_rounds(outer_size):
        arrived = [
            [move(stream, key, source) for key, source in moves] for stream in range(streams)
        ]
        product, square = apply_first(own, square, pieces_of(fresh))
        for stream in range(streams - 1):
            arrived[stream] = lax.optimization_barrier(arrived[stream])
        arrived[-1], product, square = lax.optimization_barrier((arrived[-1], product, square))
        fresh = [key for key, _ in moves]
        for stream in range(streams):
            held[stream].update(zip(fresh, arrived[stream]))
        order += fresh
        products.append(both_cores(product))
    product, square = apply_first(own, square, pieces_of(fresh))
    products.append(both_cores(product))
    panel = pieces_of(order)
    squares = both_cores(square)

    states = [start]
    middle = len(panel) // 2
    for step in range(3):
        state, value, product = apply_gram(step, panel, products, squares, states[-1:])
        states.append(state)
        early, rest = lax.optimization_barrier(
            (both_cores(product), apply_rest(value, panel[middle:]))
        )
        products = [early, both_cores(rest)]
    return apply_gram(3, panel, products, squares, [states[3], states[1]])


def solution(mesh):
    placed = (P("dp", None), P(None, "col"), P("dp", "col"), P("col", None, None))
    return jax.shard_map(
        shards, mesh=mesh, in_specs=placed, out_specs=P("dp", "col"), check_vma=False
    )
```

```python
import functools
import math

import jax
import jax.numpy as jnp
from jax import lax
from jax.experimental import pallas as pl
from jax.experimental.pallas import tpu as pltpu
from jax.sharding import PartitionSpec as P

LANES = 128
GROUP = 8
CHUNKS = 4
INNER = 4
VMEM_BYTES = 24 * 1024 * 1024
ANY = pl.BlockSpec(memory_space=pl.ANY)
VMEM = pl.BlockSpec(memory_space=pltpu.VMEM)


def lookup_kernel(codes_ref, table_ref, out_ref, ids_ref):
    subs, rows = codes_ref.shape[1:]
    width = table_ref.shape[1]
    halves = table_ref.shape[2] // LANES
    first_out = pl.program_id(0) * (subs * width)
    ids_ref[...] = codes_ref[0].astype(jnp.float32).astype(jnp.int32)

    def body(step, carry):
        base = pl.multiple_of(step * GROUP, GROUP)
        for first in range(0, rows, LANES):
            lanes = pl.ds(pl.multiple_of(pl.program_id(1) * rows + first, LANES), LANES)
            ids_all = ids_ref[pl.ds(base, GROUP), first : first + LANES]
            for pair in range(0, GROUP, 2):
                both = []
                for sub in (pair, pair + 1):
                    ids = jnp.broadcast_to(ids_all[sub : sub + 1], (width, LANES))
                    lane = jnp.bitwise_and(ids, LANES - 1)
                    picked = None
                    for half in range(halves):
                        entries = table_ref[base + sub, :, half * LANES : (half + 1) * LANES]
                        got = jnp.take_along_axis(
                            entries, lane, axis=1, mode="promise_in_bounds"
                        )
                        picked = got if half == 0 else jnp.where(ids >= half * LANES, got, picked)
                    both.append(picked)
                row = pl.multiple_of(first_out + (base + pair) * width, 2 * width)
                out_ref[pl.ds(row, 2 * width), lanes] = jnp.concatenate(both, axis=0).astype(
                    out_ref.dtype
                )
        return carry

    lax.fori_loop(0, subs // GROUP, body, 0)


def rebuild_rows(codes, table):
    blocks, subs, rows = codes.shape
    width, centroids = table.shape[1:]
    tile = min(64, subs)
    return pl.pallas_call(
        lookup_kernel,
        grid=(subs // tile, blocks),
        in_specs=[
            pl.BlockSpec((1, tile, rows), lambda m, s: (s, m, 0)),
            pl.BlockSpec((tile, width, centroids), lambda m, s: (m, 0, 0)),
        ],
        out_specs=VMEM,
        scratch_shapes=[pltpu.VMEM((tile, rows), jnp.int32)],
        out_shape=pltpu.VMEM((subs * width, blocks * rows), jnp.bfloat16),
        compiler_params=pltpu.CompilerParams(vmem_limit_bytes=VMEM_BYTES),
        name="lookup",
    )(codes, table)


def prior_kernel(factor, place_ref, rotation_any, *refs):
    outs, (rows_ref, sem) = refs[:-2], refs[-2:]
    block = rows_ref.shape[0]
    width = block // len(outs)
    first = pl.multiple_of(place_ref[0] * block, block)
    copy = pltpu.make_async_copy(rotation_any.at[pl.ds(first, block)], rows_ref, sem)
    copy.start()
    copy.wait()
    for stream, out_ref in enumerate(outs):
        rows = rows_ref[stream * width : (stream + 1) * width, :].astype(jnp.float32)
        out_ref[...] = factor * rows.T


def prior_blocks(place, rotation, block, streams, factor):
    cols = rotation.shape[1]
    return pl.pallas_call(
        functools.partial(prior_kernel, factor),
        in_specs=[pl.BlockSpec(memory_space=pltpu.SMEM), ANY],
        out_specs=[VMEM] * streams,
        out_shape=[pltpu.VMEM((cols, block // streams), jnp.float32)] * streams,
        scratch_shapes=[pltpu.VMEM((block, cols), rotation.dtype), pltpu.SemaphoreType.DMA],
        compiler_params=pltpu.CompilerParams(vmem_limit_bytes=VMEM_BYTES),
        name="prior",
    )(place, pltpu.with_memory_space_constraint(rotation, pltpu.HBM))


def turn_kernel(*refs):
    pieces, out_ref = refs[:-1], refs[-1]
    values = jnp.concatenate([piece_ref[...] for piece_ref in pieces], axis=1)
    out_ref[...] = values.astype(jnp.float32).T.astype(out_ref.dtype)


def turned(pieces):
    cols, width = pieces[0].shape
    return pl.pallas_call(
        turn_kernel,
        in_specs=[VMEM] * len(pieces),
        out_specs=VMEM,
        out_shape=pltpu.VMEM((len(pieces) * width, cols), pieces[0].dtype),
        compiler_params=pltpu.CompilerParams(vmem_limit_bytes=VMEM_BYTES),
        name="turn",
    )(*in_vmem(*pieces))


def slices_kernel(steps, streams, inner_size, place_ref, weights_ref, rows_ref, *outs):
    width = outs[0].shape[1] // inner_size
    wide = width * streams * inner_size
    rows, part_rows = outs[0].shape[0], outs[-1].shape[0]

    def scaled(first, step, stream):
        base = lax.bitwise_xor(place_ref[2], step) * wide + stream * width
        column = jnp.broadcast_to(weights_ref[:, pl.ds(first, part_rows)], (LANES, part_rows)).T
        for index in range(inner_size):
            lanes = pl.ds(pl.multiple_of(base + index * width * streams, LANES), width)
            values = rows_ref[pl.ds(first, part_rows), lanes].astype(jnp.float32)
            yield slice(index * width, (index + 1) * width), (values * column).astype(outs[0].dtype)

    for index, out_ref in enumerate(outs):
        stream, slot = divmod(index, 1 + len(steps))
        if slot:
            first = pl.multiple_of(place_ref[0] * part_rows, part_rows)
            for span, values in scaled(first, steps[slot - 1], stream):
                out_ref[:, span] = values
        else:
            for first in range(0, rows, part_rows):
                for span, values in scaled(first, 0, stream):
                    out_ref[first : first + part_rows, span] = values


def weighted_slices(place, weights, embeddings, part_rows, steps, streams, inner_size, wide):
    rows = embeddings.shape[0]
    count = 1 + len(steps)
    if part_rows % LANES or wide // streams // inner_size != LANES:
        scaled = (weights[:, None] * embeddings.astype(jnp.float32)).astype(jnp.bfloat16)
        parts = [lax.dynamic_slice_in_dim(scaled, place[2] * wide, wide, 1)]
        for step in steps:
            start = (place[0] * part_rows, (place[2] ^ step) * wide)
            parts.append(lax.dynamic_slice(scaled, start, (part_rows, wide)))
        split = [part.reshape(part.shape[0], inner_size, streams, -1) for part in parts]
        return [
            [part[:, :, stream].reshape(part.shape[0], -1) for part in split]
            for stream in range(streams)
        ]
    shapes = [(rows, wide // streams)] + [(part_rows, wide // streams)] * len(steps)
    outs = pl.pallas_call(
        functools.partial(slices_kernel, steps, streams, inner_size),
        in_specs=[pl.BlockSpec(memory_space=pltpu.SMEM), VMEM, VMEM],
        out_specs=[VMEM] * (count * streams),
        out_shape=[pltpu.VMEM(shape, jnp.bfloat16) for shape in shapes] * streams,
        compiler_params=pltpu.CompilerParams(vmem_limit_bytes=VMEM_BYTES),
        name="slices",
    )(place, *in_vmem(weights[None, :], embeddings))
    return [list(outs[first : first + count]) for first in range(0, count * streams, count)]


def cross_kernel(plan, place_ref, own_ref, rebuilt_ref, prior_ref, local_ref, *refs):
    pieces, outs = refs[: len(refs) - len(plan)], refs[len(refs) - len(plan) :]
    rows = local_ref.shape[0]
    part_rows, col = (pieces[0].shape[0], rows // pieces[0].shape[0]) if pieces else (rows, 1)
    for (targets, first_row), out_ref in zip(plan, outs):
        span = slice(first_row, first_row + out_ref.shape[0])
        width = out_ref.shape[1] // len(targets)
        left = [own_ref[span, :]]
        for index in range(len(pieces)):
            step, turn = divmod(index, col)
            first = step * rows + lax.rem(place_ref[0] + turn, col) * part_rows
            left.append(rebuilt_ref[span, pl.ds(pl.multiple_of(first, part_rows), part_rows)])
        right = []
        for target in targets:
            place = lax.bitwise_xor(place_ref[1], target)
            lanes = pl.ds(pl.multiple_of(place * width, width), width)
            right.append(
                jnp.concatenate([part[:, lanes] for part in (local_ref, *pieces)], axis=0)
            )
        total = jnp.dot(
            jnp.concatenate(left, axis=1), jnp.concatenate(right, axis=1),
            preferred_element_type=jnp.float32,
        )
        if targets[0] == 0:
            out_ref[:, :width] = (total[:, :width] + prior_ref[span, :]).astype(out_ref.dtype)
            out_ref[:, width:] = total[:, width:].astype(out_ref.dtype)
        else:
            out_ref[...] = total.astype(out_ref.dtype)


def cross_blocks(plan, dtype, place, own, rebuilt, prior, local, pieces):
    operands = in_vmem(own, rebuilt, prior, local, *pieces)
    half, width = prior.shape[0] // 2, prior.shape[1]
    return pl.pallas_call(
        functools.partial(cross_kernel, plan),
        in_specs=[pl.BlockSpec(memory_space=pltpu.SMEM)] + [VMEM] * len(operands),
        out_specs=[VMEM] * len(plan),
        out_shape=[pltpu.VMEM((half, len(targets) * width), dtype) for targets, _ in plan],
        compiler_params=pltpu.CompilerParams(vmem_limit_bytes=VMEM_BYTES),
        name="cross",
    )(place, *operands)


def product_of(value_ref, pieces, inner_ref, index):
    block_values = jnp.concatenate([piece_ref[...] for piece_ref in pieces], axis=1)
    block = block_values.shape[1]
    product = jnp.dot(value_ref[...], block_values, preferred_element_type=jnp.float32)
    inner_ref[index * block : (index + 1) * block, :] = product.T.astype(inner_ref.dtype)


def first_kernel(streams, own_ref, before_ref, *refs):
    panel, (inner_ref, square_ref) = refs[:-2], refs[-2:]
    cols, width = panel[0].shape
    square = before_ref[...]
    for index in range(len(panel) // streams):
        pieces = panel[streams * index : streams * (index + 1)]
        product_of(own_ref, pieces, inner_ref, index)
        for piece_ref in pieces:
            values = piece_ref[...].astype(jnp.float32)
            square += jnp.sum((values * values).reshape(cols // 8, 8, width), axis=0)
    square_ref[...] = square


def add_up(mine, other, sum_ref):
    first = 0
    for mine_ref, other_ref in zip(mine, other):
        sum_ref[first : first + mine_ref.shape[0], :] = mine_ref[...] + other_ref[...]
        first += mine_ref.shape[0]


def gram_rows(panel, sum_ref, index):
    chunk = panel[0].shape[0] // CHUNKS
    span = slice(index * chunk, (index + 1) * chunk)
    rows = jnp.concatenate([piece_ref[span, :] for piece_ref in panel], axis=1)
    return span, jnp.dot(rows, sum_ref[...], preferred_element_type=jnp.float32)


def apply_kernel(step, streams, count, parts, mine_square_ref, other_square_ref, *refs):
    last = step == 3
    states = 2 if last else 1
    panel, refs = refs[:count], refs[count:]
    mine, other, refs = refs[:parts], refs[parts : 2 * parts], refs[2 * parts :]
    held, refs = refs[:states], refs[states:]
    if last:
        out_ref, sum_ref = refs
    else:
        state_ref, value_ref, inner_ref, sum_ref = refs
    width = panel[0].shape[1]
    model_width = count * width
    total = jnp.sum(mine_square_ref[...] + other_square_ref[...], axis=(0, 1), keepdims=True)
    scale = model_width / (1.96 * total)
    add_up(mine, other, sum_ref)
    for index in range(CHUNKS):
        span, made = gram_rows(panel, sum_ref, index)
        if step == 2:
            made = made * scale
        else:
            made = 1.5 * held[0][span, :] - (0.5 * scale) * made
        if last:
            made = (1.5 * held[1][span, :] - 0.5 * made) * (math.sqrt(model_width) * jnp.sqrt(scale))
            out_ref[:, span] = made.T
        else:
            state_ref[span, :] = made
            value_ref[:, span] = made.T.astype(value_ref.dtype)
    if last:
        return
    for index in range(inner_ref.shape[0] // (streams * width)):
        product_of(value_ref, panel[streams * index : streams * (index + 1)], inner_ref, index)


def rest_kernel(streams, value_ref, *refs):
    panel, inner_ref = refs[:-1], refs[-1]
    for index in range(len(panel) // streams):
        product_of(value_ref, panel[streams * index : streams * (index + 1)], inner_ref, index)


def in_vmem(*values):
    return [pltpu.with_memory_space_constraint(value, pltpu.VMEM) for value in values]


def apply_first(own, square, panel):
    block = own.shape[0]
    streams = block // panel[0].shape[1]
    return pl.pallas_call(
        functools.partial(first_kernel, streams),
        in_specs=[VMEM] * (2 + len(panel)),
        out_specs=[VMEM, VMEM],
        out_shape=[
            pltpu.VMEM((len(panel) // streams * block, block), jnp.bfloat16),
            pltpu.VMEM(square.shape, jnp.float32),
        ],
        compiler_params=pltpu.CompilerParams(vmem_limit_bytes=VMEM_BYTES),
        name="first",
    )(*in_vmem(own, square, *panel))


def apply_gram(step, panel, inner, squares, held):
    mine, other = zip(*inner)
    cols, width = panel[0].shape
    block = mine[0].shape[1]
    last = step == 3
    if last:
        out_shape = jax.ShapeDtypeStruct((block, cols), jnp.float32)
    else:
        out_shape = [
            pltpu.VMEM((cols, block), jnp.float32),
            pltpu.VMEM((block, cols), jnp.bfloat16),
            pltpu.VMEM((len(panel) // 2 * width, block), jnp.bfloat16),
        ]
    operands = in_vmem(*squares, *panel, *mine, *other, *held)
    return pl.pallas_call(
        functools.partial(apply_kernel, step, block // width, len(panel), len(inner)),
        in_specs=[VMEM] * len(operands),
        out_specs=VMEM if last else [VMEM] * 3,
        out_shape=out_shape,
        scratch_shapes=[pltpu.VMEM((len(panel) * width, block), jnp.bfloat16)],
        compiler_params=pltpu.CompilerParams(vmem_limit_bytes=VMEM_BYTES),
        name="apply%d" % step,
    )(*operands)


def apply_rest(value, panel):
    block = value.shape[0]
    width = panel[0].shape[1]
    operands = in_vmem(value, *panel)
    return pl.pallas_call(
        functools.partial(rest_kernel, block // width),
        in_specs=[VMEM] * len(operands),
        out_specs=VMEM,
        out_shape=pltpu.VMEM((len(panel) * width, block), jnp.bfloat16),
        compiler_params=pltpu.CompilerParams(vmem_limit_bytes=VMEM_BYTES),
        name="rest",
    )(*operands)


def swap_cores(value):
    return lax.ppermute(value, "col", [(0, 1), (1, 0)])


def both_cores(value):
    if lax.axis_size("col") == 2:
        return value, swap_cores(value)
    total = lax.psum(value.astype(jnp.float32), "col").astype(value.dtype)
    return total, jnp.zeros_like(total)


def gather_rounds(outer_size):
    held = {(0, 0)}
    last = outer_size - 1
    rounds = []
    for k in range(1, outer_size):
        rounds.append([((k, 0), (k - 1, 0)), ((k - 1, 1), (k - 1, 0)), ((k - 1, 2), (k - 1, 0))])
    held.update(key for moves in rounds for key, _ in moves)
    rest = [(last, 1), (last, 2)] + [(k, 3) for k in range(outer_size)]
    while rest:
        moves, taken = [], set()
        for key in rest:
            ways = [("y", (key[0], key[1] ^ 2)), ("x", (key[0], key[1] ^ 1)), ("z", (key[0] - 1, key[1]))]
            if key == (last, 1):
                ways.reverse()
            if key[1] == 3:
                ways = ways[::-1] if (key[0] - 1, 3) in held else ways
            for link, source in ways:
                if source in held and link not in taken:
                    taken.add(link)
                    moves.append((key, source))
                    break
        held.update(key for key, _ in moves)
        rest = [key for key in rest if key not in held]
        rounds.append(moves)
    return rounds


def shards(embeddings, rotation, codes, codebooks):
    tok_rows, model_width = embeddings.shape
    dp, col = lax.axis_size("dp"), lax.axis_size("col")
    rows_total = tok_rows * dp
    block = model_width // dp
    inner_size = math.gcd(dp, INNER)
    outer_size = dp // inner_size
    wide = model_width // outer_size
    part_rows = tok_rows // col
    outer, inner = lax.axis_index("dp") // inner_size, lax.axis_index("dp") % inner_size
    core = lax.axis_index("col")

    def from_outer(value, step):
        pairs = [(i, (i // inner_size ^ step) * inner_size + i % inner_size) for i in range(dp)]
        return lax.ppermute(value, "dp", pairs)

    def from_inner(value, step):
        pairs = [(i, i // inner_size * inner_size + (i % inner_size ^ step)) for i in range(dp)]
        return lax.ppermute(value, "dp", pairs)

    steps = list(range(1, outer_size))
    codes_t = codes.T.astype(jnp.bfloat16)
    group_codes = [from_outer(codes_t, step) for step in steps]

    table = jnp.transpose(codebooks, (0, 2, 1)).astype(jnp.float32)
    own = rebuild_rows(codes_t[None], table)
    rotated = lax.dot_general(
        rotation, embeddings, (((0,), (1,)), ((), ())), preferred_element_type=jnp.float32
    )
    residue = rotated - own.astype(jnp.float32)
    row_error = jnp.sum(residue * residue, axis=0)
    row_error = row_error + swap_cores(row_error) if col == 2 else lax.psum(row_error, "col")
    weights = 1.0 / (1.0 + row_error / (2.0 * model_width))
    weights, group_codes = lax.optimization_barrier((weights, group_codes))

    streams = 2 if block % (2 * LANES) == 0 else 1
    width = block // streams
    place = jnp.stack([core, inner, outer]).astype(jnp.int32)
    slices = weighted_slices(
        place, weights, embeddings, part_rows, steps, streams, inner_size, wide
    )
    rebuilt = rebuild_rows(jnp.stack(group_codes), table)
    dp_index, rebuilt = lax.optimization_barrier((lax.axis_index("dp"), rebuilt))
    prior = prior_blocks(
        dp_index[None].astype(jnp.int32), rotation, block, streams, 0.2 * rows_total
    )
    half = prior[0].shape[0] // 2
    near = [(1, 2), (2, 1)]
    fetched, shares = [], []
    for stream, (_, *sends) in enumerate(slices):
        if stream:
            sends, rebuilt, shares = lax.optimization_barrier((sends, rebuilt, shares))
            fetched.append(shares)
        shares = [from_outer(send, step) for send, step in zip(sends, steps)]
    fetched.append(shares)
    starts, narrow = [], []
    for stream in range(streams):
        pieces = []
        for share in fetched[stream]:
            if part_rows % LANES:
                pieces.append(lax.all_gather(share, "col", axis=0, tiled=True))
                continue
            pieces.append(share)
            for turn in range(1, col):
                pairs = [(i, (i - turn) % col) for i in range(col)]
                pieces.append(lax.ppermute(share, "col", pairs))
        if stream:
            pieces, narrow = lax.optimization_barrier((pieces, narrow))
        blocks_for = functools.partial(
            cross_blocks,
            place=place,
            own=own,
            rebuilt=rebuilt,
            prior=prior[stream],
            local=slices[stream][0],
            pieces=pieces,
        )
        sent = blocks_for([((one, 3), side * half) for side, (one, _) in enumerate(near)], jnp.bfloat16)
        came = [from_inner(value, one) for value, (one, _) in zip(sent, near)]
        kept = blocks_for([((0, two), side * half) for side, (_, two) in enumerate(near)], jnp.float32)
        if stream + 1 < streams:
            fetched[stream + 1], came = lax.optimization_barrier((fetched[stream + 1], came))
        sums = []
        for side, (_, two) in enumerate(near):
            total = kept[side] + came[side].astype(jnp.float32)
            last = from_inner(total[:, width:].astype(jnp.bfloat16), two)
            sums.append(total[:, :width] + last.astype(jnp.float32))
        starts.append(jnp.concatenate(sums, axis=0))
        narrow.append(starts[-1].astype(jnp.bfloat16))
    start = jnp.concatenate(starts, axis=1)

    def ring(value):
        pairs = [(i, (i + inner_size) % dp) for i in range(dp)]
        return lax.ppermute(value, "dp", pairs)

    own = turned(narrow)
    held = [{(0, 0): value} for value in narrow]

    def move(stream, key, source):
        value = held[stream][source]
        return ring(value) if key[0] != source[0] else from_inner(value, key[1] ^ source[1])

    def pieces_of(keys):
        return [held[stream][key] for key in keys for stream in range(streams)]

    order, products = [(0, 0)], []
    square = jnp.zeros((8, width), jnp.float32)
    fresh = [(0, 0)]
    for moves in gather_rounds(outer_size):
        arrived = [
            [move(stream, key, source) for key, source in moves] for stream in range(streams)
        ]
        product, square = apply_first(own, square, pieces_of(fresh))
        for stream in range(streams - 1):
            arrived[stream] = lax.optimization_barrier(arrived[stream])
        arrived[-1], product, square = lax.optimization_barrier((arrived[-1], product, square))
        fresh = [key for key, _ in moves]
        for stream in range(streams):
            held[stream].update(zip(fresh, arrived[stream]))
        order += fresh
        products.append(both_cores(product))
    product, square = apply_first(own, square, pieces_of(fresh))
    products.append(both_cores(product))
    panel = pieces_of(order)
    squares = both_cores(square)

    states = [start]
    middle = len(panel) // 2
    for step in range(3):
        state, value, product = apply_gram(step, panel, products, squares, states[-1:])
        states.append(state)
        early, rest = lax.optimization_barrier(
            (both_cores(product), apply_rest(value, panel[middle:]))
        )
        products = [early, both_cores(rest)]
    return apply_gram(3, panel, products, squares, [states[3], states[1]])


def solution(mesh):
    placed = (P("dp", None), P(None, "col"), P("dp", "col"), P("col", None, None))
    return jax.shard_map(
        shards, mesh=mesh, in_specs=placed, out_specs=P("dp", "col"), check_vma=False
    )
```

```python
import functools
import math

import jax
import jax.numpy as jnp
from jax import lax
from jax.experimental import pallas as pl
from jax.experimental.pallas import tpu as pltpu
from jax.sharding import PartitionSpec as P

LANES = 128
GROUP = 8
CHUNKS = 4
INNER = 4
VMEM_BYTES = 24 * 1024 * 1024
ANY = pl.BlockSpec(memory_space=pl.ANY)
VMEM = pl.BlockSpec(memory_space=pltpu.VMEM)


def lookup_kernel(codes_ref, table_ref, out_ref, ids_ref):
    subs, rows = codes_ref.shape[1:]
    width = table_ref.shape[1]
    halves = table_ref.shape[2] // LANES
    first_out = pl.program_id(0) * (subs * width)
    ids_ref[...] = codes_ref[0].astype(jnp.float32).astype(jnp.int32)

    def body(step, carry):
        base = pl.multiple_of(step * GROUP, GROUP)
        for first in range(0, rows, LANES):
            lanes = pl.ds(pl.multiple_of(pl.program_id(1) * rows + first, LANES), LANES)
            ids_all = ids_ref[pl.ds(base, GROUP), first : first + LANES]
            for pair in range(0, GROUP, 2):
                both = []
                for sub in (pair, pair + 1):
                    ids = jnp.broadcast_to(ids_all[sub : sub + 1], (width, LANES))
                    lane = jnp.bitwise_and(ids, LANES - 1)
                    picked = None
                    for half in range(halves):
                        entries = table_ref[base + sub, :, half * LANES : (half + 1) * LANES]
                        got = jnp.take_along_axis(
                            entries, lane, axis=1, mode="promise_in_bounds"
                        )
                        picked = got if half == 0 else jnp.where(ids >= half * LANES, got, picked)
                    both.append(picked)
                row = pl.multiple_of(first_out + (base + pair) * width, 2 * width)
                out_ref[pl.ds(row, 2 * width), lanes] = jnp.concatenate(both, axis=0).astype(
                    out_ref.dtype
                )
        return carry

    lax.fori_loop(0, subs // GROUP, body, 0)


def rebuild_rows(codes, table):
    blocks, subs, rows = codes.shape
    width, centroids = table.shape[1:]
    tile = min(64, subs)
    return pl.pallas_call(
        lookup_kernel,
        grid=(subs // tile, blocks),
        in_specs=[
            pl.BlockSpec((1, tile, rows), lambda m, s: (s, m, 0)),
            pl.BlockSpec((tile, width, centroids), lambda m, s: (m, 0, 0)),
        ],
        out_specs=VMEM,
        scratch_shapes=[pltpu.VMEM((tile, rows), jnp.int32)],
        out_shape=pltpu.VMEM((subs * width, blocks * rows), jnp.bfloat16),
        compiler_params=pltpu.CompilerParams(vmem_limit_bytes=VMEM_BYTES),
        name="lookup",
    )(codes, pltpu.with_memory_space_constraint(table, pltpu.HBM))


def prior_kernel(factor, place_ref, rotation_any, *refs):
    outs, (rows_ref, sem) = refs[:-2], refs[-2:]
    block = rows_ref.shape[0]
    width = block // len(outs)
    first = pl.multiple_of(place_ref[0] * block, block)
    copy = pltpu.make_async_copy(rotation_any.at[pl.ds(first, block)], rows_ref, sem)
    copy.start()
    copy.wait()
    for stream, out_ref in enumerate(outs):
        rows = rows_ref[stream * width : (stream + 1) * width, :].astype(jnp.float32)
        out_ref[...] = factor * rows.T


def prior_blocks(place, rotation, block, streams, factor):
    cols = rotation.shape[1]
    return pl.pallas_call(
        functools.partial(prior_kernel, factor),
        in_specs=[pl.BlockSpec(memory_space=pltpu.SMEM), ANY],
        out_specs=[VMEM] * streams,
        out_shape=[pltpu.VMEM((cols, block // streams), jnp.float32)] * streams,
        scratch_shapes=[pltpu.VMEM((block, cols), rotation.dtype), pltpu.SemaphoreType.DMA],
        compiler_params=pltpu.CompilerParams(vmem_limit_bytes=VMEM_BYTES),
        name="prior",
    )(place, pltpu.with_memory_space_constraint(rotation, pltpu.HBM))


def turn_kernel(*refs):
    pieces, out_ref = refs[:-1], refs[-1]
    values = jnp.concatenate([piece_ref[...] for piece_ref in pieces], axis=1)
    out_ref[...] = values.astype(jnp.float32).T.astype(out_ref.dtype)


def turned(pieces):
    cols, width = pieces[0].shape
    return pl.pallas_call(
        turn_kernel,
        in_specs=[VMEM] * len(pieces),
        out_specs=VMEM,
        out_shape=pltpu.VMEM((len(pieces) * width, cols), pieces[0].dtype),
        compiler_params=pltpu.CompilerParams(vmem_limit_bytes=VMEM_BYTES),
        name="turn",
    )(*in_vmem(*pieces))


def slices_kernel(steps, streams, inner_size, place_ref, weights_ref, rows_ref, *outs):
    width = outs[0].shape[1] // inner_size
    wide = width * streams * inner_size
    rows, part_rows = outs[0].shape[0], outs[-1].shape[0]

    def scaled(first, step, stream):
        base = lax.bitwise_xor(place_ref[2], step) * wide + stream * width
        column = jnp.broadcast_to(weights_ref[:, pl.ds(first, part_rows)], (LANES, part_rows)).T
        for index in range(inner_size):
            lanes = pl.ds(pl.multiple_of(base + index * width * streams, LANES), width)
            values = rows_ref[pl.ds(first, part_rows), lanes].astype(jnp.float32)
            yield slice(index * width, (index + 1) * width), (values * column).astype(outs[0].dtype)

    for index, out_ref in enumerate(outs):
        stream, slot = divmod(index, 1 + len(steps))
        if slot:
            first = pl.multiple_of(place_ref[0] * part_rows, part_rows)
            for span, values in scaled(first, steps[slot - 1], stream):
                out_ref[:, span] = values
        else:
            for first in range(0, rows, part_rows):
                for span, values in scaled(first, 0, stream):
                    out_ref[first : first + part_rows, span] = values


def weighted_slices(place, weights, embeddings, part_rows, steps, streams, inner_size, wide):
    rows = embeddings.shape[0]
    count = 1 + len(steps)
    if part_rows % LANES or wide // streams // inner_size != LANES:
        scaled = (weights[:, None] * embeddings.astype(jnp.float32)).astype(jnp.bfloat16)
        parts = [lax.dynamic_slice_in_dim(scaled, place[2] * wide, wide, 1)]
        for step in steps:
            start = (place[0] * part_rows, (place[2] ^ step) * wide)
            parts.append(lax.dynamic_slice(scaled, start, (part_rows, wide)))
        split = [part.reshape(part.shape[0], inner_size, streams, -1) for part in parts]
        return [
            [part[:, :, stream].reshape(part.shape[0], -1) for part in split]
            for stream in range(streams)
        ]
    shapes = [(rows, wide // streams)] + [(part_rows, wide // streams)] * len(steps)
    outs = pl.pallas_call(
        functools.partial(slices_kernel, steps, streams, inner_size),
        in_specs=[pl.BlockSpec(memory_space=pltpu.SMEM), VMEM, VMEM],
        out_specs=[VMEM] * (count * streams),
        out_shape=[pltpu.VMEM(shape, jnp.bfloat16) for shape in shapes] * streams,
        compiler_params=pltpu.CompilerParams(vmem_limit_bytes=VMEM_BYTES),
        name="slices",
    )(place, *in_vmem(weights[None, :], embeddings))
    return [list(outs[first : first + count]) for first in range(0, count * streams, count)]


def cross_kernel(plan, place_ref, own_ref, rebuilt_ref, prior_ref, local_ref, *refs):
    pieces, outs = refs[: len(refs) - len(plan)], refs[len(refs) - len(plan) :]
    rows = local_ref.shape[0]
    part_rows, col = (pieces[0].shape[0], rows // pieces[0].shape[0]) if pieces else (rows, 1)
    for (targets, first_row), out_ref in zip(plan, outs):
        span = slice(first_row, first_row + out_ref.shape[0])
        width = out_ref.shape[1] // len(targets)
        left = [own_ref[span, :]]
        for index in range(len(pieces)):
            step, turn = divmod(index, col)
            first = step * rows + lax.rem(place_ref[0] + turn, col) * part_rows
            left.append(rebuilt_ref[span, pl.ds(pl.multiple_of(first, part_rows), part_rows)])
        right = []
        for target in targets:
            place = lax.bitwise_xor(place_ref[1], target)
            lanes = pl.ds(pl.multiple_of(place * width, width), width)
            right.append(
                jnp.concatenate([part[:, lanes] for part in (local_ref, *pieces)], axis=0)
            )
        total = jnp.dot(
            jnp.concatenate(left, axis=1), jnp.concatenate(right, axis=1),
            preferred_element_type=jnp.float32,
        )
        if targets[0] == 0:
            out_ref[:, :width] = (total[:, :width] + prior_ref[span, :]).astype(out_ref.dtype)
            out_ref[:, width:] = total[:, width:].astype(out_ref.dtype)
        else:
            out_ref[...] = total.astype(out_ref.dtype)


def cross_blocks(plan, dtype, place, own, rebuilt, prior, local, pieces):
    operands = in_vmem(own, rebuilt, prior, local, *pieces)
    half, width = prior.shape[0] // 2, prior.shape[1]
    return pl.pallas_call(
        functools.partial(cross_kernel, plan),
        in_specs=[pl.BlockSpec(memory_space=pltpu.SMEM)] + [VMEM] * len(operands),
        out_specs=[VMEM] * len(plan),
        out_shape=[pltpu.VMEM((half, len(targets) * width), dtype) for targets, _ in plan],
        compiler_params=pltpu.CompilerParams(vmem_limit_bytes=VMEM_BYTES),
        name="cross",
    )(place, *operands)


def product_of(value_ref, pieces, inner_ref, index):
    block_values = jnp.concatenate([piece_ref[...] for piece_ref in pieces], axis=1)
    block = block_values.shape[1]
    product = jnp.dot(value_ref[...], block_values, preferred_element_type=jnp.float32)
    inner_ref[index * block : (index + 1) * block, :] = product.T.astype(inner_ref.dtype)


def first_kernel(streams, own_ref, before_ref, *refs):
    panel, (inner_ref, square_ref) = refs[:-2], refs[-2:]
    cols, width = panel[0].shape
    square = before_ref[...]
    for index in range(len(panel) // streams):
        pieces = panel[streams * index : streams * (index + 1)]
        product_of(own_ref, pieces, inner_ref, index)
        for piece_ref in pieces:
            values = piece_ref[...].astype(jnp.float32)
            square += jnp.sum((values * values).reshape(cols // 8, 8, width), axis=0)
    square_ref[...] = square


def add_up(mine, other, sum_ref):
    first = 0
    for mine_ref, other_ref in zip(mine, other):
        sum_ref[first : first + mine_ref.shape[0], :] = mine_ref[...] + other_ref[...]
        first += mine_ref.shape[0]


def gram_rows(panel, sum_ref, index):
    chunk = panel[0].shape[0] // CHUNKS
    span = slice(index * chunk, (index + 1) * chunk)
    rows = jnp.concatenate([piece_ref[span, :] for piece_ref in panel], axis=1)
    return span, jnp.dot(rows, sum_ref[...], preferred_element_type=jnp.float32)


def apply_kernel(step, streams, count, parts, mine_square_ref, other_square_ref, *refs):
    last = step == 3
    states = 2 if last else 1
    panel, refs = refs[:count], refs[count:]
    mine, other, refs = refs[:parts], refs[parts : 2 * parts], refs[2 * parts :]
    held, refs = refs[:states], refs[states:]
    if last:
        out_ref, sum_ref = refs
    else:
        state_ref, value_ref, inner_ref, sum_ref = refs
    width = panel[0].shape[1]
    model_width = count * width
    total = jnp.sum(mine_square_ref[...] + other_square_ref[...], axis=(0, 1), keepdims=True)
    scale = model_width / (1.96 * total)
    add_up(mine, other, sum_ref)
    for index in range(CHUNKS):
        span, made = gram_rows(panel, sum_ref, index)
        if step == 2:
            made = made * scale
        else:
            made = 1.5 * held[0][span, :] - (0.5 * scale) * made
        if last:
            made = (1.5 * held[1][span, :] - 0.5 * made) * (math.sqrt(model_width) * jnp.sqrt(scale))
            out_ref[:, span] = made.T
        else:
            state_ref[span, :] = made
            value_ref[:, span] = made.T.astype(value_ref.dtype)
    if last:
        return
    for index in range(inner_ref.shape[0] // (streams * width)):
        product_of(value_ref, panel[streams * index : streams * (index + 1)], inner_ref, index)


def rest_kernel(streams, value_ref, *refs):
    panel, inner_ref = refs[:-1], refs[-1]
    for index in range(len(panel) // streams):
        product_of(value_ref, panel[streams * index : streams * (index + 1)], inner_ref, index)


def in_vmem(*values):
    return [pltpu.with_memory_space_constraint(value, pltpu.VMEM) for value in values]


def apply_first(own, square, panel):
    block = own.shape[0]
    streams = block // panel[0].shape[1]
    return pl.pallas_call(
        functools.partial(first_kernel, streams),
        in_specs=[VMEM] * (2 + len(panel)),
        out_specs=[VMEM, VMEM],
        out_shape=[
            pltpu.VMEM((len(panel) // streams * block, block), jnp.bfloat16),
            pltpu.VMEM(square.shape, jnp.float32),
        ],
        compiler_params=pltpu.CompilerParams(vmem_limit_bytes=VMEM_BYTES),
        name="first",
    )(*in_vmem(own, square, *panel))


def apply_gram(step, panel, inner, squares, held):
    mine, other = zip(*inner)
    cols, width = panel[0].shape
    block = mine[0].shape[1]
    last = step == 3
    if last:
        out_shape = jax.ShapeDtypeStruct((block, cols), jnp.float32)
    else:
        out_shape = [
            pltpu.VMEM((cols, block), jnp.float32),
            pltpu.VMEM((block, cols), jnp.bfloat16),
            pltpu.VMEM((len(panel) // 2 * width, block), jnp.bfloat16),
        ]
    operands = in_vmem(*squares, *panel, *mine, *other, *held)
    return pl.pallas_call(
        functools.partial(apply_kernel, step, block // width, len(panel), len(inner)),
        in_specs=[VMEM] * len(operands),
        out_specs=VMEM if last else [VMEM] * 3,
        out_shape=out_shape,
        scratch_shapes=[pltpu.VMEM((len(panel) * width, block), jnp.bfloat16)],
        compiler_params=pltpu.CompilerParams(vmem_limit_bytes=VMEM_BYTES),
        name="apply%d" % step,
    )(*operands)


def apply_rest(value, panel):
    block = value.shape[0]
    width = panel[0].shape[1]
    operands = in_vmem(value, *panel)
    return pl.pallas_call(
        functools.partial(rest_kernel, block // width),
        in_specs=[VMEM] * len(operands),
        out_specs=VMEM,
        out_shape=pltpu.VMEM((len(panel) * width, block), jnp.bfloat16),
        compiler_params=pltpu.CompilerParams(vmem_limit_bytes=VMEM_BYTES),
        name="rest",
    )(*operands)


def swap_cores(value):
    return lax.ppermute(value, "col", [(0, 1), (1, 0)])


def both_cores(value):
    if lax.axis_size("col") == 2:
        return value, swap_cores(value)
    total = lax.psum(value.astype(jnp.float32), "col").astype(value.dtype)
    return total, jnp.zeros_like(total)


def gather_rounds(outer_size):
    held = {(0, 0)}
    last = outer_size - 1
    rounds = []
    for k in range(1, outer_size):
        rounds.append([((k, 0), (k - 1, 0)), ((k - 1, 1), (k - 1, 0)), ((k - 1, 2), (k - 1, 0))])
    held.update(key for moves in rounds for key, _ in moves)
    rest = [(last, 1), (last, 2)] + [(k, 3) for k in range(outer_size)]
    while rest:
        moves, taken = [], set()
        for key in rest:
            ways = [("y", (key[0], key[1] ^ 2)), ("x", (key[0], key[1] ^ 1)), ("z", (key[0] - 1, key[1]))]
            if key == (last, 1):
                ways.reverse()
            if key[1] == 3:
                ways = ways[::-1] if (key[0] - 1, 3) in held else ways
            for link, source in ways:
                if source in held and link not in taken:
                    taken.add(link)
                    moves.append((key, source))
                    break
        held.update(key for key, _ in moves)
        rest = [key for key in rest if key not in held]
        rounds.append(moves)
    return rounds


def shards(embeddings, rotation, codes, codebooks):
    tok_rows, model_width = embeddings.shape
    dp, col = lax.axis_size("dp"), lax.axis_size("col")
    rows_total = tok_rows * dp
    block = model_width // dp
    inner_size = math.gcd(dp, INNER)
    outer_size = dp // inner_size
    wide = model_width // outer_size
    part_rows = tok_rows // col
    outer, inner = lax.axis_index("dp") // inner_size, lax.axis_index("dp") % inner_size
    core = lax.axis_index("col")

    def from_outer(value, step):
        pairs = [(i, (i // inner_size ^ step) * inner_size + i % inner_size) for i in range(dp)]
        return lax.ppermute(value, "dp", pairs)

    def from_inner(value, step):
        pairs = [(i, i // inner_size * inner_size + (i % inner_size ^ step)) for i in range(dp)]
        return lax.ppermute(value, "dp", pairs)

    steps = list(range(1, outer_size))
    codes_t = codes.T.astype(jnp.bfloat16)
    group_codes = [from_outer(codes_t, step) for step in steps]

    table = jnp.transpose(codebooks, (0, 2, 1)).astype(jnp.float32)
    own = rebuild_rows(codes_t[None], table)
    rotated = lax.dot_general(
        rotation, embeddings, (((0,), (1,)), ((), ())), preferred_element_type=jnp.float32
    )
    residue = rotated - own.astype(jnp.float32)
    row_error = jnp.sum(residue * residue, axis=0)
    row_error = row_error + swap_cores(row_error) if col == 2 else lax.psum(row_error, "col")
    weights = 1.0 / (1.0 + row_error / (2.0 * model_width))
    weights, group_codes = lax.optimization_barrier((weights, group_codes))

    streams = 2 if block % (2 * LANES) == 0 else 1
    width = block // streams
    place = jnp.stack([core, inner, outer]).astype(jnp.int32)
    slices = weighted_slices(
        place, weights, embeddings, part_rows, steps, streams, inner_size, wide
    )
    rebuilt = rebuild_rows(jnp.stack(group_codes), table)
    dp_index, rebuilt = lax.optimization_barrier((lax.axis_index("dp"), rebuilt))
    prior = prior_blocks(
        dp_index[None].astype(jnp.int32), rotation, block, streams, 0.2 * rows_total
    )
    half = prior[0].shape[0] // 2
    near = [(1, 2), (2, 1)]
    fetched, shares = [], []
    for stream, (_, *sends) in enumerate(slices):
        if stream:
            sends, rebuilt, shares = lax.optimization_barrier((sends, rebuilt, shares))
            fetched.append(shares)
        shares = [from_outer(send, step) for send, step in zip(sends, steps)]
    fetched.append(shares)
    starts, narrow = [], []
    for stream in range(streams):
        pieces = []
        for share in fetched[stream]:
            if part_rows % LANES:
                pieces.append(lax.all_gather(share, "col", axis=0, tiled=True))
                continue
            pieces.append(share)
            for turn in range(1, col):
                pairs = [(i, (i - turn) % col) for i in range(col)]
                pieces.append(lax.ppermute(share, "col", pairs))
        if stream:
            pieces, narrow = lax.optimization_barrier((pieces, narrow))
        blocks_for = functools.partial(
            cross_blocks,
            place=place,
            own=own,
            rebuilt=rebuilt,
            prior=prior[stream],
            local=slices[stream][0],
            pieces=pieces,
        )
        sent = blocks_for([((one, 3), side * half) for side, (one, _) in enumerate(near)], jnp.bfloat16)
        came = [from_inner(value, one) for value, (one, _) in zip(sent, near)]
        kept = blocks_for([((0, two), side * half) for side, (_, two) in enumerate(near)], jnp.float32)
        if stream + 1 < streams:
            fetched[stream + 1], came = lax.optimization_barrier((fetched[stream + 1], came))
        sums = []
        for side, (_, two) in enumerate(near):
            total = kept[side] + came[side].astype(jnp.float32)
            last = from_inner(total[:, width:].astype(jnp.bfloat16), two)
            sums.append(total[:, :width] + last.astype(jnp.float32))
        starts.append(jnp.concatenate(sums, axis=0))
        narrow.append(starts[-1].astype(jnp.bfloat16))
    start = jnp.concatenate(starts, axis=1)

    def ring(value):
        pairs = [(i, (i + inner_size) % dp) for i in range(dp)]
        return lax.ppermute(value, "dp", pairs)

    own = turned(narrow)
    held = [{(0, 0): value} for value in narrow]

    def move(stream, key, source):
        value = held[stream][source]
        return ring(value) if key[0] != source[0] else from_inner(value, key[1] ^ source[1])

    def pieces_of(keys):
        return [held[stream][key] for key in keys for stream in range(streams)]

    order, products = [(0, 0)], []
    square = jnp.zeros((8, width), jnp.float32)
    fresh = [(0, 0)]
    for moves in gather_rounds(outer_size):
        arrived = [
            [move(stream, key, source) for key, source in moves] for stream in range(streams)
        ]
        product, square = apply_first(own, square, pieces_of(fresh))
        for stream in range(streams - 1):
            arrived[stream] = lax.optimization_barrier(arrived[stream])
        arrived[-1], product, square = lax.optimization_barrier((arrived[-1], product, square))
        fresh = [key for key, _ in moves]
        for stream in range(streams):
            held[stream].update(zip(fresh, arrived[stream]))
        order += fresh
        products.append(both_cores(product))
    product, square = apply_first(own, square, pieces_of(fresh))
    products.append(both_cores(product))
    panel = pieces_of(order)
    squares = both_cores(square)

    states = [start]
    middle = len(panel) // 2
    for step in range(3):
        state, value, product = apply_gram(step, panel, products, squares, states[-1:])
        states.append(state)
        early, rest = lax.optimization_barrier(
            (both_cores(product), apply_rest(value, panel[middle:]))
        )
        products = [early, both_cores(rest)]
    return apply_gram(3, panel, products, squares, [states[3], states[1]])


def solution(mesh):
    placed = (P("dp", None), P(None, "col"), P("dp", "col"), P("col", None, None))
    return jax.shard_map(
        shards, mesh=mesh, in_specs=placed, out_specs=P("dp", "col"), check_vma=False
    )
```
